32 devices in a mesh: cand: 4 (over x, core), row: 4 (over z), col: 2 (over y).
Axes of the slice: x: 2, y: 2, z: 4, core: 2. Of those that a mesh axis runs over, the one named last changes fastest.
Arguments:
- embedding: bfloat16 [1024, 1536], P(('row', 'col')), may hold values from -6 to 6
- bases_table: bfloat16 [4, 1536], replicated, may hold values from -10 to 10
- edit_pos: int32 [256], P('cand'), parts along dimension 0, may hold values from 0 to 1023
- edit_tok: int32 [256], P('cand'), parts along dimension 0, may hold values from 0 to 3
- w_row: bfloat16 [1536, 128], replicated, may hold values from -0.15625 to 0.15625
- w_col: bfloat16 [1536, 128], replicated, may hold values from -0.15625 to 0.15625
- dist_gain: float32 [128], replicated, may hold values from -4 to 4
- first_kernel: bfloat16 [3, 3, 128, 128], replicated, may hold values from -0.1875 to 0.1875
- second_kernel: bfloat16 [3, 3, 128, 128], replicated, may hold values from -0.1875 to 0.1875
- head_weight: bfloat16 [128], replicated, may hold values from -0.5 to 0.5
Outputs:
- contact: float32 [1024, 256], P(('cand', 'row'), 'col'), parts along dimension 0
The draws below stay inside these ranges and needn't reach their ends.
There are 4 independent parts, one for each index of `cand`. The reference program is written for one: setup_inputs(seed, part) draws one part's arguments, and reference() takes and returns one part's arrays. A program takes and returns all parts, laid end to end along the dimension named above; an argument that names none is the same for every part. Nothing has to cross between parts.
Inputs may be any that keep to these rules, and one draw needn't show every extreme that they name: `edit_pos`: two substitutions may fall on the same input bin.
All inputs are finite; a program needn't handle non-finite values.
Results may differ from the reference program's by a relative error of at most 0.015.
Values may be sent and summed in bfloat16 or wider, within the bound.
No kernel may reach another device: no remote copies, remote signals or barrier semaphores. Data moves between devices by JAX's collectives and lax.ppermute only.
A program may use at most 64 MiB of HBM per device.

```python
import math
import jax
import jax.numpy as jnp
from jax import lax

SEQ_CH = 1536
PAIR_CH = 128
POOL = 4
FIRST_SPACING = 2
SECOND_SPACING = 4
EDITS = 64
BASES = 4
SEQ_BINS = 1024


def plant(result, rng, least, largest):
    dims = result.shape
    index_at = [jax.random.randint(jax.random.fold_in(rng, axis), (), 0, dims[axis]) for axis in range(len(dims))]
    result = result.at[tuple(index_at)].set(least)
    longest = dims.index(max(dims))
    index_at[longest] = (index_at[longest] + 1) % dims[longest]
    return result.at[tuple(index_at)].set(largest)


def levels(stream_key, extent, pieces, low, high):
    loudness, own = 1.0, jax.random.fold_in(stream_key, 6)
    for dim, shards_of in pieces:
        heights = jnp.exp(jax.random.uniform(jax.random.fold_in(own, dim), (shards_of,), jnp.float32, low / len(pieces), high / len(pieces)))
        loudness = loudness * jnp.repeat(heights, extent[dim] // shards_of).reshape([-1 if axis == dim else 1 for axis in range(len(extent))])
    return loudness


def normal_values(key, shape, spread, reach, pieces=(), kind=jnp.bfloat16):
    gain = levels(key, shape, pieces, -0.22, 0.18) if pieces else 1.0
    array = jax.random.normal(key, shape, jnp.float32) * spread * gain
    return jnp.minimum(jnp.maximum(array, -reach), reach).astype(kind)


def setup_inputs(seed: int = 0, part: int = 0) -> dict:
    splits = jax.random.split(jax.random.key(seed), 11)
    part_keys = jax.random.split(jax.random.fold_in(splits[10], part), 11)
    return {
        "embedding": normal_values(splits[0], (SEQ_BINS, SEQ_CH), 1.0, 6.0, ((0, 8),)),
        "bases_table": normal_values(splits[1], (BASES, SEQ_CH), 2.0, 10.0),
        "edit_pos": plant(jax.random.randint(part_keys[2], (EDITS,), 0, SEQ_BINS), jax.random.fold_in(part_keys[2], 1), 0, SEQ_BINS - 1).astype(jnp.int32),
        "edit_tok": plant(jax.random.randint(part_keys[3], (EDITS,), 0, BASES), jax.random.fold_in(part_keys[3], 1), 0, BASES - 1).astype(jnp.int32),
        "w_row": normal_values(splits[4], (SEQ_CH, PAIR_CH), SEQ_CH ** -0.5, 0.15625),
        "w_col": normal_values(splits[5], (SEQ_CH, PAIR_CH), SEQ_CH ** -0.5, 0.15625),
        "dist_gain": normal_values(splits[6], (PAIR_CH,), 1.0, 4.0, (), jnp.float32),
        "first_kernel": normal_values(splits[7], (3, 3, PAIR_CH, PAIR_CH), (9 * PAIR_CH) ** -0.5, 0.1875),
        "second_kernel": normal_values(splits[8], (3, 3, PAIR_CH, PAIR_CH), (9 * PAIR_CH) ** -0.5, 0.1875),
        "head_weight": normal_values(splits[9], (PAIR_CH,), PAIR_CH ** -0.5, 0.5),
    }


def spaced_convolve(features, weight, dilation):
    size = features.shape[0]
    channels = features.shape[2]
    padded = jnp.pad(features, ((dilation, dilation), (dilation, dilation), (0, 0)))
    summed = jnp.zeros((size * size, weight.shape[3]), jnp.float32)
    for a in range(3):
        for b in range(3):
            window = padded[dilation * a:dilation * a + size, dilation * b:dilation * b + size]
            summed = summed + jnp.dot(window.reshape(size * size, channels), weight[a, b], preferred_element_type=jnp.float32)
    return summed.reshape(size, size, weight.shape[3])


def reference(embedding, bases_table, edit_pos, edit_tok, w_row, w_col, dist_gain, first_kernel, second_kernel, head_weight):
    seq_bins = embedding.shape[0]
    channels = embedding.shape[1]
    map_bins = seq_bins // POOL
    edit_delta = jnp.zeros((seq_bins, channels), jnp.float32).at[edit_pos].add(bases_table[edit_tok].astype(jnp.float32))
    edited = embedding.astype(jnp.float32) + edit_delta
    pooled = jnp.mean(edited.reshape(map_bins, POOL, channels), axis=1).astype(jnp.bfloat16)
    row_proj = jnp.dot(pooled, w_row, preferred_element_type=jnp.float32).astype(jnp.bfloat16)
    col_proj = jnp.dot(pooled, w_col, preferred_element_type=jnp.float32).astype(jnp.bfloat16)
    bin_index = jnp.arange(map_bins, dtype=jnp.int32)
    distance = jnp.abs(bin_index[:, None] - bin_index[None, :]).astype(jnp.float32)
    dist_feat = jnp.log1p(distance) * (1.0 / math.log(map_bins))
    pair_grid = jax.nn.relu(row_proj.astype(jnp.float32)[:, None, :] + col_proj.astype(jnp.float32)[None, :, :]
                           + dist_gain[None, None, :] * dist_feat[:, :, None]).astype(jnp.bfloat16)
    first_hidden = (pair_grid.astype(jnp.float32) + jax.nn.relu(spaced_convolve(pair_grid, first_kernel, FIRST_SPACING))).astype(jnp.bfloat16)
    second_hidden = first_hidden.astype(jnp.float32) + jax.nn.relu(spaced_convolve(first_hidden, second_kernel, SECOND_SPACING))
    score = jnp.dot(second_hidden.reshape(map_bins * map_bins, -1), head_weight.astype(jnp.float32),
                    precision=lax.Precision.HIGHEST).reshape(map_bins, map_bins)
    return 0.5 * (score + score.T)
```

```python
import math

import jax
import jax.numpy as jnp
from jax import lax
from jax.sharding import PartitionSpec as P

POOL = 4
FIRST_SPACING = 2
SECOND_SPACING = 4
BASES = 4
MARGIN = FIRST_SPACING + SECOND_SPACING


def projected(embedding, bases_table, edit_pos, edit_tok, w_row, w_col, first_bin):
    shard_bins = embedding.shape[0]
    pooled_bins = shard_bins // POOL
    bins = first_bin // POOL + jnp.arange(pooled_bins, dtype=jnp.int32)
    in_bin = bins[:, None] == (edit_pos // POOL)[None, :]
    is_base = edit_tok[:, None] == jnp.arange(BASES, dtype=jnp.int32)[None, :]
    counts = jnp.dot(
        in_bin.astype(jnp.bfloat16), is_base.astype(jnp.bfloat16), preferred_element_type=jnp.float32
    ).astype(jnp.bfloat16)
    take = (
        jnp.arange(shard_bins, dtype=jnp.int32)[None, :] // POOL
        == jnp.arange(pooled_bins, dtype=jnp.int32)[:, None]
    ).astype(jnp.bfloat16)
    summed = jnp.dot(take, embedding, preferred_element_type=jnp.float32) + jnp.dot(
        counts, bases_table, preferred_element_type=jnp.float32
    )
    pooled = (summed * (1.0 / POOL)).astype(jnp.bfloat16)
    both = jnp.concatenate([w_row, w_col], axis=1)
    return jnp.dot(pooled, both, preferred_element_type=jnp.float32).astype(jnp.bfloat16)


def gathered(block):
    count = lax.axis_size(("row", "col"))
    copies = jnp.broadcast_to(block[None], (count, *block.shape))
    got = lax.all_to_all(copies, ("row", "col"), 0, 0)
    return got.reshape(count * block.shape[0], block.shape[1])


def mirrored_tile(score):
    n_rows, n_cols = lax.axis_size("row"), lax.axis_size("col")
    row_at, col_at = lax.axis_index("row"), lax.axis_index("col")
    height, breadth = score.shape
    size = min(height, breadth)
    wide = breadth > height
    parts = max(height, breadth) // size
    pieces = jnp.stack(
        [
            (score[:, k * size : (k + 1) * size] if wide else score[k * size : (k + 1) * size]).T
            for k in range(parts)
        ]
    )
    own = (row_at if wide else col_at) % parts
    received = []
    for turn in range(parts):
        pairs = []
        for r in range(n_rows):
            for c in range(n_cols):
                if wide:
                    to = (parts * c + (turn + r) % parts, r // parts)
                else:
                    to = (c // parts, parts * r + (turn + c) % parts)
                pairs.append((r * n_cols + c, to[0] * n_cols + to[1]))
        piece = lax.dynamic_index_in_dim(pieces, (own + turn) % parts, 0, keepdims=False)
        received.append(lax.ppermute(piece, ("row", "col"), pairs))
    stacked = jnp.stack(received)
    placed = [
        lax.dynamic_index_in_dim(stacked, (own - sub) % parts, 0, keepdims=False) for sub in range(parts)
    ]
    return jnp.concatenate(placed, axis=1 if wide else 0)


def spaced_convolve(padded, weight, dilation):
    return lax.conv_general_dilated(
        padded[None],
        weight,
        (1, 1),
        "VALID",
        rhs_dilation=(dilation, dilation),
        dimension_numbers=("NHWC", "HWIO", "NHWC"),
        preferred_element_type=jnp.float32,
    )[0]


def on_device(
    embedding,
    bases_table,
    edit_pos,
    edit_tok,
    w_row,
    w_col,
    dist_gain,
    first_kernel,
    second_kernel,
    head_weight,
):
    n_rows, n_cols = lax.axis_size("row"), lax.axis_size("col")
    row_at, col_at = lax.axis_index("row"), lax.axis_index("col")
    shard_bins = embedding.shape[0]
    map_bins = shard_bins * n_rows * n_cols // POOL
    height, breadth = map_bins // n_rows, map_bins // n_cols
    first_bin = (row_at * n_cols + col_at) * shard_bins
    block = projected(embedding, bases_table, edit_pos, edit_tok, w_row, w_col, first_bin)
    every = jnp.pad(gathered(block), ((MARGIN, MARGIN), (0, 0)))
    channels = w_row.shape[1]
    row_start, col_start = row_at * height, col_at * breadth
    pair_rows, pair_cols = height + 2 * MARGIN, breadth + 2 * MARGIN
    row_proj = lax.dynamic_slice(every, (row_start, 0), (pair_rows, channels))
    col_proj = lax.dynamic_slice(every, (col_start, channels), (pair_cols, channels))
    row_bins = row_start - MARGIN + jnp.arange(pair_rows, dtype=jnp.int32)
    col_bins = col_start - MARGIN + jnp.arange(pair_cols, dtype=jnp.int32)
    distance = jnp.abs(row_bins[:, None] - col_bins[None, :]).astype(jnp.float32)
    dist_feat = jnp.log1p(distance) * (1.0 / math.log(map_bins))
    inside = ((row_bins >= 0) & (row_bins < map_bins))[:, None] & (
        (col_bins >= 0) & (col_bins < map_bins)
    )[None, :]
    pair_value = jax.nn.relu(
        row_proj.astype(jnp.float32)[:, None, :]
        + col_proj.astype(jnp.float32)[None, :, :]
        + dist_gain[None, None, :] * dist_feat[:, :, None]
    )
    pair = jnp.where(inside[:, :, None], pair_value, 0.0).astype(jnp.bfloat16)
    edge = FIRST_SPACING
    hidden = pair[edge:-edge, edge:-edge].astype(jnp.float32) + jax.nn.relu(
        spaced_convolve(pair, first_kernel, FIRST_SPACING)
    )
    hidden = jnp.where(inside[edge:-edge, edge:-edge, None], hidden, 0.0).astype(jnp.bfloat16)
    edge = SECOND_SPACING
    last = hidden[edge:-edge, edge:-edge].astype(jnp.float32) + jax.nn.relu(
        spaced_convolve(hidden, second_kernel, SECOND_SPACING)
    )
    score = jnp.sum(last * head_weight.astype(jnp.float32), axis=2)
    return 0.5 * (score + mirrored_tile(score))


def solution(mesh):
    placed = (P(("row", "col"), None), P(), P("cand"), P("cand"), P(), P(), P(), P(), P(), P())
    return jax.shard_map(
        on_device, mesh=mesh, in_specs=placed, out_specs=P(("cand", "row"), "col"), check_vma=False
    )
```

```python
import functools
import math

import jax
import jax.numpy as jnp
from jax import lax
from jax.experimental import pallas as pl
from jax.experimental.pallas import tpu as pltpu
from jax.sharding import PartitionSpec as P

POOL = 4
FIRST_SPACING = 2
SECOND_SPACING = 4
BASES = 4
MARGIN = FIRST_SPACING + SECOND_SPACING
PAD = 8
OUTSIDE = -1e30


def projected(embedding, bases_table, edit_pos, edit_tok, w_row, w_col, first_bin):
    shard_bins = embedding.shape[0]
    pooled_bins = shard_bins // POOL
    bins = first_bin // POOL + jnp.arange(pooled_bins, dtype=jnp.int32)
    in_bin = bins[:, None] == (edit_pos // POOL)[None, :]
    is_base = edit_tok[:, None] == jnp.arange(BASES, dtype=jnp.int32)[None, :]
    counts = jnp.dot(
        in_bin.astype(jnp.bfloat16), is_base.astype(jnp.bfloat16), preferred_element_type=jnp.float32
    ).astype(jnp.bfloat16)
    take = (
        jnp.arange(shard_bins, dtype=jnp.int32)[None, :] // POOL
        == jnp.arange(pooled_bins, dtype=jnp.int32)[:, None]
    ).astype(jnp.bfloat16)
    summed = jnp.dot(take, embedding, preferred_element_type=jnp.float32) + jnp.dot(
        counts, bases_table, preferred_element_type=jnp.float32
    )
    pooled = (summed * (1.0 / POOL)).astype(jnp.bfloat16)
    both = jnp.concatenate([w_row, w_col], axis=1)
    return jnp.dot(pooled, both, preferred_element_type=jnp.float32).astype(jnp.bfloat16)


def gathered(block):
    count = lax.axis_size(("row", "col"))
    copies = jnp.broadcast_to(block[None], (count, *block.shape))
    got = lax.all_to_all(copies, ("row", "col"), 0, 0)
    return got.reshape(count * block.shape[0], block.shape[1])


def mirrored_tile(score):
    n_rows, n_cols = lax.axis_size("row"), lax.axis_size("col")
    row_at, col_at = lax.axis_index("row"), lax.axis_index("col")
    height, breadth = score.shape
    size = min(height, breadth)
    wide = breadth > height
    parts = max(height, breadth) // size
    pieces = jnp.stack(
        [
            (score[:, k * size : (k + 1) * size] if wide else score[k * size : (k + 1) * size]).T
            for k in range(parts)
        ]
    )
    own = (row_at if wide else col_at) % parts
    received = []
    for turn in range(parts):
        pairs = []
        for r in range(n_rows):
            for c in range(n_cols):
                if wide:
                    to = (parts * c + (turn + r) % parts, r // parts)
                else:
                    to = (c // parts, parts * r + (turn + c) % parts)
                pairs.append((r * n_cols + c, to[0] * n_cols + to[1]))
        piece = lax.dynamic_index_in_dim(pieces, (own + turn) % parts, 0, keepdims=False)
        received.append(lax.ppermute(piece, ("row", "col"), pairs))
    stacked = jnp.stack(received)
    placed = [
        lax.dynamic_index_in_dim(stacked, (own - sub) % parts, 0, keepdims=False) for sub in range(parts)
    ]
    return jnp.concatenate(placed, axis=1 if wide else 0)


def relu(x):
    return jnp.maximum(x, 0.0)


def map_kernel(
    map_bins, height, breadth, at_ref, proj_ref, gain_ref, first_ref, second_ref, head_ref,
    score_ref, row_ref, col_ref, dist_ref, pair_ref, hidden_ref,
):
    channels = gain_ref.shape[1]
    wide = breadth + 2 * PAD
    pair_rows = height + 2 * MARGIN
    hidden_rows = height + 2 * SECOND_SPACING
    row_start = pl.multiple_of(at_ref[0], height)
    col_start = pl.multiple_of(at_ref[1], breadth)
    outside = jnp.full((PAD, channels), OUTSIDE, jnp.float32)
    for part, ref in enumerate((row_ref, col_ref)):
        ref[:PAD] = outside
        ref[PAD + map_bins :] = outside
        ref[PAD : PAD + map_bins] = proj_ref[:, part * channels : (part + 1) * channels].astype(
            jnp.float32
        )
    span = dist_ref.shape[0]
    step = lax.broadcasted_iota(jnp.int32, (span, channels), 0) - (pair_rows - 1)
    apart = jnp.abs(step + (col_start - PAD - row_start + MARGIN)).astype(jnp.float32)
    dist_ref[...] = gain_ref[...] * (jnp.log1p(apart) * (1.0 / math.log(map_bins)))
    col_part = col_ref[pl.ds(col_start, wide)]

    def build(p):
        row_part = row_ref[pl.ds(row_start + (PAD - MARGIN) + p, 1)]
        value = relu(col_part + dist_ref[pl.ds(pair_rows - 1 - p, wide)] + row_part)
        shifted = [pltpu.roll(value, FIRST_SPACING, 0), value, pltpu.roll(value, wide - FIRST_SPACING, 0)]
        pair_ref[p] = jnp.concatenate([x.astype(jnp.bfloat16) for x in shifted], axis=1)

    pl.loop(0, pair_rows, unroll=4)(build)

    def paired(ref, start, offsets, spacing, weight):
        lhs = jnp.concatenate(
            [
                jnp.concatenate([ref[start + base + k * spacing] for k in range(4)], axis=1)
                for base in offsets
            ],
            axis=0,
        )
        return jnp.dot(lhs, weight[...], preferred_element_type=jnp.float32)

    first_offsets = (0, 1, 4, 5)

    @pl.loop(0, hidden_rows // 8)
    def first_layer(m):
        start = m * 8
        out = relu(paired(pair_ref, start, first_offsets, FIRST_SPACING, first_ref))
        for n, base in enumerate(first_offsets):
            for half in range(2):
                a = start + base + half * FIRST_SPACING
                conv = out[n * wide : (n + 1) * wide, half * channels : (half + 1) * channels]
                own = pair_ref[a + FIRST_SPACING, :, channels : 2 * channels].astype(jnp.float32)
                value = own + conv
                ahead = pltpu.roll(value, wide - SECOND_SPACING, 0)
                taps = [
                    ahead[:breadth],
                    value[PAD : PAD + breadth],
                    ahead[2 * SECOND_SPACING : 2 * SECOND_SPACING + breadth],
                ]
                hidden_ref[a] = jnp.concatenate([x.astype(jnp.bfloat16) for x in taps], axis=1)

    edge = SECOND_SPACING
    blank = jnp.zeros((edge, breadth, 3 * channels), jnp.bfloat16)

    @pl.when(row_start == 0)
    def _():
        hidden_ref[:edge] = blank

    @pl.when(row_start == map_bins - height)
    def _():
        hidden_ref[hidden_rows - edge :] = blank

    at_bin = lax.broadcasted_iota(jnp.int32, (hidden_rows, 16, channels), 1)

    @pl.when(col_start == 0)
    def _():
        old = hidden_ref[:, :16, :channels].astype(jnp.float32)
        hidden_ref[:, :16, :channels] = jnp.where(at_bin < edge, 0.0, old).astype(jnp.bfloat16)

    @pl.when(col_start == map_bins - breadth)
    def _():
        old = hidden_ref[:, breadth - 16 :, 2 * channels :].astype(jnp.float32)
        hidden_ref[:, breadth - 16 :, 2 * channels :] = jnp.where(
            at_bin >= 16 - edge, 0.0, old
        ).astype(jnp.bfloat16)

    second_offsets = (0, 1, 2, 3)

    @pl.loop(0, height // 8)
    def second_layer(m):
        start = pl.multiple_of(m * 8, 8)
        out = relu(paired(hidden_ref, start, second_offsets, SECOND_SPACING, second_ref))
        last = []
        for n, base in enumerate(second_offsets):
            halves = []
            for half in range(2):
                o = start + base + half * SECOND_SPACING
                conv = out[n * breadth : (n + 1) * breadth, half * channels : (half + 1) * channels]
                own = hidden_ref[o + SECOND_SPACING, :, channels : 2 * channels].astype(jnp.float32)
                halves.append((own + conv).astype(jnp.bfloat16))
            last.append(jnp.concatenate(halves, axis=1))
        got = lax.dot_general(
            head_ref[...],
            jnp.concatenate(last, axis=0),
            (((1,), (1,)), ((), ())),
            preferred_element_type=jnp.float32,
        )
        lines = [got[half : half + 1, n * breadth : (n + 1) * breadth] for half in range(2) for n in range(4)]
        score_ref[pl.ds(start, 8)] = jnp.concatenate(lines, axis=0)


def tile_scores(every, at, dist_gain, first_kernel, second_kernel, head_weight, height, breadth):
    map_bins = every.shape[0]
    channels = dist_gain.shape[0]
    wide = breadth + 2 * PAD
    pair_rows = height + 2 * MARGIN
    span = -(-(pair_rows + wide) // 8) * 8
    nothing = jnp.zeros((3 * channels, channels), jnp.bfloat16)

    def paired_weight(kernel):
        taps = [kernel[a].reshape(3 * channels, channels) for a in range(3)]
        left = jnp.concatenate([*taps, nothing], axis=0)
        right = jnp.concatenate([nothing, *taps], axis=0)
        return jnp.concatenate([left, right], axis=1)

    zero = jnp.zeros_like(head_weight)
    head = jnp.stack(
        [jnp.concatenate([head_weight, zero]), jnp.concatenate([zero, head_weight])]
        + [jnp.concatenate([zero, zero])] * 14
    )
    return pl.pallas_call(
        functools.partial(map_kernel, map_bins, height, breadth),
        out_shape=jax.ShapeDtypeStruct((height, breadth), jnp.float32),
        in_specs=[pl.BlockSpec(memory_space=pltpu.SMEM)] + [pl.BlockSpec(memory_space=pltpu.VMEM)] * 5,
        out_specs=pl.BlockSpec(memory_space=pltpu.VMEM),
        scratch_shapes=[
            pltpu.VMEM((map_bins + 2 * PAD, channels), jnp.float32),
            pltpu.VMEM((map_bins + 2 * PAD, channels), jnp.float32),
            pltpu.VMEM((span, channels), jnp.float32),
            pltpu.VMEM((pair_rows, wide, 3 * channels), jnp.bfloat16),
            pltpu.VMEM((height + 2 * SECOND_SPACING, breadth, 3 * channels), jnp.bfloat16),
        ],
        compiler_params=pltpu.CompilerParams(vmem_limit_bytes=40 * 1024 * 1024),
    )(at, every, dist_gain[None], paired_weight(first_kernel), paired_weight(second_kernel), head)


def on_device(
    embedding,
    bases_table,
    edit_pos,
    edit_tok,
    w_row,
    w_col,
    dist_gain,
    first_kernel,
    second_kernel,
    head_weight,
):
    n_rows, n_cols = lax.axis_size("row"), lax.axis_size("col")
    row_at, col_at = lax.axis_index("row"), lax.axis_index("col")
    shard_bins = embedding.shape[0]
    map_bins = shard_bins * n_rows * n_cols // POOL
    height, breadth = map_bins // n_rows, map_bins // n_cols
    first_bin = (row_at * n_cols + col_at) * shard_bins
    block = projected(embedding, bases_table, edit_pos, edit_tok, w_row, w_col, first_bin)
    at = jnp.stack([row_at * height, col_at * breadth]).astype(jnp.int32)
    score = tile_scores(
        gathered(block), at, dist_gain, first_kernel, second_kernel, head_weight, height, breadth
    )
    return 0.5 * (score + mirrored_tile(score))


def solution(mesh):
    placed = (P(("row", "col"), None), P(), P("cand"), P("cand"), P(), P(), P(), P(), P(), P())
    return jax.shard_map(
        on_device, mesh=mesh, in_specs=placed, out_specs=P(("cand", "row"), "col"), check_vma=False
    )
```

```python
import functools
import math

import jax
import jax.numpy as jnp
from jax import lax
from jax.experimental import pallas as pl
from jax.experimental.pallas import tpu as pltpu
from jax.sharding import PartitionSpec as P

POOL = 4
FIRST_SPACING = 2
SECOND_SPACING = 4
BASES = 4
MARGIN = FIRST_SPACING + SECOND_SPACING
PAD = 8
GROUP = 8
OUTSIDE = -1e30


def project_kernel(
    at_ref, embedding_ref, bases_ref, pos_ref, tok_ref, w_row_ref, w_col_ref, copies_ref
):
    shard_bins = embedding_ref.shape[0]
    copies, pooled_bins, _ = copies_ref.shape
    edits = pos_ref.shape[1]
    bins = at_ref[0] + lax.broadcasted_iota(jnp.int32, (pooled_bins, edits), 0) * POOL
    ahead = pos_ref[...] - bins
    in_bin = ((ahead >= 0) & (ahead < POOL)).astype(jnp.float32)
    back = lax.broadcasted_iota(jnp.int32, (pooled_bins, shard_bins), 1) - POOL * (
        lax.broadcasted_iota(jnp.int32, (pooled_bins, shard_bins), 0)
    )
    take = ((back >= 0) & (back < POOL)).astype(jnp.float32).astype(jnp.bfloat16)
    summed = jnp.dot(take, embedding_ref[...], preferred_element_type=jnp.float32)
    for base in range(BASES):
        is_base = (tok_ref[...] == base).astype(jnp.float32)
        count = jnp.sum(in_bin * is_base, axis=1, keepdims=True)
        summed = summed + count * bases_ref[base : base + 1].astype(jnp.float32)
    pooled = (summed * (1.0 / POOL)).astype(jnp.bfloat16)
    both = jnp.concatenate(
        [
            jnp.dot(pooled, ref[...], preferred_element_type=jnp.float32).astype(jnp.bfloat16)
            for ref in (w_row_ref, w_col_ref)
        ],
        axis=1,
    )
    for k in range(copies):
        copies_ref[k] = both


def projected(embedding, bases_table, edit_pos, edit_tok, w_row, w_col, first_bin, copies):
    vmem = pl.BlockSpec(memory_space=pltpu.VMEM)
    return pl.pallas_call(
        project_kernel,
        out_shape=jax.ShapeDtypeStruct(
            (copies, embedding.shape[0] // POOL, 2 * w_row.shape[1]), jnp.bfloat16
        ),
        in_specs=[pl.BlockSpec(memory_space=pltpu.SMEM)] + [vmem] * 6,
        out_specs=vmem,
        compiler_params=pltpu.CompilerParams(vmem_limit_bytes=16 * 1024 * 1024),
    )(first_bin[None].astype(jnp.int32), embedding, bases_table, edit_pos[None], edit_tok[None], w_row, w_col)


def gathered(copies):
    got = lax.all_to_all(copies, ("row", "col"), 0, 0)
    return got.reshape(-1, got.shape[2])


def join_kernel(wide, at_ref, score_ref, *refs):
    *received_refs, out_ref = refs
    parts = len(received_refs)
    size = min(score_ref.shape)
    pieces = [ref[...].T for ref in received_refs]
    for sub in range(parts):
        piece = pieces[0]
        for turn in range(1, parts):
            piece = jnp.where((sub + turn) % parts == at_ref[0], pieces[turn], piece)
        along = slice(sub * size, (sub + 1) * size)
        where = (slice(None), along) if wide else (along, slice(None))
        out_ref[where] = 0.5 * (score_ref[where] + piece)


def symmetrised(score):
    n_rows, n_cols = lax.axis_size("row"), lax.axis_size("col")
    row_at, col_at = lax.axis_index("row"), lax.axis_index("col")
    height, breadth = score.shape
    size = min(height, breadth)
    wide = breadth > height
    parts = max(height, breadth) // size
    own = (row_at if wide else col_at) % parts
    received = []
    for turn in range(parts):
        pairs = []
        for r in range(n_rows):
            for c in range(n_cols):
                if wide:
                    to = (parts * c + (turn + r) % parts, r // parts)
                else:
                    to = (c // parts, parts * r + (turn + c) % parts)
                pairs.append((r * n_cols + c, to[0] * n_cols + to[1]))
        first = ((own + turn) % parts) * size
        piece = lax.dynamic_slice(score, (0, first) if wide else (first, 0), (size, size))
        received.append(lax.ppermute(piece, ("row", "col"), pairs))
    vmem = pl.BlockSpec(memory_space=pltpu.VMEM)
    return pl.pallas_call(
        functools.partial(join_kernel, wide),
        out_shape=jax.ShapeDtypeStruct(score.shape, jnp.float32),
        in_specs=[pl.BlockSpec(memory_space=pltpu.SMEM)] + [vmem] * (1 + parts),
        out_specs=vmem,
    )(own[None].astype(jnp.int32), score, *received)


def relu(x):
    return jnp.maximum(x, 0.0)


def map_kernel(
    map_bins, height, breadth, at_ref, proj_ref, gain_ref, first_ref, second_ref, head_ref,
    score_ref, row_ref, col_ref, dist_ref, pair_ref, hidden_ref, pairs_one_ref, pairs_two_ref,
):
    channels = gain_ref.shape[1]
    wide = breadth + 2 * PAD
    pair_rows = height + 2 * MARGIN
    hidden_rows = height + 2 * SECOND_SPACING
    row_start = pl.multiple_of(at_ref[0], height)
    col_start = pl.multiple_of(at_ref[1], breadth)
    depth = 3 * channels
    for ref, given in ((pairs_one_ref, first_ref), (pairs_two_ref, second_ref)):
        ref[: 3 * depth, :channels] = given[...]
        ref[3 * depth :, :channels] = jnp.zeros((depth, channels), jnp.bfloat16)
        ref[:depth, channels:] = jnp.zeros((depth, channels), jnp.bfloat16)
        ref[depth:, channels:] = given[...]
    outside = jnp.full((PAD, channels), OUTSIDE, jnp.float32)
    for part, ref in enumerate((row_ref, col_ref)):
        ref[:PAD] = outside
        ref[PAD + map_bins :] = outside
        ref[PAD : PAD + map_bins] = proj_ref[:, part * channels : (part + 1) * channels].astype(
            jnp.float32
        )
    span = dist_ref.shape[0]
    step = lax.broadcasted_iota(jnp.int32, (span, channels), 0) - (pair_rows - 1)
    apart = jnp.abs(step + (col_start - PAD - row_start + MARGIN)).astype(jnp.float32)
    dist_ref[...] = gain_ref[...] * (jnp.log1p(apart) * (1.0 / math.log(map_bins)))
    at_edge = lax.broadcasted_iota(jnp.int32, (PAD, channels), 0)
    edge = SECOND_SPACING
    left = jnp.where((at_edge >= edge) | (col_start > 0), 1.0, 0.0)
    right = jnp.where((at_edge < PAD - edge) | (col_start < map_bins - breadth), 1.0, 0.0)
    above = jnp.where(row_start > 0, 1.0, 0.0)
    below = jnp.where(row_start < map_bins - height, 1.0, 0.0)

    def build(p):
        row_part = row_ref[pl.ds(row_start + (PAD - MARGIN + p), 1)]
        value = relu(
            col_ref[pl.ds(col_start, wide)] + dist_ref[pair_rows - 1 - p : pair_rows - 1 - p + wide] + row_part
        )
        shifted = [pltpu.roll(value, FIRST_SPACING, 0), value, pltpu.roll(value, wide - FIRST_SPACING, 0)]
        pair_ref[p] = jnp.concatenate([x.astype(jnp.bfloat16) for x in shifted], axis=1)

    def paired(ref, start, offsets, spacing, weight):
        lhs = jnp.concatenate(
            [
                jnp.concatenate([ref[start + base + k * spacing] for k in range(4)], axis=1)
                for base in offsets
            ],
            axis=0,
        )
        return jnp.dot(lhs, weight[...], preferred_element_type=jnp.float32)

    def keep_hidden(start, offsets, out):
        for n, base in enumerate(offsets):
            for half in range(2):
                a = start + base + half * FIRST_SPACING
                conv = out[n * wide : (n + 1) * wide, half * channels : (half + 1) * channels]
                own = pair_ref[a + FIRST_SPACING, :, channels : 2 * channels].astype(jnp.float32)
                value = own + relu(conv)
                if a < edge:
                    value = value * above
                if a >= hidden_rows - edge:
                    value = value * below
                ahead = pltpu.roll(value, wide - edge, 0)
                taps = [
                    jnp.concatenate([ahead[:PAD] * left, ahead[PAD:breadth]], axis=0),
                    value[PAD : PAD + breadth],
                    jnp.concatenate([ahead[PAD:breadth], ahead[breadth : breadth + PAD] * right], axis=0),
                ]
                hidden_ref[a] = jnp.concatenate([x.astype(jnp.bfloat16) for x in taps], axis=1)

    def keep_score(start, offsets, out):
        last = []
        for n, base in enumerate(offsets):
            halves = []
            for half in range(2):
                o = start + base + half * edge
                conv = out[n * breadth : (n + 1) * breadth, half * channels : (half + 1) * channels]
                own = hidden_ref[o + edge, :, channels : 2 * channels].astype(jnp.float32)
                halves.append((own + relu(conv)).astype(jnp.bfloat16))
            last.append(jnp.concatenate(halves, axis=1))
        got = lax.dot_general(
            head_ref[...],
            jnp.concatenate(last, axis=0),
            (((1,), (1,)), ((), ())),
            preferred_element_type=jnp.float32,
        )
        count = len(offsets)
        lines = [got[half : half + 1, n * breadth : (n + 1) * breadth] for half in range(2) for n in range(count)]
        score_ref[start : start + 8] = jnp.concatenate(lines, axis=0)

    first_offsets, second_offsets = (0, 1, 4, 5), (0, 1, 2, 3)
    first_groups, second_groups = hidden_rows // GROUP, height // GROUP
    for p in range(2 * GROUP):
        build(p)
    for s in range(first_groups + 1):
        one = two = None
        if s < first_groups:
            one = paired(pair_ref, s * GROUP, first_offsets, FIRST_SPACING, pairs_one_ref)
        for p in range((s + 2) * GROUP, min((s + 3) * GROUP, pair_rows)):
            build(p)
        if 0 <= s - 2 < second_groups:
            two = paired(hidden_ref, (s - 2) * GROUP, second_offsets, SECOND_SPACING, pairs_two_ref)
        if one is not None:
            keep_hidden(s * GROUP, first_offsets, one)
        if two is not None:
            keep_score((s - 2) * GROUP, second_offsets, two)


def tile_scores(every, at, dist_gain, first_kernel, second_kernel, head_weight, height, breadth):
    map_bins = every.shape[0]
    channels = dist_gain.shape[0]
    wide = breadth + 2 * PAD
    pair_rows = height + 2 * MARGIN
    span = -(-(pair_rows + wide) // 8) * 8
    zero = jnp.zeros_like(head_weight)
    head = jnp.stack(
        [jnp.concatenate([head_weight, zero]), jnp.concatenate([zero, head_weight])]
        + [jnp.concatenate([zero, zero])] * 14
    )
    return pl.pallas_call(
        functools.partial(map_kernel, map_bins, height, breadth),
        out_shape=jax.ShapeDtypeStruct((height, breadth), jnp.float32),
        in_specs=[pl.BlockSpec(memory_space=pltpu.SMEM)] + [pl.BlockSpec(memory_space=pltpu.VMEM)] * 5,
        out_specs=pl.BlockSpec(memory_space=pltpu.VMEM),
        scratch_shapes=[
            pltpu.VMEM((map_bins + 2 * PAD, channels), jnp.float32),
            pltpu.VMEM((map_bins + 2 * PAD, channels), jnp.float32),
            pltpu.VMEM((span, channels), jnp.float32),
            pltpu.VMEM((pair_rows, wide, 3 * channels), jnp.bfloat16),
            pltpu.VMEM((height + 2 * SECOND_SPACING, breadth, 3 * channels), jnp.bfloat16),
            pltpu.VMEM((12 * channels, 2 * channels), jnp.bfloat16),
            pltpu.VMEM((12 * channels, 2 * channels), jnp.bfloat16),
        ],
        compiler_params=pltpu.CompilerParams(vmem_limit_bytes=40 * 1024 * 1024),
    )(
        at,
        every,
        dist_gain[None],
        first_kernel.reshape(9 * channels, channels),
        second_kernel.reshape(9 * channels, channels),
        head,
    )


def on_device(
    embedding,
    bases_table,
    edit_pos,
    edit_tok,
    w_row,
    w_col,
    dist_gain,
    first_kernel,
    second_kernel,
    head_weight,
):
    n_rows, n_cols = lax.axis_size("row"), lax.axis_size("col")
    row_at, col_at = lax.axis_index("row"), lax.axis_index("col")
    shard_bins = embedding.shape[0]
    map_bins = shard_bins * n_rows * n_cols // POOL
    height, breadth = map_bins // n_rows, map_bins // n_cols
    first_bin = (row_at * n_cols + col_at) * shard_bins
    copies = projected(
        embedding, bases_table, edit_pos, edit_tok, w_row, w_col, first_bin, n_rows * n_cols
    )
    at = jnp.stack([row_at * height, col_at * breadth]).astype(jnp.int32)
    score = tile_scores(
        gathered(copies), at, dist_gain, first_kernel, second_kernel, head_weight, height, breadth
    )
    return symmetrised(score)


def solution(mesh):
    placed = (P(("row", "col"), None), P(), P("cand"), P("cand"), P(), P(), P(), P(), P(), P())
    return jax.shard_map(
        on_device, mesh=mesh, in_specs=placed, out_specs=P(("cand", "row"), "col"), check_vma=False
    )
```

```python
import functools
import math

import jax
import jax.numpy as jnp
from jax import lax
from jax.experimental import pallas as pl
from jax.experimental.pallas import tpu as pltpu
from jax.sharding import PartitionSpec as P

POOL = 4
FIRST_SPACING = 2
SECOND_SPACING = 4
BASES = 4
MARGIN = FIRST_SPACING + SECOND_SPACING
PAD = 8
GROUP = 8
OUTSIDE = -1e30


def plan(n_rows, n_cols):
    wide = n_rows > n_cols
    blocks = max(n_rows, n_cols)
    assert blocks == 2 * min(n_rows, n_cols)

    def owner(i, j):
        return i * n_cols + j // 2 if wide else (i // 2) * n_cols + j

    held = {}
    for i in range(blocks):
        for j in range(blocks):
            held.setdefault(owner(i, j), []).append((i, j))

    def other(device, block):
        return next(b for b in held[device] if b != block)

    jobs, target = {}, {}

    def assign(device, kept, sent):
        place = held[device].index(kept)
        jobs[device] = (*kept, *sent, int(kept[0] == kept[1]), place)
        target[device] = owner(*sent)

    def walk(device, block):
        while device not in jobs:
            if block[0] == block[1]:
                return device, block
            sent = (block[1], block[0])
            assign(device, block, sent)
            device = owner(*sent)
            block = other(device, sent)
        return None, None

    for d in range(blocks):
        start = owner(d, d)
        if start not in jobs:
            end, last = walk(start, other(start, (d, d)))
            assign(end, last, (d, d))
    for device in sorted(held):
        if device not in jobs:
            walk(device, held[device][0])
    return [jobs[device] for device in sorted(jobs)], target


def relu(x):
    return jnp.maximum(x, 0.0)


def lookup(table):
    n_cols = lax.axis_size("col")
    here = lax.axis_index("row") * n_cols + lax.axis_index("col")
    found = []
    for values in zip(*table):
        value = jnp.int32(values[0])
        for device in range(1, len(values)):
            value = jnp.where(here == device, jnp.int32(values[device]), value)
        found.append(value)
    return found


def project_kernel(
    map_bins, embedding_hbm, bases_hbm, pos_hbm, tok_hbm, w_row_hbm, w_col_hbm, gain_hbm, head_hbm,
    copies_ref, dist_ref, head_ref,
    embedding_ref, bases_ref, pos_ref, tok_ref, w_row_ref, w_col_ref, gain_ref, weight_ref, arrived,
):
    moves = [
        pltpu.make_async_copy(source, target, arrived.at[n])
        for n, (source, target) in enumerate(
            (
                (embedding_hbm, embedding_ref),
                (w_row_hbm, w_row_ref),
                (w_col_hbm, w_col_ref),
                (pos_hbm, pos_ref),
                (tok_hbm, tok_ref),
                (bases_hbm, bases_ref),
                (gain_hbm, gain_ref),
                (head_hbm, weight_ref),
            )
        )
    ]
    for move in moves:
        move.start()
    got_embedding, got_w_row, got_w_col, *small = moves
    shard_bins = embedding_ref.shape[0]
    copies, pooled_bins, _ = copies_ref.shape
    channels = gain_ref.shape[1]
    edits = pos_ref.shape[1]
    span = dist_ref.shape[0]
    apart = jnp.abs(lax.broadcasted_iota(jnp.int32, (span, channels), 0) - span // 2)
    feature = jnp.log1p(apart.astype(jnp.float32)) * (1.0 / math.log(map_bins))
    first_bin = (lax.axis_index("row") * lax.axis_size("col") + lax.axis_index("col")) * shard_bins
    bins = first_bin + lax.broadcasted_iota(jnp.int32, (pooled_bins, edits), 0) * POOL
    back = lax.broadcasted_iota(jnp.int32, (pooled_bins, shard_bins), 1) - POOL * (
        lax.broadcasted_iota(jnp.int32, (pooled_bins, shard_bins), 0)
    )
    take = ((back >= 0) & (back < POOL)).astype(jnp.float32).astype(jnp.bfloat16)
    for move in small:
        move.wait()
    dist_ref[...] = gain_ref[...] * feature
    weight = jnp.concatenate([weight_ref[...].astype(jnp.float32)] * 2, axis=1)
    line = lax.broadcasted_iota(jnp.int32, head_ref.shape, 0)
    half = lax.broadcasted_iota(jnp.int32, head_ref.shape, 1) >= channels
    head_ref[...] = jnp.where(line == half.astype(jnp.int32), weight, 0.0).astype(jnp.bfloat16)
    ahead = pos_ref[...] - bins
    in_bin = ((ahead >= 0) & (ahead < POOL)).astype(jnp.float32)
    edited = None
    for base in range(BASES):
        is_base = (tok_ref[...] == base).astype(jnp.float32)
        count = jnp.sum(in_bin * is_base, axis=1, keepdims=True)
        term = count * bases_ref[base : base + 1].astype(jnp.float32)
        edited = term if edited is None else edited + term
    got_embedding.wait()
    summed = edited + jnp.dot(take, embedding_ref[...], preferred_element_type=jnp.float32)
    pooled = (summed * (1.0 / POOL)).astype(jnp.bfloat16)
    sides = []
    for move, ref in ((got_w_row, w_row_ref), (got_w_col, w_col_ref)):
        move.wait()
        sides.append(jnp.dot(pooled, ref[...], preferred_element_type=jnp.float32).astype(jnp.bfloat16))
    both = jnp.concatenate(sides, axis=1)
    for k in range(copies):
        copies_ref[k] = both


def projected(embedding, bases_table, edit_pos, edit_tok, w_row, w_col, dist_gain, head_weight, map_bins, copies):
    vmem = pl.BlockSpec(memory_space=pltpu.VMEM)
    operands = (
        embedding,
        bases_table,
        edit_pos[None],
        edit_tok[None],
        w_row,
        w_col,
        dist_gain[None],
        head_weight[None],
    )
    channels = w_row.shape[1]
    return pl.pallas_call(
        functools.partial(project_kernel, map_bins),
        out_shape=(
            jax.ShapeDtypeStruct((copies, embedding.shape[0] // POOL, 2 * channels), jnp.bfloat16),
            jax.ShapeDtypeStruct((2 * map_bins + 4 * PAD, channels), jnp.float32),
            jax.ShapeDtypeStruct((16, 2 * channels), jnp.bfloat16),
        ),
        in_specs=[pl.BlockSpec(memory_space=pltpu.HBM)] * 8,
        out_specs=(vmem, vmem, vmem),
        scratch_shapes=[pltpu.VMEM(x.shape, x.dtype) for x in operands] + [pltpu.SemaphoreType.DMA((8,))],
        compiler_params=pltpu.CompilerParams(vmem_limit_bytes=16 * 1024 * 1024),
    )(*operands)


def map_kernel(
    map_bins, size, table, proj_ref, dist_table_ref, first_ref, second_ref, head_ref,
    kept_ref, sent_ref, row_ref, col_ref, pair_ref, hidden_ref, pairs_one_ref, pairs_two_ref, score_ref,
):
    channels = dist_table_ref.shape[1]
    block_wide = size + 2 * PAD
    wide = 2 * block_wide
    breadth = 2 * size
    pair_rows = size + 2 * MARGIN
    hidden_rows = size + 2 * SECOND_SPACING
    depth = 3 * channels
    edge = SECOND_SPACING
    row_a, col_a, row_b, col_b, diagonal, _ = lookup(table)
    blocks = [
        (pl.multiple_of(row_a * size, size), pl.multiple_of(col_a * size, size)),
        (pl.multiple_of(row_b * size, size), pl.multiple_of(col_b * size, size)),
    ]
    outside = jnp.full((PAD, channels), OUTSIDE, jnp.float32)
    for part, ref in enumerate((row_ref, col_ref)):
        ref[:PAD] = outside
        ref[PAD + map_bins :] = outside
        ref[PAD : PAD + map_bins] = proj_ref[:, part * channels : (part + 1) * channels].astype(
            jnp.float32
        )
    for ref, given in ((pairs_one_ref, first_ref), (pairs_two_ref, second_ref)):
        ref[: 3 * depth, :channels] = given[...]
        ref[3 * depth :, :channels] = jnp.zeros((depth, channels), jnp.bfloat16)
        ref[:depth, channels:] = jnp.zeros((depth, channels), jnp.bfloat16)
        ref[depth:, channels:] = given[...]
    zero_apart = dist_table_ref.shape[0] // 2
    at_edge = lax.broadcasted_iota(jnp.int32, (PAD, channels), 0)
    last_start = map_bins - size
    left = [jnp.where((at_edge >= edge) | (col > 0), 1.0, 0.0) for _, col in blocks]
    right = [jnp.where((at_edge < PAD - edge) | (col < last_start), 1.0, 0.0) for _, col in blocks]
    above = [jnp.where(row > 0, 1.0, 0.0) for row, _ in blocks]
    below = [jnp.where(row < last_start, 1.0, 0.0) for row, _ in blocks]

    def build(p):
        values = []
        for row, col in blocks:
            row_part = row_ref[pl.ds(row + (PAD - MARGIN + p), 1)]
            apart = dist_table_ref[pl.ds(col - row + (zero_apart - PAD + MARGIN - p), block_wide)]
            values.append(relu(col_ref[pl.ds(col, block_wide)] + apart + row_part))
        value = jnp.concatenate(values, axis=0)
        shifted = [pltpu.roll(value, FIRST_SPACING, 0), value, pltpu.roll(value, wide - FIRST_SPACING, 0)]
        pair_ref[p] = jnp.concatenate([x.astype(jnp.bfloat16) for x in shifted], axis=1)

    def paired(ref, start, offsets, spacing, weight):
        lhs = jnp.concatenate(
            [
                jnp.concatenate([ref[start + base + k * spacing] for k in range(4)], axis=1)
                for base in offsets
            ],
            axis=0,
        )
        return jnp.dot(lhs, weight[...], preferred_element_type=jnp.float32)

    def keep_hidden(start, offsets, out):
        for n, base in enumerate(offsets):
            for half in range(2):
                a = start + base + half * FIRST_SPACING
                conv = out[n * wide : (n + 1) * wide, half * channels : (half + 1) * channels]
                own = pair_ref[a + FIRST_SPACING, :, channels : 2 * channels].astype(jnp.float32)
                value = own + relu(conv)
                for rows, flags in ((a < edge, above), (a >= hidden_rows - edge, below)):
                    if rows:
                        value = jnp.concatenate(
                            [value[:block_wide] * flags[0], value[block_wide:] * flags[1]], axis=0
                        )
                ahead = pltpu.roll(value, wide - edge, 0)
                before, middle, after = [], [], []
                for b in range(2):
                    at = b * block_wide
                    before += [ahead[at : at + PAD] * left[b], ahead[at + PAD : at + size]]
                    middle += [value[at + PAD : at + PAD + size]]
                    after += [ahead[at + PAD : at + size], ahead[at + size : at + size + PAD] * right[b]]
                hidden_ref[a] = jnp.concatenate(
                    [jnp.concatenate(x, axis=0).astype(jnp.bfloat16) for x in (before, middle, after)], axis=1
                )

    def keep_score(start, offsets, out):
        last = []
        for n, base in enumerate(offsets):
            halves = []
            for half in range(2):
                o = start + base + half * edge
                conv = out[n * breadth : (n + 1) * breadth, half * channels : (half + 1) * channels]
                own = hidden_ref[o + edge, :, channels : 2 * channels].astype(jnp.float32)
                halves.append((own + relu(conv)).astype(jnp.bfloat16))
            last.append(jnp.concatenate(halves, axis=1))
        got = lax.dot_general(
            head_ref[...],
            jnp.concatenate(last, axis=0),
            (((1,), (1,)), ((), ())),
            preferred_element_type=jnp.float32,
        )
        count = len(offsets)
        lines = [got[half : half + 1, n * breadth : (n + 1) * breadth] for half in range(2) for n in range(count)]
        score_ref[start : start + 8] = jnp.concatenate(lines, axis=0)

    first_offsets, second_offsets = (0, 1, 4, 5), (0, 1, 2, 3)
    first_groups, second_groups = hidden_rows // GROUP, size // GROUP
    for p in range(2 * GROUP):
        build(p)
    for s in range(first_groups + 1):
        one = two = None
        if s < first_groups:
            one = paired(pair_ref, s * GROUP, first_offsets, FIRST_SPACING, pairs_one_ref)
        for p in range((s + 2) * GROUP, min((s + 3) * GROUP, pair_rows)):
            build(p)
        if 0 <= s - 2 < second_groups:
            two = paired(hidden_ref, (s - 2) * GROUP, second_offsets, SECOND_SPACING, pairs_two_ref)
        if one is not None:
            keep_hidden(s * GROUP, first_offsets, one)
        if two is not None:
            keep_score((s - 2) * GROUP, second_offsets, two)
    score = score_ref[...]
    turned = score.T
    first, second = score[:, :size], score[:, size:]
    turned_first, turned_second = turned[:size], turned[size:]
    alone = diagonal == 1
    kept_ref[...] = 0.5 * (first + jnp.where(alone, turned_first, turned_second))
    sent_ref[...] = 0.5 * (second + jnp.where(alone, turned_second, turned_first))


def block_scores(every, dist_table, first_kernel, second_kernel, head, size, table):
    map_bins = every.shape[0]
    channels = dist_table.shape[1]
    wide = 2 * (size + 2 * PAD)
    vmem = pl.BlockSpec(memory_space=pltpu.VMEM)
    block = jax.ShapeDtypeStruct((size, size), jnp.float32)
    return pl.pallas_call(
        functools.partial(map_kernel, map_bins, size, table),
        out_shape=(block, block),
        in_specs=[vmem] * 5,
        out_specs=(vmem, vmem),
        scratch_shapes=[
            pltpu.VMEM((map_bins + 2 * PAD, channels), jnp.float32),
            pltpu.VMEM((map_bins + 2 * PAD, channels), jnp.float32),
            pltpu.VMEM((size + 2 * MARGIN, wide, 3 * channels), jnp.bfloat16),
            pltpu.VMEM((size + 2 * SECOND_SPACING, 2 * size, 3 * channels), jnp.bfloat16),
            pltpu.VMEM((12 * channels, 2 * channels), jnp.bfloat16),
            pltpu.VMEM((12 * channels, 2 * channels), jnp.bfloat16),
            pltpu.VMEM((size, 2 * size), jnp.float32),
        ],
        compiler_params=pltpu.CompilerParams(vmem_limit_bytes=40 * 1024 * 1024),
    )(
        every,
        dist_table,
        first_kernel.reshape(9 * channels, channels),
        second_kernel.reshape(9 * channels, channels),
        head,
    )


def on_device(
    embedding,
    bases_table,
    edit_pos,
    edit_tok,
    w_row,
    w_col,
    dist_gain,
    first_kernel,
    second_kernel,
    head_weight,
):
    n_rows, n_cols = lax.axis_size("row"), lax.axis_size("col")
    devices = n_rows * n_cols
    map_bins = embedding.shape[0] * devices // POOL
    table, target = plan(n_rows, n_cols)
    size = map_bins // max(n_rows, n_cols)
    copies, dist_table, head = projected(
        embedding, bases_table, edit_pos, edit_tok, w_row, w_col, dist_gain, head_weight, map_bins, devices
    )
    got = lax.all_to_all(copies, ("row", "col"), 0, 0)
    every = got.reshape(map_bins, got.shape[2])
    kept, sent = block_scores(every, dist_table, first_kernel, second_kernel, head, size, table)
    received = lax.ppermute(sent, ("row", "col"), [(device, target[device]) for device in range(devices)])
    place = lookup(table)[5]
    axis = 1 if n_rows > n_cols else 0
    return jnp.where(
        place == 0,
        jnp.concatenate([kept, received], axis=axis),
        jnp.concatenate([received, kept], axis=axis),
    )


def solution(mesh):
    placed = (P(("row", "col"), None), P(), P("cand"), P("cand"), P(), P(), P(), P(), P(), P())
    return jax.shard_map(
        on_device, mesh=mesh, in_specs=placed, out_specs=P(("cand", "row"), "col"), check_vma=False
    )
```

```python
import functools
import math

import jax
import jax.numpy as jnp
from jax import lax
from jax.experimental import pallas as pl
from jax.experimental.pallas import tpu as pltpu
from jax.sharding import PartitionSpec as P

POOL = 4
FIRST_SPACING = 2
SECOND_SPACING = 4
BASES = 4
MARGIN = FIRST_SPACING + SECOND_SPACING
PAD = 8
GROUP = 8
OUTSIDE = -1e30


def plan(n_rows, n_cols):
    wide = n_rows > n_cols
    blocks = max(n_rows, n_cols)
    assert blocks == 2 * min(n_rows, n_cols)

    def owner(i, j):
        return i * n_cols + j // 2 if wide else (i // 2) * n_cols + j

    held = {}
    for i in range(blocks):
        for j in range(blocks):
            held.setdefault(owner(i, j), []).append((i, j))

    def other(device, block):
        return next(b for b in held[device] if b != block)

    jobs, target = {}, {}

    def assign(device, kept, sent):
        place = held[device].index(kept)
        jobs[device] = (*kept, *sent, int(kept[0] == kept[1]), place)
        target[device] = owner(*sent)

    def walk(device, block):
        while device not in jobs:
            if block[0] == block[1]:
                return device, block
            sent = (block[1], block[0])
            assign(device, block, sent)
            device = owner(*sent)
            block = other(device, sent)
        return None, None

    for d in range(blocks):
        start = owner(d, d)
        if start not in jobs:
            end, last = walk(start, other(start, (d, d)))
            assign(end, last, (d, d))
    for device in sorted(held):
        if device not in jobs:
            walk(device, held[device][0])
    return [jobs[device] for device in sorted(jobs)], target


def relu(x):
    return jnp.maximum(x, 0.0)


def lookup(table):
    n_cols = lax.axis_size("col")
    here = lax.axis_index("row") * n_cols + lax.axis_index("col")
    found = []
    for values in zip(*table):
        value = jnp.int32(values[0])
        for device in range(1, len(values)):
            value = jnp.where(here == device, jnp.int32(values[device]), value)
        found.append(value)
    return found


def project_kernel(
    map_bins, embedding_hbm, bases_hbm, pos_hbm, tok_hbm, w_row_hbm, w_col_hbm, gain_hbm, head_hbm,
    copies_ref, dist_ref, head_ref,
    embedding_ref, bases_ref, pos_ref, tok_ref, w_row_ref, w_col_ref, gain_ref, weight_ref, arrived,
):
    moves = [
        pltpu.make_async_copy(source, target, arrived.at[n])
        for n, (source, target) in enumerate(
            (
                (embedding_hbm, embedding_ref),
                (w_row_hbm, w_row_ref),
                (w_col_hbm, w_col_ref),
                (pos_hbm, pos_ref),
                (tok_hbm, tok_ref),
                (bases_hbm, bases_ref),
                (gain_hbm, gain_ref),
                (head_hbm, weight_ref),
            )
        )
    ]
    for move in moves:
        move.start()
    got_embedding, got_w_row, got_w_col, *small = moves
    shard_bins = embedding_ref.shape[0]
    copies, pooled_bins, _ = copies_ref.shape
    channels = gain_ref.shape[1]
    edits = pos_ref.shape[1]
    span = dist_ref.shape[0]
    apart = jnp.abs(lax.broadcasted_iota(jnp.int32, (span, channels), 0) - span // 2)
    feature = jnp.log1p(apart.astype(jnp.float32)) * (1.0 / math.log(map_bins))
    first_bin = (lax.axis_index("row") * lax.axis_size("col") + lax.axis_index("col")) * shard_bins
    bins = first_bin + lax.broadcasted_iota(jnp.int32, (pooled_bins, edits), 0) * POOL
    back = lax.broadcasted_iota(jnp.int32, (pooled_bins, shard_bins), 1) - POOL * (
        lax.broadcasted_iota(jnp.int32, (pooled_bins, shard_bins), 0)
    )
    take = ((back >= 0) & (back < POOL)).astype(jnp.float32).astype(jnp.bfloat16)
    for move in small:
        move.wait()
    dist_ref[...] = gain_ref[...] * feature
    weight = jnp.concatenate([weight_ref[...].astype(jnp.float32)] * 2, axis=1)
    line = lax.broadcasted_iota(jnp.int32, head_ref.shape, 0)
    half = lax.broadcasted_iota(jnp.int32, head_ref.shape, 1) >= channels
    head_ref[...] = jnp.where(line == half.astype(jnp.int32), weight, 0.0).astype(jnp.bfloat16)
    ahead = pos_ref[...] - bins
    in_bin = ((ahead >= 0) & (ahead < POOL)).astype(jnp.float32)
    edited = None
    for base in range(BASES):
        is_base = (tok_ref[...] == base).astype(jnp.float32)
        count = jnp.sum(in_bin * is_base, axis=1, keepdims=True)
        term = count * bases_ref[base : base + 1].astype(jnp.float32)
        edited = term if edited is None else edited + term
    got_embedding.wait()
    summed = edited + jnp.dot(take, embedding_ref[...], preferred_element_type=jnp.float32)
    pooled = (summed * (1.0 / POOL)).astype(jnp.bfloat16)
    sides = []
    for move, ref in ((got_w_row, w_row_ref), (got_w_col, w_col_ref)):
        move.wait()
        sides.append(jnp.dot(pooled, ref[...], preferred_element_type=jnp.float32).astype(jnp.bfloat16))
    both = jnp.concatenate(sides, axis=1)
    for k in range(copies):
        copies_ref[k] = both


def projected(embedding, bases_table, edit_pos, edit_tok, w_row, w_col, dist_gain, head_weight, map_bins, copies):
    vmem = pl.BlockSpec(memory_space=pltpu.VMEM)
    operands = (
        embedding,
        bases_table,
        edit_pos[None],
        edit_tok[None],
        w_row,
        w_col,
        dist_gain[None],
        head_weight[None],
    )
    channels = w_row.shape[1]
    return pl.pallas_call(
        functools.partial(project_kernel, map_bins),
        out_shape=(
            jax.ShapeDtypeStruct((copies, embedding.shape[0] // POOL, 2 * channels), jnp.bfloat16),
            jax.ShapeDtypeStruct((2 * map_bins + 4 * PAD, channels), jnp.float32),
            jax.ShapeDtypeStruct((16, 2 * channels), jnp.bfloat16),
        ),
        in_specs=[pl.BlockSpec(memory_space=pltpu.HBM)] * 8,
        out_specs=(vmem, vmem, vmem),
        scratch_shapes=[pltpu.VMEM(x.shape, x.dtype) for x in operands] + [pltpu.SemaphoreType.DMA((8,))],
        compiler_params=pltpu.CompilerParams(vmem_limit_bytes=60 * 1024 * 1024),
    )(*operands)


def map_kernel(
    map_bins, size, table, proj_ref, dist_table_ref, first_ref, second_ref, head_ref,
    kept_ref, sent_ref, row_ref, col_ref, pair_ref, hidden_ref, pairs_one_ref, pairs_two_ref, score_ref,
):
    channels = dist_table_ref.shape[1]
    block_wide = size + 2 * SECOND_SPACING
    wide = 2 * block_wide
    spread = block_wide + PAD
    breadth = 2 * size
    pair_rows = size + 2 * MARGIN
    hidden_rows = size + 2 * SECOND_SPACING
    depth = 3 * channels
    edge = SECOND_SPACING
    row_a, col_a, row_b, col_b, diagonal, _ = lookup(table)
    blocks = [
        (pl.multiple_of(row_a * size, size), pl.multiple_of(col_a * size, size)),
        (pl.multiple_of(row_b * size, size), pl.multiple_of(col_b * size, size)),
    ]
    outside = jnp.full((2 * PAD, channels), OUTSIDE, jnp.float32)
    for part, ref in enumerate((row_ref, col_ref)):
        ref[:PAD] = outside[:PAD]
        ref[PAD + map_bins :] = outside
        ref[PAD : PAD + map_bins] = proj_ref[:, part * channels : (part + 1) * channels].astype(
            jnp.float32
        )
    for ref, given in ((pairs_one_ref, first_ref), (pairs_two_ref, second_ref)):
        ref[: 3 * depth, :channels] = given[...]
        ref[3 * depth :, :channels] = jnp.zeros((depth, channels), jnp.bfloat16)
        ref[:depth, channels:] = jnp.zeros((depth, channels), jnp.bfloat16)
        ref[depth:, channels:] = given[...]
    zero_apart = dist_table_ref.shape[0] // 2
    at_edge = lax.broadcasted_iota(jnp.int32, (PAD, channels), 0)
    last_start = map_bins - size
    left = [jnp.where((at_edge >= edge) | (col > 0), 1.0, 0.0) for _, col in blocks]
    right = [jnp.where((at_edge < PAD - edge) | (col < last_start), 1.0, 0.0) for _, col in blocks]
    above = [jnp.where(row > 0, 1.0, 0.0) for row, _ in blocks]
    below = [jnp.where(row < last_start, 1.0, 0.0) for row, _ in blocks]

    def build(p):
        values = []
        for row, col in blocks:
            row_part = row_ref[pl.ds(row + (PAD - MARGIN + p), 1)]
            apart = dist_table_ref[pl.ds(col - row + (zero_apart - p), spread)]
            values.append(relu(col_ref[pl.ds(col + (PAD - MARGIN), spread)] + apart + row_part))
        taps = []
        for b in range(3):
            moved = [
                (pltpu.roll(x, spread - b * FIRST_SPACING, 0) if b else x)[:block_wide] for x in values
            ]
            taps.append(jnp.concatenate(moved, axis=0).astype(jnp.bfloat16))
        pair_ref[p] = jnp.concatenate(taps, axis=1)

    def paired(ref, start, offsets, spacing, weight):
        lhs = jnp.concatenate(
            [
                jnp.concatenate([ref[start + base + k * spacing] for k in range(4)], axis=1)
                for base in offsets
            ],
            axis=0,
        )
        return jnp.dot(lhs, weight[...], preferred_element_type=jnp.float32)

    def keep_hidden(start, offsets, out):
        for n, base in enumerate(offsets):
            for half in range(2):
                a = start + base + half * FIRST_SPACING
                conv = out[n * wide : (n + 1) * wide, half * channels : (half + 1) * channels]
                own = pair_ref[a + FIRST_SPACING, :, channels : 2 * channels].astype(jnp.float32)
                value = own + relu(conv)
                for rows, flags in ((a < edge, above), (a >= hidden_rows - edge, below)):
                    if rows:
                        value = jnp.concatenate(
                            [value[:block_wide] * flags[0], value[block_wide:] * flags[1]], axis=0
                        )
                ahead = pltpu.roll(value, wide - edge, 0)
                before, middle, after = [], [], []
                for b in range(2):
                    at = b * block_wide
                    before += [value[at : at + PAD] * left[b], value[at + PAD : at + size]]
                    middle += [ahead[at : at + size]]
                    after += [value[at + PAD : at + size], value[at + size : at + size + PAD] * right[b]]
                hidden_ref[a] = jnp.concatenate(
                    [jnp.concatenate(x, axis=0).astype(jnp.bfloat16) for x in (before, middle, after)], axis=1
                )

    def keep_score(start, offsets, out):
        last = []
        for n, base in enumerate(offsets):
            halves = []
            for half in range(2):
                o = start + base + half * edge
                conv = out[n * breadth : (n + 1) * breadth, half * channels : (half + 1) * channels]
                own = hidden_ref[o + edge, :, channels : 2 * channels].astype(jnp.float32)
                halves.append((own + relu(conv)).astype(jnp.bfloat16))
            last.append(jnp.concatenate(halves, axis=1))
        got = lax.dot_general(
            head_ref[...],
            jnp.concatenate(last, axis=0),
            (((1,), (1,)), ((), ())),
            preferred_element_type=jnp.float32,
        )
        count = len(offsets)
        lines = [got[half : half + 1, n * breadth : (n + 1) * breadth] for half in range(2) for n in range(count)]
        score_ref[start : start + 8] = jnp.concatenate(lines, axis=0)

    first_offsets, second_offsets = (0, 1, 4, 5), (0, 1, 2, 3)
    first_groups, second_groups = hidden_rows // GROUP, size // GROUP
    for p in range(2 * GROUP):
        build(p)
    for s in range(first_groups + 1):
        one = two = None
        if s < first_groups:
            one = paired(pair_ref, s * GROUP, first_offsets, FIRST_SPACING, pairs_one_ref)
        for p in range((s + 2) * GROUP, min((s + 3) * GROUP, pair_rows)):
            build(p)
        if 0 <= s - 2 < second_groups:
            two = paired(hidden_ref, (s - 2) * GROUP, second_offsets, SECOND_SPACING, pairs_two_ref)
        if one is not None:
            keep_hidden(s * GROUP, first_offsets, one)
        if two is not None:
            keep_score((s - 2) * GROUP, second_offsets, two)
    score = score_ref[...]
    turned = score.T
    first, second = score[:, :size], score[:, size:]
    turned_first, turned_second = turned[:size], turned[size:]
    alone = diagonal == 1
    kept_ref[...] = 0.5 * (first + jnp.where(alone, turned_first, turned_second))
    sent_ref[...] = 0.5 * (second + jnp.where(alone, turned_second, turned_first))


def block_scores(every, dist_table, first_kernel, second_kernel, head, size, table):
    map_bins = every.shape[0]
    channels = dist_table.shape[1]
    wide = 2 * (size + 2 * SECOND_SPACING)
    vmem = pl.BlockSpec(memory_space=pltpu.VMEM)
    block = jax.ShapeDtypeStruct((size, size), jnp.float32)
    return pl.pallas_call(
        functools.partial(map_kernel, map_bins, size, table),
        out_shape=(block, block),
        in_specs=[vmem] * 5,
        out_specs=(vmem, vmem),
        scratch_shapes=[
            pltpu.VMEM((map_bins + 3 * PAD, channels), jnp.float32),
            pltpu.VMEM((map_bins + 3 * PAD, channels), jnp.float32),
            pltpu.VMEM((size + 2 * MARGIN, wide, 3 * channels), jnp.bfloat16),
            pltpu.VMEM((size + 2 * SECOND_SPACING, 2 * size, 3 * channels), jnp.bfloat16),
            pltpu.VMEM((12 * channels, 2 * channels), jnp.bfloat16),
            pltpu.VMEM((12 * channels, 2 * channels), jnp.bfloat16),
            pltpu.VMEM((size, 2 * size), jnp.float32),
        ],
        compiler_params=pltpu.CompilerParams(vmem_limit_bytes=40 * 1024 * 1024),
    )(
        every,
        dist_table,
        first_kernel.reshape(9 * channels, channels),
        second_kernel.reshape(9 * channels, channels),
        head,
    )


def on_device(
    embedding,
    bases_table,
    edit_pos,
    edit_tok,
    w_row,
    w_col,
    dist_gain,
    first_kernel,
    second_kernel,
    head_weight,
):
    n_rows, n_cols = lax.axis_size("row"), lax.axis_size("col")
    devices = n_rows * n_cols
    map_bins = embedding.shape[0] * devices // POOL
    table, target = plan(n_rows, n_cols)
    size = map_bins // max(n_rows, n_cols)
    copies, dist_table, head = projected(
        embedding, bases_table, edit_pos, edit_tok, w_row, w_col, dist_gain, head_weight, map_bins, devices
    )
    got = lax.all_to_all(copies, ("row", "col"), 0, 0)
    every = got.reshape(map_bins, got.shape[2])
    kept, sent = block_scores(every, dist_table, first_kernel, second_kernel, head, size, table)
    received = lax.ppermute(sent, ("row", "col"), [(device, target[device]) for device in range(devices)])
    place = lookup(table)[5]
    axis = 1 if n_rows > n_cols else 0
    return jnp.where(
        place == 0,
        jnp.concatenate([kept, received], axis=axis),
        jnp.concatenate([received, kept], axis=axis),
    )


def solution(mesh):
    placed = (P(("row", "col"), None), P(), P("cand"), P("cand"), P(), P(), P(), P(), P(), P())
    return jax.shard_map(
        on_device, mesh=mesh, in_specs=placed, out_specs=P(("cand", "row"), "col"), check_vma=False
    )
```

```python
import functools
import math

import jax
import jax.numpy as jnp
from jax import lax
from jax.experimental import pallas as pl
from jax.experimental.pallas import tpu as pltpu
from jax.sharding import PartitionSpec as P

POOL = 4
FIRST_SPACING = 2
SECOND_SPACING = 4
BASES = 4
MARGIN = FIRST_SPACING + SECOND_SPACING
PAD = 8
GROUP = 8
OUTSIDE = -1e30


def plan(n_rows, n_cols):
    wide = n_rows > n_cols
    blocks = max(n_rows, n_cols)
    assert blocks == 2 * min(n_rows, n_cols)

    def owner(i, j):
        return i * n_cols + j // 2 if wide else (i // 2) * n_cols + j

    held = {}
    for i in range(blocks):
        for j in range(blocks):
            held.setdefault(owner(i, j), []).append((i, j))

    def other(device, block):
        return next(b for b in held[device] if b != block)

    jobs, target = {}, {}

    def assign(device, kept, sent):
        place = held[device].index(kept)
        jobs[device] = (*kept, *sent, int(kept[0] == kept[1]), place)
        target[device] = owner(*sent)

    def walk(device, block):
        while device not in jobs:
            if block[0] == block[1]:
                return device, block
            sent = (block[1], block[0])
            assign(device, block, sent)
            device = owner(*sent)
            block = other(device, sent)
        return None, None

    for d in range(blocks):
        start = owner(d, d)
        if start not in jobs:
            end, last = walk(start, other(start, (d, d)))
            assign(end, last, (d, d))
    for device in sorted(held):
        if device not in jobs:
            walk(device, held[device][0])
    return [jobs[device] for device in sorted(jobs)], target


def relu(x):
    return jnp.maximum(x, 0.0)


def lookup(table):
    n_cols = lax.axis_size("col")
    here = lax.axis_index("row") * n_cols + lax.axis_index("col")
    found = []
    for values in zip(*table):
        value = jnp.int32(values[0])
        for device in range(1, len(values)):
            value = jnp.where(here == device, jnp.int32(values[device]), value)
        found.append(value)
    return found


def project_kernel(
    map_bins, embedding_hbm, bases_hbm, pos_hbm, tok_hbm, w_row_hbm, w_col_hbm, gain_hbm, head_hbm,
    copies_ref, dist_ref, head_ref,
    embedding_ref, bases_ref, pos_ref, tok_ref, w_row_ref, w_col_ref, gain_ref, weight_ref, arrived,
):
    moves = [
        pltpu.make_async_copy(source, target, arrived.at[n])
        for n, (source, target) in enumerate(
            (
                (embedding_hbm, embedding_ref),
                (w_row_hbm, w_row_ref),
                (w_col_hbm, w_col_ref),
                (pos_hbm, pos_ref),
                (tok_hbm, tok_ref),
                (bases_hbm, bases_ref),
                (gain_hbm, gain_ref),
                (head_hbm, weight_ref),
            )
        )
    ]
    for move in moves:
        move.start()
    got_embedding, got_w_row, got_w_col, *small = moves
    shard_bins = embedding_ref.shape[0]
    copies, pooled_bins, _ = copies_ref.shape
    channels = gain_ref.shape[1]
    edits = pos_ref.shape[1]
    span = dist_ref.shape[0]
    apart = jnp.abs(lax.broadcasted_iota(jnp.int32, (span, channels), 0) - span // 2)
    feature = jnp.log1p(apart.astype(jnp.float32)) * (1.0 / math.log(map_bins))
    first_bin = (lax.axis_index("row") * lax.axis_size("col") + lax.axis_index("col")) * shard_bins
    bins = first_bin + lax.broadcasted_iota(jnp.int32, (pooled_bins, edits), 0) * POOL
    back = lax.broadcasted_iota(jnp.int32, (pooled_bins, shard_bins), 1) - POOL * (
        lax.broadcasted_iota(jnp.int32, (pooled_bins, shard_bins), 0)
    )
    take = ((back >= 0) & (back < POOL)).astype(jnp.float32).astype(jnp.bfloat16)
    for move in small:
        move.wait()
    dist_ref[...] = gain_ref[...] * feature
    weight = jnp.concatenate([weight_ref[...].astype(jnp.float32)] * 2, axis=1)
    line = lax.broadcasted_iota(jnp.int32, head_ref.shape, 0)
    half = lax.broadcasted_iota(jnp.int32, head_ref.shape, 1) >= channels
    head_ref[...] = jnp.where(line == half.astype(jnp.int32), weight, 0.0).astype(jnp.bfloat16)
    ahead = pos_ref[...] - bins
    in_bin = ((ahead >= 0) & (ahead < POOL)).astype(jnp.float32)
    edited = None
    for base in range(BASES):
        is_base = (tok_ref[...] == base).astype(jnp.float32)
        count = jnp.sum(in_bin * is_base, axis=1, keepdims=True)
        term = count * bases_ref[base : base + 1].astype(jnp.float32)
        edited = term if edited is None else edited + term
    got_embedding.wait()
    summed = edited + jnp.dot(take, embedding_ref[...], preferred_element_type=jnp.float32)
    pooled = (summed * (1.0 / POOL)).astype(jnp.bfloat16)
    sides = []
    for move, ref in ((got_w_row, w_row_ref), (got_w_col, w_col_ref)):
        move.wait()
        sides.append(jnp.dot(pooled, ref[...], preferred_element_type=jnp.float32).astype(jnp.bfloat16))
    both = jnp.concatenate(sides, axis=1)
    for k in range(copies):
        copies_ref[k] = both


def projected(embedding, bases_table, edit_pos, edit_tok, w_row, w_col, dist_gain, head_weight, map_bins, copies):
    vmem = pl.BlockSpec(memory_space=pltpu.VMEM)
    operands = (
        embedding,
        bases_table,
        edit_pos[None],
        edit_tok[None],
        w_row,
        w_col,
        dist_gain[None],
        head_weight[None],
    )
    channels = w_row.shape[1]
    return pl.pallas_call(
        functools.partial(project_kernel, map_bins),
        out_shape=(
            jax.ShapeDtypeStruct((copies, embedding.shape[0] // POOL, 2 * channels), jnp.bfloat16),
            jax.ShapeDtypeStruct((2 * map_bins + 4 * PAD, channels), jnp.float32),
            jax.ShapeDtypeStruct((16, 2 * channels), jnp.bfloat16),
        ),
        in_specs=[pl.BlockSpec(memory_space=pltpu.HBM)] * 8,
        out_specs=(vmem, vmem, vmem),
        scratch_shapes=[pltpu.VMEM(x.shape, x.dtype) for x in operands] + [pltpu.SemaphoreType.DMA((8,))],
        compiler_params=pltpu.CompilerParams(vmem_limit_bytes=16 * 1024 * 1024),
    )(*(pltpu.with_memory_space_constraint(x, pltpu.HBM) for x in operands))


def map_kernel(
    map_bins, size, table, proj_ref, dist_table_ref, first_ref, second_ref, head_ref,
    kept_ref, sent_ref, row_ref, col_ref, pair_ref, hidden_ref, pairs_one_ref, pairs_two_ref, score_ref,
):
    channels = dist_table_ref.shape[1]
    block_wide = size + 2 * SECOND_SPACING
    wide = 2 * block_wide
    spread = block_wide + PAD
    breadth = 2 * size
    pair_rows = size + 2 * MARGIN
    hidden_rows = size + 2 * SECOND_SPACING
    depth = 3 * channels
    edge = SECOND_SPACING
    row_a, col_a, row_b, col_b, diagonal, _ = lookup(table)
    blocks = [
        (pl.multiple_of(row_a * size, size), pl.multiple_of(col_a * size, size)),
        (pl.multiple_of(row_b * size, size), pl.multiple_of(col_b * size, size)),
    ]
    outside = jnp.full((2 * PAD, channels), OUTSIDE, jnp.float32)
    for part, ref in enumerate((row_ref, col_ref)):
        ref[:PAD] = outside[:PAD]
        ref[PAD + map_bins :] = outside
        ref[PAD : PAD + map_bins] = proj_ref[:, part * channels : (part + 1) * channels].astype(
            jnp.float32
        )
    for ref, given in ((pairs_one_ref, first_ref), (pairs_two_ref, second_ref)):
        ref[: 3 * depth, :channels] = given[...]
        ref[3 * depth :, :channels] = jnp.zeros((depth, channels), jnp.bfloat16)
        ref[:depth, channels:] = jnp.zeros((depth, channels), jnp.bfloat16)
        ref[depth:, channels:] = given[...]
    zero_apart = dist_table_ref.shape[0] // 2
    at_edge = lax.broadcasted_iota(jnp.int32, (PAD, channels), 0)
    last_start = map_bins - size
    left = [jnp.where((at_edge >= edge) | (col > 0), 1.0, 0.0) for _, col in blocks]
    right = [jnp.where((at_edge < PAD - edge) | (col < last_start), 1.0, 0.0) for _, col in blocks]
    above = [jnp.where(row > 0, 1.0, 0.0) for row, _ in blocks]
    below = [jnp.where(row < last_start, 1.0, 0.0) for row, _ in blocks]

    def build(p):
        values = []
        for row, col in blocks:
            row_part = row_ref[pl.ds(row + (PAD - MARGIN + p), 1)]
            apart = dist_table_ref[pl.ds(col - row + (zero_apart - p), spread)]
            values.append(relu(col_ref[pl.ds(col + (PAD - MARGIN), spread)] + apart + row_part))
        taps = []
        for b in range(3):
            moved = [
                (pltpu.roll(x, spread - b * FIRST_SPACING, 0) if b else x)[:block_wide] for x in values
            ]
            taps.append(jnp.concatenate(moved, axis=0).astype(jnp.bfloat16))
        pair_ref[p] = jnp.concatenate(taps, axis=1)

    def paired(ref, start, offsets, spacing, weight):
        lhs = jnp.concatenate(
            [
                jnp.concatenate([ref[start + base + k * spacing] for k in range(4)], axis=1)
                for base in offsets
            ],
            axis=0,
        )
        return jnp.dot(lhs, weight[...], preferred_element_type=jnp.float32)

    def keep_hidden(start, offsets, out):
        for n, base in enumerate(offsets):
            for half in range(2):
                a = start + base + half * FIRST_SPACING
                conv = out[n * wide : (n + 1) * wide, half * channels : (half + 1) * channels]
                own = pair_ref[a + FIRST_SPACING, :, channels : 2 * channels].astype(jnp.float32)
                value = own + relu(conv)
                for rows, flags in ((a < edge, above), (a >= hidden_rows - edge, below)):
                    if rows:
                        value = jnp.concatenate(
                            [value[:block_wide] * flags[0], value[block_wide:] * flags[1]], axis=0
                        )
                ahead = pltpu.roll(value, wide - edge, 0)
                before, middle, after = [], [], []
                for b in range(2):
                    at = b * block_wide
                    before += [value[at : at + PAD] * left[b], value[at + PAD : at + size]]
                    middle += [ahead[at : at + size]]
                    after += [value[at + PAD : at + size], value[at + size : at + size + PAD] * right[b]]
                hidden_ref[a] = jnp.concatenate(
                    [jnp.concatenate(x, axis=0).astype(jnp.bfloat16) for x in (before, middle, after)], axis=1
                )

    def keep_score(start, offsets, out):
        last = []
        for n, base in enumerate(offsets):
            halves = []
            for half in range(2):
                o = start + base + half * edge
                conv = out[n * breadth : (n + 1) * breadth, half * channels : (half + 1) * channels]
                own = hidden_ref[o + edge, :, channels : 2 * channels].astype(jnp.float32)
                halves.append((own + relu(conv)).astype(jnp.bfloat16))
            last.append(jnp.concatenate(halves, axis=1))
        got = lax.dot_general(
            head_ref[...],
            jnp.concatenate(last, axis=0),
            (((1,), (1,)), ((), ())),
            preferred_element_type=jnp.float32,
        )
        count = len(offsets)
        lines = [got[half : half + 1, n * breadth : (n + 1) * breadth] for half in range(2) for n in range(count)]
        score_ref[start : start + 8] = jnp.concatenate(lines, axis=0)

    first_offsets, second_offsets = (0, 1, 4, 5), (0, 1, 2, 3)
    first_groups, second_groups = hidden_rows // GROUP, size // GROUP
    for p in range(2 * GROUP):
        build(p)
    for s in range(first_groups + 1):
        one = two = None
        if s < first_groups:
            one = paired(pair_ref, s * GROUP, first_offsets, FIRST_SPACING, pairs_one_ref)
        for p in range((s + 2) * GROUP, min((s + 3) * GROUP, pair_rows)):
            build(p)
        if 0 <= s - 2 < second_groups:
            two = paired(hidden_ref, (s - 2) * GROUP, second_offsets, SECOND_SPACING, pairs_two_ref)
        if one is not None:
            keep_hidden(s * GROUP, first_offsets, one)
        if two is not None:
            keep_score((s - 2) * GROUP, second_offsets, two)
    score = score_ref[...]
    turned = score.T
    first, second = score[:, :size], score[:, size:]
    turned_first, turned_second = turned[:size], turned[size:]
    alone = diagonal == 1
    kept_ref[...] = 0.5 * (first + jnp.where(alone, turned_first, turned_second))
    sent_ref[...] = 0.5 * (second + jnp.where(alone, turned_second, turned_first))


def block_scores(every, dist_table, first_kernel, second_kernel, head, size, table):
    map_bins = every.shape[0]
    channels = dist_table.shape[1]
    wide = 2 * (size + 2 * SECOND_SPACING)
    vmem = pl.BlockSpec(memory_space=pltpu.VMEM)
    block = jax.ShapeDtypeStruct((size, size), jnp.float32)
    return pl.pallas_call(
        functools.partial(map_kernel, map_bins, size, table),
        out_shape=(block, block),
        in_specs=[vmem] * 5,
        out_specs=(vmem, vmem),
        scratch_shapes=[
            pltpu.VMEM((map_bins + 3 * PAD, channels), jnp.float32),
            pltpu.VMEM((map_bins + 3 * PAD, channels), jnp.float32),
            pltpu.VMEM((size + 2 * MARGIN, wide, 3 * channels), jnp.bfloat16),
            pltpu.VMEM((size + 2 * SECOND_SPACING, 2 * size, 3 * channels), jnp.bfloat16),
            pltpu.VMEM((12 * channels, 2 * channels), jnp.bfloat16),
            pltpu.VMEM((12 * channels, 2 * channels), jnp.bfloat16),
            pltpu.VMEM((size, 2 * size), jnp.float32),
        ],
        compiler_params=pltpu.CompilerParams(vmem_limit_bytes=40 * 1024 * 1024),
    )(
        every,
        dist_table,
        first_kernel.reshape(9 * channels, channels),
        second_kernel.reshape(9 * channels, channels),
        head,
    )


def on_device(
    embedding,
    bases_table,
    edit_pos,
    edit_tok,
    w_row,
    w_col,
    dist_gain,
    first_kernel,
    second_kernel,
    head_weight,
):
    n_rows, n_cols = lax.axis_size("row"), lax.axis_size("col")
    devices = n_rows * n_cols
    map_bins = embedding.shape[0] * devices // POOL
    table, target = plan(n_rows, n_cols)
    size = map_bins // max(n_rows, n_cols)
    copies, dist_table, head = projected(
        embedding, bases_table, edit_pos, edit_tok, w_row, w_col, dist_gain, head_weight, map_bins, devices
    )
    got = lax.all_to_all(copies, ("row", "col"), 0, 0)
    every = got.reshape(map_bins, got.shape[2])
    kept, sent = block_scores(every, dist_table, first_kernel, second_kernel, head, size, table)
    received = lax.ppermute(sent, ("row", "col"), [(device, target[device]) for device in range(devices)])
    place = lookup(table)[5]
    axis = 1 if n_rows > n_cols else 0
    return jnp.where(
        place == 0,
        jnp.concatenate([kept, received], axis=axis),
        jnp.concatenate([received, kept], axis=axis),
    )


def solution(mesh):
    placed = (P(("row", "col"), None), P(), P("cand"), P("cand"), P(), P(), P(), P(), P(), P())
    return jax.shard_map(
        on_device, mesh=mesh, in_specs=placed, out_specs=P(("cand", "row"), "col"), check_vma=False
    )
```

```python
import functools
import math

import jax
import jax.numpy as jnp
from jax import lax
from jax.experimental import pallas as pl
from jax.experimental.pallas import tpu as pltpu
from jax.sharding import PartitionSpec as P

POOL = 4
FIRST_SPACING = 2
SECOND_SPACING = 4
BASES = 4
MARGIN = FIRST_SPACING + SECOND_SPACING
PAD = 8
GROUP = 8
PAIRS_PER_DOT = 1
OUTSIDE = -1e30


def plan(n_rows, n_cols):
    wide = n_rows > n_cols
    blocks = max(n_rows, n_cols)
    assert blocks == 2 * min(n_rows, n_cols)

    def owner(i, j):
        return i * n_cols + j // 2 if wide else (i // 2) * n_cols + j

    held = {}
    for i in range(blocks):
        for j in range(blocks):
            held.setdefault(owner(i, j), []).append((i, j))

    def other(device, block):
        return next(b for b in held[device] if b != block)

    jobs, target = {}, {}

    def assign(device, kept, sent):
        place = held[device].index(kept)
        jobs[device] = (*kept, *sent, int(kept[0] == kept[1]), place)
        target[device] = owner(*sent)

    def walk(device, block):
        while device not in jobs:
            if block[0] == block[1]:
                return device, block
            sent = (block[1], block[0])
            assign(device, block, sent)
            device = owner(*sent)
            block = other(device, sent)
        return None, None

    for d in range(blocks):
        start = owner(d, d)
        if start not in jobs:
            end, last = walk(start, other(start, (d, d)))
            assign(end, last, (d, d))
    for device in sorted(held):
        if device not in jobs:
            walk(device, held[device][0])
    return [jobs[device] for device in sorted(jobs)], target


def relu(x):
    return jnp.maximum(x, 0.0)


def lookup(table):
    n_cols = lax.axis_size("col")
    here = lax.axis_index("row") * n_cols + lax.axis_index("col")
    found = []
    for values in zip(*table):
        value = jnp.int32(values[0])
        for device in range(1, len(values)):
            value = jnp.where(here == device, jnp.int32(values[device]), value)
        found.append(value)
    return found


def project_kernel(
    map_bins, embedding_hbm, bases_hbm, pos_hbm, tok_hbm, w_row_hbm, w_col_hbm, gain_hbm, head_hbm,
    copies_ref, dist_ref, head_ref,
    embedding_ref, bases_ref, pos_ref, tok_ref, w_row_ref, w_col_ref, gain_ref, weight_ref, arrived,
):
    moves = [
        pltpu.make_async_copy(source, target, arrived.at[n])
        for n, (source, target) in enumerate(
            (
                (embedding_hbm, embedding_ref),
                (w_row_hbm, w_row_ref),
                (w_col_hbm, w_col_ref),
                (pos_hbm, pos_ref),
                (tok_hbm, tok_ref),
                (bases_hbm, bases_ref),
                (gain_hbm, gain_ref),
                (head_hbm, weight_ref),
            )
        )
    ]
    for move in moves:
        move.start()
    got_embedding, got_w_row, got_w_col, *small = moves
    shard_bins = embedding_ref.shape[0]
    copies, pooled_bins, _ = copies_ref.shape
    channels = gain_ref.shape[1]
    edits = pos_ref.shape[1]
    span = dist_ref.shape[0]
    apart = jnp.abs(lax.broadcasted_iota(jnp.int32, (span, channels), 0) - span // 2)
    feature = jnp.log1p(apart.astype(jnp.float32)) * (1.0 / math.log(map_bins))
    first_bin = (lax.axis_index("row") * lax.axis_size("col") + lax.axis_index("col")) * shard_bins
    bins = first_bin + lax.broadcasted_iota(jnp.int32, (pooled_bins, edits), 0) * POOL
    back = lax.broadcasted_iota(jnp.int32, (pooled_bins, shard_bins), 1) - POOL * (
        lax.broadcasted_iota(jnp.int32, (pooled_bins, shard_bins), 0)
    )
    take = ((back >= 0) & (back < POOL)).astype(jnp.float32).astype(jnp.bfloat16)
    for move in small:
        move.wait()
    dist_ref[...] = gain_ref[...] * feature
    weight = jnp.concatenate([weight_ref[...].astype(jnp.float32)] * 2, axis=1)
    line = lax.broadcasted_iota(jnp.int32, head_ref.shape, 0)
    half = lax.broadcasted_iota(jnp.int32, head_ref.shape, 1) >= channels
    head_ref[...] = jnp.where(line == half.astype(jnp.int32), weight, 0.0).astype(jnp.bfloat16)
    ahead = pos_ref[...] - bins
    in_bin = ((ahead >= 0) & (ahead < POOL)).astype(jnp.float32)
    edited = None
    for base in range(BASES):
        is_base = (tok_ref[...] == base).astype(jnp.float32)
        count = jnp.sum(in_bin * is_base, axis=1, keepdims=True)
        term = count * bases_ref[base : base + 1].astype(jnp.float32)
        edited = term if edited is None else edited + term
    got_embedding.wait()
    summed = edited + jnp.dot(take, embedding_ref[...], preferred_element_type=jnp.float32)
    pooled = (summed * (1.0 / POOL)).astype(jnp.bfloat16)
    sides = []
    for move, ref in ((got_w_row, w_row_ref), (got_w_col, w_col_ref)):
        move.wait()
        sides.append(jnp.dot(pooled, ref[...], preferred_element_type=jnp.float32).astype(jnp.bfloat16))
    both = jnp.concatenate(sides, axis=1)
    for k in range(copies):
        copies_ref[k] = both


def projected(embedding, bases_table, edit_pos, edit_tok, w_row, w_col, dist_gain, head_weight, map_bins, copies):
    vmem = pl.BlockSpec(memory_space=pltpu.VMEM)
    operands = (
        embedding,
        bases_table,
        edit_pos[None],
        edit_tok[None],
        w_row,
        w_col,
        dist_gain[None],
        head_weight[None],
    )
    channels = w_row.shape[1]
    return pl.pallas_call(
        functools.partial(project_kernel, map_bins),
        out_shape=(
            jax.ShapeDtypeStruct((copies, embedding.shape[0] // POOL, 2 * channels), jnp.bfloat16),
            jax.ShapeDtypeStruct((2 * map_bins + 4 * PAD, channels), jnp.float32),
            jax.ShapeDtypeStruct((16, 2 * channels), jnp.bfloat16),
        ),
        in_specs=[pl.BlockSpec(memory_space=pltpu.HBM)] * 8,
        out_specs=(vmem, vmem, vmem),
        scratch_shapes=[pltpu.VMEM(x.shape, x.dtype) for x in operands] + [pltpu.SemaphoreType.DMA((8,))],
        compiler_params=pltpu.CompilerParams(vmem_limit_bytes=16 * 1024 * 1024),
    )(*(pltpu.with_memory_space_constraint(x, pltpu.HBM) for x in operands))


def map_kernel(
    map_bins, size, table, proj_ref, dist_table_ref, first_ref, second_ref, head_ref,
    kept_ref, sent_ref, row_ref, col_ref, pair_ref, hidden_ref, pairs_one_ref, pairs_two_ref, score_ref, filled,
):
    channels = dist_table_ref.shape[1]
    block_wide = size + 2 * SECOND_SPACING
    wide = 2 * block_wide
    spread = block_wide + PAD
    breadth = 2 * size
    pair_rows = size + 2 * MARGIN
    hidden_rows = size + 2 * SECOND_SPACING
    depth = 3 * channels
    edge = SECOND_SPACING
    row_a, col_a, row_b, col_b, diagonal, _ = lookup(table)
    blocks = [
        (pl.multiple_of(row_a * size, size), pl.multiple_of(col_a * size, size)),
        (pl.multiple_of(row_b * size, size), pl.multiple_of(col_b * size, size)),
    ]
    outside = jnp.full((2 * PAD, channels), OUTSIDE, jnp.float32)
    for part, ref in enumerate((row_ref, col_ref)):
        ref[:PAD] = outside[:PAD]
        ref[PAD + map_bins :] = outside
        ref[PAD : PAD + map_bins] = proj_ref[:, part * channels : (part + 1) * channels].astype(
            jnp.float32
        )
    fills = []
    for ref, given in ((pairs_one_ref, first_ref), (pairs_two_ref, second_ref)):
        ref[3 * depth :, :channels] = jnp.zeros((depth, channels), jnp.bfloat16)
        ref[:depth, channels:] = jnp.zeros((depth, channels), jnp.bfloat16)
        for half in range(2):
            place = ref.at[pl.ds(half * depth, 3 * depth), pl.ds(half * channels, channels)]
            fills.append(pltpu.make_async_copy(given, place, filled.at[len(fills)]))
            fills[-1].start()
    zero_apart = dist_table_ref.shape[0] // 2
    at_edge = lax.broadcasted_iota(jnp.int32, (PAD, channels), 0)
    last_start = map_bins - size
    left = [jnp.where((at_edge >= edge) | (col > 0), 1.0, 0.0) for _, col in blocks]
    right = [jnp.where((at_edge < PAD - edge) | (col < last_start), 1.0, 0.0) for _, col in blocks]
    above = [jnp.where(row > 0, 1.0, 0.0) for row, _ in blocks]
    below = [jnp.where(row < last_start, 1.0, 0.0) for row, _ in blocks]

    def build(p):
        values = []
        for row, col in blocks:
            row_part = row_ref[pl.ds(row + (PAD - MARGIN + p), 1)]
            apart = dist_table_ref[pl.ds(col - row + (zero_apart - p), spread)]
            values.append(relu(col_ref[pl.ds(col + (PAD - MARGIN), spread)] + apart + row_part))
        taps = []
        for b in range(3):
            moved = [
                (pltpu.roll(x, spread - b * FIRST_SPACING, 0) if b else x)[:block_wide] for x in values
            ]
            taps.append(jnp.concatenate(moved, axis=0).astype(jnp.bfloat16))
        pair_ref[p] = jnp.concatenate(taps, axis=1)

    def paired(ref, start, offsets, spacing, weight):
        parts = []
        for n in range(0, len(offsets), PAIRS_PER_DOT):
            rows = [
                jnp.concatenate([ref[start + base + k * spacing] for k in range(4)], axis=1)
                for base in offsets[n : n + PAIRS_PER_DOT]
            ]
            lhs = rows[0] if len(rows) == 1 else jnp.concatenate(rows, axis=0)
            out = jnp.dot(lhs, weight[...], preferred_element_type=jnp.float32)
            height = out.shape[0] // len(rows)
            parts += [out[k * height : (k + 1) * height] for k in range(len(rows))]
        return parts

    def keep_hidden(start, offsets, out):
        for n, base in enumerate(offsets):
            for half in range(2):
                a = start + base + half * FIRST_SPACING
                conv = out[n][:, half * channels : (half + 1) * channels]
                own = pair_ref[a + FIRST_SPACING, :, channels : 2 * channels].astype(jnp.float32)
                value = own + relu(conv)
                for rows, flags in ((a < edge, above), (a >= hidden_rows - edge, below)):
                    if rows:
                        value = jnp.concatenate(
                            [value[:block_wide] * flags[0], value[block_wide:] * flags[1]], axis=0
                        )
                ahead = pltpu.roll(value, wide - edge, 0)
                before, middle, after = [], [], []
                for b in range(2):
                    at = b * block_wide
                    before += [value[at : at + PAD] * left[b], value[at + PAD : at + size]]
                    middle += [ahead[at : at + size]]
                    after += [value[at + PAD : at + size], value[at + size : at + size + PAD] * right[b]]
                hidden_ref[a] = jnp.concatenate(
                    [jnp.concatenate(x, axis=0).astype(jnp.bfloat16) for x in (before, middle, after)], axis=1
                )

    def keep_score(start, offsets, out):
        last = []
        for n, base in enumerate(offsets):
            halves = []
            for half in range(2):
                o = start + base + half * edge
                conv = out[n][:, half * channels : (half + 1) * channels]
                own = hidden_ref[o + edge, :, channels : 2 * channels].astype(jnp.float32)
                halves.append((own + relu(conv)).astype(jnp.bfloat16))
            last.append(jnp.concatenate(halves, axis=1))
        got = lax.dot_general(
            head_ref[...],
            jnp.concatenate(last, axis=0),
            (((1,), (1,)), ((), ())),
            preferred_element_type=jnp.float32,
        )
        count = len(offsets)
        lines = [got[half : half + 1, n * breadth : (n + 1) * breadth] for half in range(2) for n in range(count)]
        score_ref[start : start + 8] = jnp.concatenate(lines, axis=0)

    first_offsets, second_offsets = (0, 1, 4, 5), (0, 1, 2, 3)
    first_groups, second_groups = hidden_rows // GROUP, size // GROUP
    for p in range(2 * GROUP):
        build(p)
    for fill in fills:
        fill.wait()
    for s in range(first_groups + 1):
        one = two = None
        if s < first_groups:
            one = paired(pair_ref, s * GROUP, first_offsets, FIRST_SPACING, pairs_one_ref)
        for p in range((s + 2) * GROUP, min((s + 3) * GROUP, pair_rows)):
            build(p)
        if 0 <= s - 2 < second_groups:
            two = paired(hidden_ref, (s - 2) * GROUP, second_offsets, SECOND_SPACING, pairs_two_ref)
        if one is not None:
            keep_hidden(s * GROUP, first_offsets, one)
        if two is not None:
            keep_score((s - 2) * GROUP, second_offsets, two)
    score = score_ref[...]
    turned = score.T
    first, second = score[:, :size], score[:, size:]
    turned_first, turned_second = turned[:size], turned[size:]
    alone = diagonal == 1
    kept_ref[...] = 0.5 * (first + jnp.where(alone, turned_first, turned_second))
    sent_ref[...] = 0.5 * (second + jnp.where(alone, turned_second, turned_first))


def block_scores(every, dist_table, first_kernel, second_kernel, head, size, table):
    map_bins = every.shape[0]
    channels = dist_table.shape[1]
    wide = 2 * (size + 2 * SECOND_SPACING)
    vmem = pl.BlockSpec(memory_space=pltpu.VMEM)
    block = jax.ShapeDtypeStruct((size, size), jnp.float32)
    return pl.pallas_call(
        functools.partial(map_kernel, map_bins, size, table),
        out_shape=(block, block),
        in_specs=[vmem] * 5,
        out_specs=(vmem, vmem),
        scratch_shapes=[
            pltpu.VMEM((map_bins + 3 * PAD, channels), jnp.float32),
            pltpu.VMEM((map_bins + 3 * PAD, channels), jnp.float32),
            pltpu.VMEM((size + 2 * MARGIN, wide, 3 * channels), jnp.bfloat16),
            pltpu.VMEM((size + 2 * SECOND_SPACING, 2 * size, 3 * channels), jnp.bfloat16),
            pltpu.VMEM((12 * channels, 2 * channels), jnp.bfloat16),
            pltpu.VMEM((12 * channels, 2 * channels), jnp.bfloat16),
            pltpu.VMEM((size, 2 * size), jnp.float32),
            pltpu.SemaphoreType.DMA((4,)),
        ],
        compiler_params=pltpu.CompilerParams(vmem_limit_bytes=40 * 1024 * 1024),
    )(
        every,
        dist_table,
        first_kernel.reshape(9 * channels, channels),
        second_kernel.reshape(9 * channels, channels),
        head,
    )


def on_device(
    embedding,
    bases_table,
    edit_pos,
    edit_tok,
    w_row,
    w_col,
    dist_gain,
    first_kernel,
    second_kernel,
    head_weight,
):
    n_rows, n_cols = lax.axis_size("row"), lax.axis_size("col")
    devices = n_rows * n_cols
    map_bins = embedding.shape[0] * devices // POOL
    table, target = plan(n_rows, n_cols)
    size = map_bins // max(n_rows, n_cols)
    copies, dist_table, head = projected(
        embedding, bases_table, edit_pos, edit_tok, w_row, w_col, dist_gain, head_weight, map_bins, devices
    )
    got = lax.all_to_all(copies, ("row", "col"), 0, 0)
    every = got.reshape(map_bins, got.shape[2])
    kept, sent = block_scores(every, dist_table, first_kernel, second_kernel, head, size, table)
    received = lax.ppermute(sent, ("row", "col"), [(device, target[device]) for device in range(devices)])
    place = lookup(table)[5]
    axis = 1 if n_rows > n_cols else 0
    return jnp.where(
        place == 0,
        jnp.concatenate([kept, received], axis=axis),
        jnp.concatenate([received, kept], axis=axis),
    )


def solution(mesh):
    placed = (P(("row", "col"), None), P(), P("cand"), P("cand"), P(), P(), P(), P(), P(), P())
    return jax.shard_map(
        on_device, mesh=mesh, in_specs=placed, out_specs=P(("cand", "row"), "col"), check_vma=False
    )
```

```python
import functools
import math

import jax
import jax.numpy as jnp
from jax import lax
from jax.experimental import pallas as pl
from jax.experimental.pallas import tpu as pltpu
from jax.sharding import PartitionSpec as P

POOL = 4
FIRST_SPACING = 2
SECOND_SPACING = 4
BASES = 4
MARGIN = FIRST_SPACING + SECOND_SPACING
PAD = 8
GROUP = 8
OUTSIDE = -1e30


def plan(n_rows, n_cols):
    wide = n_rows > n_cols
    blocks = max(n_rows, n_cols)
    assert blocks == 2 * min(n_rows, n_cols)

    def owner(i, j):
        return i * n_cols + j // 2 if wide else (i // 2) * n_cols + j

    held = {}
    for i in range(blocks):
        for j in range(blocks):
            held.setdefault(owner(i, j), []).append((i, j))

    def other(device, block):
        return next(b for b in held[device] if b != block)

    jobs, target = {}, {}

    def assign(device, kept, sent):
        place = held[device].index(kept)
        jobs[device] = (*kept, *sent, int(kept[0] == kept[1]), place)
        target[device] = owner(*sent)

    def walk(device, block):
        while device not in jobs:
            if block[0] == block[1]:
                return device, block
            sent = (block[1], block[0])
            assign(device, block, sent)
            device = owner(*sent)
            block = other(device, sent)
        return None, None

    for d in range(blocks):
        start = owner(d, d)
        if start not in jobs:
            end, last = walk(start, other(start, (d, d)))
            assign(end, last, (d, d))
    for device in sorted(held):
        if device not in jobs:
            walk(device, held[device][0])
    return [jobs[device] for device in sorted(jobs)], target


def relu(x):
    return jnp.maximum(x, 0.0)


def lookup(table):
    n_cols = lax.axis_size("col")
    here = lax.axis_index("row") * n_cols + lax.axis_index("col")
    found = []
    for values in zip(*table):
        value = jnp.int32(values[0])
        for device in range(1, len(values)):
            value = jnp.where(here == device, jnp.int32(values[device]), value)
        found.append(value)
    return found


def project_kernel(
    map_bins, embedding_hbm, bases_hbm, pos_hbm, tok_hbm, w_row_hbm, w_col_hbm, gain_hbm, head_hbm,
    copies_ref, dist_ref, head_ref,
    embedding_ref, bases_ref, pos_ref, tok_ref, w_row_ref, w_col_ref, gain_ref, weight_ref, arrived,
):
    moves = [
        pltpu.make_async_copy(source, target, arrived.at[n])
        for n, (source, target) in enumerate(
            (
                (embedding_hbm, embedding_ref),
                (w_row_hbm, w_row_ref),
                (w_col_hbm, w_col_ref),
                (pos_hbm, pos_ref),
                (tok_hbm, tok_ref),
                (bases_hbm, bases_ref),
                (gain_hbm, gain_ref),
                (head_hbm, weight_ref),
            )
        )
    ]
    for move in moves:
        move.start()
    got_embedding, got_w_row, got_w_col, *small = moves
    shard_bins = embedding_ref.shape[0]
    copies, pooled_bins, _ = copies_ref.shape
    channels = gain_ref.shape[1]
    edits = pos_ref.shape[1]
    span = dist_ref.shape[0]
    apart = jnp.abs(lax.broadcasted_iota(jnp.int32, (span, channels), 0) - span // 2)
    feature = jnp.log1p(apart.astype(jnp.float32)) * (1.0 / math.log(map_bins))
    first_bin = (lax.axis_index("row") * lax.axis_size("col") + lax.axis_index("col")) * shard_bins
    bins = first_bin + lax.broadcasted_iota(jnp.int32, (pooled_bins, edits), 0) * POOL
    back = lax.broadcasted_iota(jnp.int32, (pooled_bins, shard_bins), 1) - POOL * (
        lax.broadcasted_iota(jnp.int32, (pooled_bins, shard_bins), 0)
    )
    take = ((back >= 0) & (back < POOL)).astype(jnp.float32).astype(jnp.bfloat16)
    for move in small:
        move.wait()
    dist_ref[...] = gain_ref[...] * feature
    weight = jnp.concatenate([weight_ref[...].astype(jnp.float32)] * 2, axis=1)
    line = lax.broadcasted_iota(jnp.int32, head_ref.shape, 0)
    half = lax.broadcasted_iota(jnp.int32, head_ref.shape, 1) >= channels
    head_ref[...] = jnp.where(line == half.astype(jnp.int32), weight, 0.0).astype(jnp.bfloat16)
    ahead = pos_ref[...] - bins
    in_bin = ((ahead >= 0) & (ahead < POOL)).astype(jnp.float32)
    edited = None
    for base in range(BASES):
        is_base = (tok_ref[...] == base).astype(jnp.float32)
        count = jnp.sum(in_bin * is_base, axis=1, keepdims=True)
        term = count * bases_ref[base : base + 1].astype(jnp.float32)
        edited = term if edited is None else edited + term
    got_embedding.wait()
    summed = edited + jnp.dot(take, embedding_ref[...], preferred_element_type=jnp.float32)
    pooled = (summed * (1.0 / POOL)).astype(jnp.bfloat16)
    sides = []
    for move, ref in ((got_w_row, w_row_ref), (got_w_col, w_col_ref)):
        move.wait()
        sides.append(jnp.dot(pooled, ref[...], preferred_element_type=jnp.float32).astype(jnp.bfloat16))
    both = jnp.concatenate(sides, axis=1)
    for k in range(copies):
        copies_ref[k] = both


def projected(embedding, bases_table, edit_pos, edit_tok, w_row, w_col, dist_gain, head_weight, map_bins, copies):
    vmem = pl.BlockSpec(memory_space=pltpu.VMEM)
    operands = (
        embedding,
        bases_table,
        edit_pos[None],
        edit_tok[None],
        w_row,
        w_col,
        dist_gain[None],
        head_weight[None],
    )
    channels = w_row.shape[1]
    return pl.pallas_call(
        functools.partial(project_kernel, map_bins),
        out_shape=(
            jax.ShapeDtypeStruct((copies, embedding.shape[0] // POOL, 2 * channels), jnp.bfloat16),
            jax.ShapeDtypeStruct((2 * map_bins + 4 * PAD, channels), jnp.float32),
            jax.ShapeDtypeStruct((16, 2 * channels), jnp.bfloat16),
        ),
        in_specs=[pl.BlockSpec(memory_space=pltpu.HBM)] * 8,
        out_specs=(vmem, vmem, vmem),
        scratch_shapes=[pltpu.VMEM(x.shape, x.dtype) for x in operands] + [pltpu.SemaphoreType.DMA((8,))],
        compiler_params=pltpu.CompilerParams(vmem_limit_bytes=16 * 1024 * 1024),
    )(*(pltpu.with_memory_space_constraint(x, pltpu.HBM) for x in operands))


def map_kernel(
    map_bins, size, table, proj_ref, dist_table_ref, weights_ref, head_ref,
    kept_ref, sent_ref, row_ref, col_ref, pair_ref, pair_step_ref, hidden_ref, hidden_step_ref, score_ref,
):
    channels = dist_table_ref.shape[1]
    block_wide = size + 2 * SECOND_SPACING
    wide = 2 * block_wide
    spread = block_wide + PAD
    breadth = 2 * size
    pair_rows = size + 2 * MARGIN
    hidden_rows = size + 2 * SECOND_SPACING
    edge = SECOND_SPACING
    row_a, col_a, row_b, col_b, diagonal, _ = lookup(table)
    blocks = [
        (pl.multiple_of(row_a * size, size), pl.multiple_of(col_a * size, size)),
        (pl.multiple_of(row_b * size, size), pl.multiple_of(col_b * size, size)),
    ]
    outside = jnp.full((2 * PAD, channels), OUTSIDE, jnp.float32)
    for part, ref in enumerate((row_ref, col_ref)):
        ref[:PAD] = outside[:PAD]
        ref[PAD + map_bins :] = outside
        ref[PAD : PAD + map_bins] = proj_ref[:, part * channels : (part + 1) * channels].astype(
            jnp.float32
        )
    zero_apart = dist_table_ref.shape[0] // 2
    at_edge = lax.broadcasted_iota(jnp.int32, (PAD, channels), 0)
    last_start = map_bins - size
    left = [jnp.where((at_edge >= edge) | (col > 0), 1.0, 0.0) for _, col in blocks]
    right = [jnp.where((at_edge < PAD - edge) | (col < last_start), 1.0, 0.0) for _, col in blocks]
    above = [jnp.where(row > 0, 1.0, 0.0) for row, _ in blocks]
    below = [jnp.where(row < last_start, 1.0, 0.0) for row, _ in blocks]

    def build(p):
        values = []
        for row, col in blocks:
            row_part = row_ref[pl.ds(row + (PAD - MARGIN + p), 1)]
            apart = dist_table_ref[pl.ds(col - row + (zero_apart - p), spread)]
            values.append(relu(col_ref[pl.ds(col + (PAD - MARGIN), spread)] + apart + row_part))
        taps = []
        for b in range(3):
            moved = [
                (pltpu.roll(x, spread - b * FIRST_SPACING, 0) if b else x)[:block_wide] for x in values
            ]
            taps.append(jnp.concatenate(moved, axis=0).astype(jnp.bfloat16))
        pair_ref[p] = jnp.concatenate(taps, axis=1)
        if p >= 2 * FIRST_SPACING:
            before = p - 2 * FIRST_SPACING
            pair_step_ref[before] = pair_ref[before] - pair_ref[p]

    def four_rows(ref, step_ref, start, offsets, spacing, weights):
        def pairs_of(source, k):
            rows = [
                jnp.concatenate(
                    [source[start + base + k * spacing], source[start + base + (k + 1) * spacing]], axis=1
                )
                for base in offsets
            ]
            return jnp.concatenate(rows, axis=0)

        def times(lhs, which):
            return jnp.dot(lhs, weights_ref[weights, which], preferred_element_type=jnp.float32)

        shared = times(pairs_of(ref, 2), 1)
        low = times(pairs_of(step_ref, 0), 0)
        high = times(pairs_of(step_ref, 2), 2)
        tall = shared.shape[0] // len(offsets)
        found = []
        for n in range(len(offsets)):
            rows = []
            for k in range(4):
                down = slice(n * tall, (n + 1) * tall)
                across = slice((k % 2) * channels, (k % 2 + 1) * channels)
                rows.append((low if k < 2 else high)[down, across] + shared[down, across])
            found.append(rows)
        return found

    def keep_hidden(start, offsets, out):
        for n, base in enumerate(offsets):
            for k in range(4):
                a = start + base + k * FIRST_SPACING
                own = pair_ref[a + FIRST_SPACING, :, channels : 2 * channels].astype(jnp.float32)
                value = own + relu(out[n][k])
                for rows, flags in ((a < edge, above), (a >= hidden_rows - edge, below)):
                    if rows:
                        value = jnp.concatenate(
                            [value[:block_wide] * flags[0], value[block_wide:] * flags[1]], axis=0
                        )
                ahead = pltpu.roll(value, wide - edge, 0)
                before, middle, after = [], [], []
                for b in range(2):
                    at = b * block_wide
                    before += [value[at : at + PAD] * left[b], value[at + PAD : at + size]]
                    middle += [ahead[at : at + size]]
                    after += [value[at + PAD : at + size], value[at + size : at + size + PAD] * right[b]]
                hidden_ref[a] = jnp.concatenate(
                    [jnp.concatenate(x, axis=0).astype(jnp.bfloat16) for x in (before, middle, after)], axis=1
                )
        for a in range(start, start + GROUP):
            if a >= 2 * edge:
                hidden_step_ref[a - 2 * edge] = hidden_ref[a - 2 * edge] - hidden_ref[a]

    def keep_score(start, offsets, out):
        last = []
        for n, base in enumerate(offsets):
            rows = []
            for k in range(4):
                o = start + base + k * edge
                own = hidden_ref[o + edge, :, channels : 2 * channels].astype(jnp.float32)
                rows.append((own + relu(out[n][k])).astype(jnp.bfloat16))
            last += [jnp.concatenate(rows[:2], axis=1), jnp.concatenate(rows[2:], axis=1)]
        got = lax.dot_general(
            head_ref[...],
            jnp.concatenate(last, axis=0),
            (((1,), (1,)), ((), ())),
            preferred_element_type=jnp.float32,
        )
        lines = []
        for k in range(4):
            for n in range(len(offsets)):
                at = (2 * n + k // 2) * breadth
                lines.append(got[k % 2 : k % 2 + 1, at : at + breadth])
        score_ref[start : start + 2 * GROUP] = jnp.concatenate(lines, axis=0)

    first_offsets, second_offsets = (0, 1), (0, 1, 2, 3)
    first_groups = hidden_rows // GROUP
    for p in range(2 * GROUP):
        build(p)
    for s in range(first_groups + 1):
        one = two = None
        if s < first_groups:
            one = four_rows(pair_ref, pair_step_ref, s * GROUP, first_offsets, FIRST_SPACING, 0)
        for p in range((s + 2) * GROUP, min((s + 3) * GROUP, pair_rows)):
            build(p)
        if s >= 3 and s % 2 == 1:
            two = four_rows(hidden_ref, hidden_step_ref, (s - 3) * GROUP, second_offsets, edge, 1)
        if one is not None:
            keep_hidden(s * GROUP, first_offsets, one)
        if two is not None:
            keep_score((s - 3) * GROUP, second_offsets, two)
    score = score_ref[...]
    turned = score.T
    first, second = score[:, :size], score[:, size:]
    turned_first, turned_second = turned[:size], turned[size:]
    alone = diagonal == 1
    kept_ref[...] = 0.5 * (first + jnp.where(alone, turned_first, turned_second))
    sent_ref[...] = 0.5 * (second + jnp.where(alone, turned_second, turned_first))


def weights_kernel(first_ref, second_ref, weights_ref):
    depth = weights_ref.shape[2] // 2
    channels = weights_ref.shape[3] // 2
    for n, ref in enumerate((first_ref, second_ref)):
        g0, g1, g2 = (ref[a * depth : (a + 1) * depth] for a in range(3))
        both = (g0.astype(jnp.float32) + g2.astype(jnp.float32)).astype(jnp.bfloat16)
        none = jnp.zeros_like(g0)
        for which, quarters in enumerate(
            ((g0, none, g1, g0), (both, g1, g1, both), (-g2, -g1, none, -g2))
        ):
            for q, quarter in enumerate(quarters):
                down, across = (q // 2) * depth, (q % 2) * channels
                weights_ref[n, which, down : down + depth, across : across + channels] = quarter


def combined_weights(first_kernel, second_kernel):
    channels = first_kernel.shape[3]
    vmem = pl.BlockSpec(memory_space=pltpu.VMEM)
    return pl.pallas_call(
        weights_kernel,
        out_shape=jax.ShapeDtypeStruct((2, 3, 6 * channels, 2 * channels), jnp.bfloat16),
        in_specs=[vmem] * 2,
        out_specs=vmem,
        compiler_params=pltpu.CompilerParams(vmem_limit_bytes=8 * 1024 * 1024),
    )(first_kernel.reshape(9 * channels, channels), second_kernel.reshape(9 * channels, channels))


def block_scores(every, dist_table, weights, head, size, table):
    map_bins = every.shape[0]
    channels = dist_table.shape[1]
    wide = 2 * (size + 2 * SECOND_SPACING)
    vmem = pl.BlockSpec(memory_space=pltpu.VMEM)
    block = jax.ShapeDtypeStruct((size, size), jnp.float32)
    return pl.pallas_call(
        functools.partial(map_kernel, map_bins, size, table),
        out_shape=(block, block),
        in_specs=[vmem] * 4,
        out_specs=(vmem, vmem),
        scratch_shapes=[
            pltpu.VMEM((map_bins + 3 * PAD, channels), jnp.float32),
            pltpu.VMEM((map_bins + 3 * PAD, channels), jnp.float32),
            pltpu.VMEM((size + 2 * MARGIN, wide, 3 * channels), jnp.bfloat16),
            pltpu.VMEM((size + 2 * SECOND_SPACING, wide, 3 * channels), jnp.bfloat16),
            pltpu.VMEM((size + 2 * SECOND_SPACING, 2 * size, 3 * channels), jnp.bfloat16),
            pltpu.VMEM((size, 2 * size, 3 * channels), jnp.bfloat16),
            pltpu.VMEM((size, 2 * size), jnp.float32),
        ],
        compiler_params=pltpu.CompilerParams(vmem_limit_bytes=40 * 1024 * 1024),
    )(every, dist_table, weights, head)


def on_device(
    embedding,
    bases_table,
    edit_pos,
    edit_tok,
    w_row,
    w_col,
    dist_gain,
    first_kernel,
    second_kernel,
    head_weight,
):
    n_rows, n_cols = lax.axis_size("row"), lax.axis_size("col")
    devices = n_rows * n_cols
    map_bins = embedding.shape[0] * devices // POOL
    table, target = plan(n_rows, n_cols)
    size = map_bins // max(n_rows, n_cols)
    copies, dist_table, head = projected(
        embedding, bases_table, edit_pos, edit_tok, w_row, w_col, dist_gain, head_weight, map_bins, devices
    )
    got = lax.all_to_all(copies, ("row", "col"), 0, 0)
    every = got.reshape(map_bins, got.shape[2])
    weights = combined_weights(first_kernel, second_kernel)
    kept, sent = block_scores(every, dist_table, weights, head, size, table)
    received = lax.ppermute(sent, ("row", "col"), [(device, target[device]) for device in range(devices)])
    place = lookup(table)[5]
    axis = 1 if n_rows > n_cols else 0
    return jnp.where(
        place == 0,
        jnp.concatenate([kept, received], axis=axis),
        jnp.concatenate([received, kept], axis=axis),
    )


def solution(mesh):
    placed = (P(("row", "col"), None), P(), P("cand"), P("cand"), P(), P(), P(), P(), P(), P())
    return jax.shard_map(
        on_device, mesh=mesh, in_specs=placed, out_specs=P(("cand", "row"), "col"), check_vma=False
    )
```

```python
import functools
import math

import jax
import jax.numpy as jnp
from jax import lax
from jax.experimental import pallas as pl
from jax.experimental.pallas import tpu as pltpu
from jax.sharding import PartitionSpec as P

POOL = 4
FIRST_SPACING = 2
SECOND_SPACING = 4
BASES = 4
MARGIN = FIRST_SPACING + SECOND_SPACING
PAD = 8
GROUP = 8
OUTSIDE = -1e30


def plan(n_rows, n_cols):
    wide = n_rows > n_cols
    blocks = max(n_rows, n_cols)
    assert blocks == 2 * min(n_rows, n_cols)

    def owner(i, j):
        return i * n_cols + j // 2 if wide else (i // 2) * n_cols + j

    held = {}
    for i in range(blocks):
        for j in range(blocks):
            held.setdefault(owner(i, j), []).append((i, j))

    def other(device, block):
        return next(b for b in held[device] if b != block)

    jobs, target = {}, {}

    def assign(device, kept, sent):
        place = held[device].index(kept)
        jobs[device] = (*kept, *sent, int(kept[0] == kept[1]), place)
        target[device] = owner(*sent)

    def walk(device, block):
        while device not in jobs:
            if block[0] == block[1]:
                return device, block
            sent = (block[1], block[0])
            assign(device, block, sent)
            device = owner(*sent)
            block = other(device, sent)
        return None, None

    for d in range(blocks):
        start = owner(d, d)
        if start not in jobs:
            end, last = walk(start, other(start, (d, d)))
            assign(end, last, (d, d))
    for device in sorted(held):
        if device not in jobs:
            walk(device, held[device][0])
    return [jobs[device] for device in sorted(jobs)], target


def tiles_of(size):
    return (size + 2 * PAD) // 4


def relu(x):
    return jnp.maximum(x, 0.0)


def lookup(table):
    n_cols = lax.axis_size("col")
    here = lax.axis_index("row") * n_cols + lax.axis_index("col")
    found = []
    for values in zip(*table):
        value = jnp.int32(values[0])
        for device in range(1, len(values)):
            value = jnp.where(here == device, jnp.int32(values[device]), value)
        found.append(value)
    return found


def project_kernel(
    map_bins, size, table, embedding_hbm, bases_hbm, pos_hbm, tok_hbm, w_row_hbm, w_col_hbm, gain_hbm, head_hbm,
    copies_ref, dist_ref, head_ref,
    embedding_ref, bases_ref, pos_ref, tok_ref, w_row_ref, w_col_ref, gain_ref, weight_ref, arrived,
):
    moves = [
        pltpu.make_async_copy(source, target, arrived.at[n])
        for n, (source, target) in enumerate(
            (
                (embedding_hbm, embedding_ref),
                (w_row_hbm, w_row_ref),
                (w_col_hbm, w_col_ref),
                (pos_hbm, pos_ref),
                (tok_hbm, tok_ref),
                (bases_hbm, bases_ref),
                (gain_hbm, gain_ref),
                (head_hbm, weight_ref),
            )
        )
    ]
    for move in moves:
        move.start()
    got_embedding, got_w_row, got_w_col, *small = moves
    shard_bins = embedding_ref.shape[0]
    copies, pooled_bins, _ = copies_ref.shape
    channels = gain_ref.shape[1]
    edits = pos_ref.shape[1]
    row_a, col_a, row_b, col_b, _, _ = lookup(table)
    phases, count, _ = dist_ref.shape
    at = lax.broadcasted_iota(jnp.int32, (count, channels), 0)
    lane = at & 7
    start = jnp.where((lane & 2) == 0, (col_a - row_a) * size, (col_b - row_b) * size)
    start = start + 4 * (at >> 3) + 2 * (lane >> 2) + (lane & 1) - 2 - 4 * ((size + 2 * MARGIN) // 4 - 1)
    feature = [
        jnp.log1p(jnp.abs(start - phase).astype(jnp.float32)) * (1.0 / math.log(map_bins))
        for phase in range(phases)
    ]
    first_bin = (lax.axis_index("row") * lax.axis_size("col") + lax.axis_index("col")) * shard_bins
    bins = first_bin + lax.broadcasted_iota(jnp.int32, (pooled_bins, edits), 0) * POOL
    back = lax.broadcasted_iota(jnp.int32, (pooled_bins, shard_bins), 1) - POOL * (
        lax.broadcasted_iota(jnp.int32, (pooled_bins, shard_bins), 0)
    )
    take = ((back >= 0) & (back < POOL)).astype(jnp.float32).astype(jnp.bfloat16)
    for move in small:
        move.wait()
    for phase in range(phases):
        dist_ref[phase] = gain_ref[...] * feature[phase]
    weight = jnp.concatenate([weight_ref[...].astype(jnp.float32)] * 2, axis=1)
    line = lax.broadcasted_iota(jnp.int32, head_ref.shape, 0)
    half = lax.broadcasted_iota(jnp.int32, head_ref.shape, 1) >= channels
    head_ref[...] = jnp.where(line == half.astype(jnp.int32), weight, 0.0).astype(jnp.bfloat16)
    ahead = pos_ref[...] - bins
    in_bin = ((ahead >= 0) & (ahead < POOL)).astype(jnp.float32)
    edited = None
    for base in range(BASES):
        is_base = (tok_ref[...] == base).astype(jnp.float32)
        count = jnp.sum(in_bin * is_base, axis=1, keepdims=True)
        term = count * bases_ref[base : base + 1].astype(jnp.float32)
        edited = term if edited is None else edited + term
    got_embedding.wait()
    summed = edited + jnp.dot(take, embedding_ref[...], preferred_element_type=jnp.float32)
    pooled = (summed * (1.0 / POOL)).astype(jnp.bfloat16)
    sides = []
    for move, ref in ((got_w_row, w_row_ref), (got_w_col, w_col_ref)):
        move.wait()
        sides.append(jnp.dot(pooled, ref[...], preferred_element_type=jnp.float32).astype(jnp.bfloat16))
    both = jnp.concatenate(sides, axis=1)
    for k in range(copies):
        copies_ref[k] = both


def projected(embedding, bases_table, edit_pos, edit_tok, w_row, w_col, dist_gain, head_weight, map_bins, copies, size, table):
    vmem = pl.BlockSpec(memory_space=pltpu.VMEM)
    operands = (
        embedding,
        bases_table,
        edit_pos[None],
        edit_tok[None],
        w_row,
        w_col,
        dist_gain[None],
        head_weight[None],
    )
    channels = w_row.shape[1]
    return pl.pallas_call(
        functools.partial(project_kernel, map_bins, size, table),
        out_shape=(
            jax.ShapeDtypeStruct((copies, embedding.shape[0] // POOL, 2 * channels), jnp.bfloat16),
            jax.ShapeDtypeStruct((4, 8 * (tiles_of(size) + (size + 2 * MARGIN) // 4 - 1), channels), jnp.float32),
            jax.ShapeDtypeStruct((16, 2 * channels), jnp.bfloat16),
        ),
        in_specs=[pl.BlockSpec(memory_space=pltpu.HBM)] * 8,
        out_specs=(vmem, vmem, vmem),
        scratch_shapes=[pltpu.VMEM(x.shape, x.dtype) for x in operands] + [pltpu.SemaphoreType.DMA((8,))],
        compiler_params=pltpu.CompilerParams(vmem_limit_bytes=16 * 1024 * 1024),
    )(*(pltpu.with_memory_space_constraint(x, pltpu.HBM) for x in operands))


def map_kernel(
    map_bins, size, table, proj_ref, dist_ref, first_ref, second_ref, head_ref,
    kept_ref, sent_ref, row_ref, col_ref, own_ref, moved_ref, hidden_ref, pairs_one_ref, pairs_two_ref,
    mixed_ref, score_ref, filled,
):
    channels = head_ref.shape[1] // 2
    tiles = tiles_of(size)
    wide = 16 * (tiles - 2)
    breadth = 4 * size
    pair_rows = size + 2 * MARGIN
    couples = pair_rows // 2
    hidden_couples = size // 2 + SECOND_SPACING
    depth = 3 * channels
    row_a, col_a, row_b, col_b, diagonal, _ = lookup(table)
    rows, cols = (row_a * size, row_b * size), (col_a * size, col_b * size)
    fills = []
    for ref, given in ((pairs_one_ref, first_ref), (pairs_two_ref, second_ref)):
        ref[3 * depth :, :channels] = jnp.zeros((depth, channels), jnp.bfloat16)
        ref[:depth, channels:] = jnp.zeros((depth, channels), jnp.bfloat16)
        for half in range(2):
            place = ref.at[pl.ds(half * depth, 3 * depth), pl.ds(half * channels, channels)]
            fills.append(pltpu.make_async_copy(given, place, filled.at[len(fills)]))
            fills[-1].start()

    def of_block(lane, values):
        return jnp.where((lane & 2) == 0, values[0], values[1])

    def spread(ref, part, offset, along):
        count = ref.shape[0]
        at = lax.broadcasted_iota(jnp.int32, (count, map_bins), 0)
        lane = at & 7
        bins = along(at >> 3, lane) + of_block(lane, offset)
        hot = (bins == lax.broadcasted_iota(jnp.int32, (count, map_bins), 1)).astype(jnp.float32)
        found = jnp.dot(
            hot.astype(jnp.bfloat16),
            proj_ref[:, part * channels : (part + 1) * channels],
            preferred_element_type=jnp.float32,
        )
        bins = bins[:, :channels]
        ref[...] = jnp.where((bins >= 0) & (bins < map_bins), found, OUTSIDE)

    spread(col_ref, 1, cols, lambda tile, lane: 4 * tile + 2 * (lane >> 2) + (lane & 1) - PAD)
    spread(row_ref, 0, rows, lambda row, lane: row - MARGIN)
    lane = lax.broadcasted_iota(jnp.int32, (16, channels), 0) & 7
    last_start = map_bins - size
    left = of_block(lane, [jnp.where(col > 0, 1.0, 0.0) for col in cols])
    right = of_block(lane, [jnp.where(col < last_start, 1.0, 0.0) for col in cols])
    above = of_block(lane, [jnp.where(row > 0, 1.0, 0.0) for row in rows])
    below = of_block(lane, [jnp.where(row < last_start, 1.0, 0.0) for row in rows])

    def couple(two):
        parts = [x.reshape(-1, 1, 8, channels) for x in two]
        return jnp.concatenate(parts, axis=1).reshape(-1, channels).astype(jnp.bfloat16)

    def build(c):
        values, ahead = [], []
        for p in (2 * c, 2 * c + 1):
            at = 8 * (pair_rows // 4 - 1 - p // 4)
            apart = dist_ref[p % 4, at : at + 8 * tiles]
            line = jnp.concatenate([row_ref[8 * p : 8 * p + 8]] * tiles, axis=0)
            value = relu(col_ref[...] + apart + line)
            values.append(value[8 : 8 * (tiles - 1)])
            ahead.append(pltpu.roll(value, 8 * tiles - 4, 0)[: 8 * (tiles - 1)])
        own_ref[c] = couple(values)
        moved_ref[c] = couple(ahead)

    def paired(taps, bases, step, weight):
        lhs = [
            jnp.concatenate([tap for k in range(4) for tap in taps(base + k * step)], axis=1) for base in bases
        ]
        out = jnp.dot(jnp.concatenate(lhs, axis=0), weight[...], preferred_element_type=jnp.float32)
        tall = out.shape[0] // len(bases)
        return [
            [out[n * tall : (n + 1) * tall, half * channels : (half + 1) * channels] for half in range(2)]
            for n in range(len(bases))
        ]

    def first_taps(c):
        return moved_ref[c, :wide], own_ref[c], moved_ref[c, 16 : wide + 16]

    def second_taps(c):
        return tuple(hidden_ref[c, 16 * b : 16 * b + breadth] for b in range(3))

    def keep_hidden(bases, out):
        for n, base in enumerate(bases):
            for half in range(2):
                c = base + half
                value = own_ref[c + 1].astype(jnp.float32) + relu(out[n][half])
                for edge, flags in ((c < 2, above), (c >= hidden_couples - 2, below)):
                    if edge:
                        value = value * jnp.concatenate([flags] * (tiles - 2), axis=0)
                value = jnp.concatenate(
                    [value[:16] * left, value[16 : wide - 16], value[wide - 16 :] * right], axis=0
                )
                hidden_ref[c] = value.astype(jnp.bfloat16)

    def keep_score(bases, out):
        last = []
        for n, base in enumerate(bases):
            halves = []
            for half in range(2):
                own = hidden_ref[base + 2 * half + 2, 16 : 16 + breadth].astype(jnp.float32)
                halves.append((own + relu(out[n][half])).astype(jnp.bfloat16))
            last.append(jnp.concatenate(halves, axis=1))
        got = lax.dot_general(
            head_ref[...],
            jnp.concatenate(last, axis=0),
            (((1,), (1,)), ((), ())),
            preferred_element_type=jnp.float32,
        )
        lines = [got[half : half + 1, n * breadth : (n + 1) * breadth] for half in range(2) for n in range(2)]
        mixed_ref[bases[0] : bases[0] + 4] = jnp.concatenate(lines, axis=0)

    first_groups, second_groups = hidden_couples // 4, size // 8
    for c in range(8):
        build(c)
    for fill in fills:
        fill.wait()
    for s in range(first_groups + 1):
        one = two = None
        first_bases, second_bases = (4 * s, 4 * s + 2), (4 * (s - 2), 4 * (s - 2) + 1)
        if s < first_groups:
            one = paired(first_taps, first_bases, 1, pairs_one_ref)
        for c in range(4 * (s + 2), min(4 * (s + 3), couples)):
            build(c)
        if 0 <= s - 2 < second_groups:
            two = paired(second_taps, second_bases, 2, pairs_two_ref)
        if one is not None:
            keep_hidden(first_bases, one)
        if two is not None:
            keep_score(second_bases, two)
    source = lax.broadcasted_iota(jnp.int32, (breadth, breadth), 0)
    place = ((source >> 3) & 1) * (2 * size) + ((source >> 1) & 1) * size
    place = place + 4 * (source >> 4) + 2 * ((source >> 2) & 1) + (source & 1)
    order = (place == lax.broadcasted_iota(jnp.int32, (breadth, breadth), 1)).astype(jnp.float32)
    order = order.astype(jnp.bfloat16)
    rest, ordered = mixed_ref[...], None
    for _ in range(3):
        piece = rest.astype(jnp.bfloat16)
        rest = rest - piece.astype(jnp.float32)
        moved = jnp.dot(piece, order, preferred_element_type=jnp.float32)
        ordered = moved if ordered is None else ordered + moved
    for row in range(2):
        score_ref[pl.ds(row, size // 2, 2)] = ordered[:, row * 2 * size : (row + 1) * 2 * size]
    score = score_ref[...]
    turned = score.T
    first, second = score[:, :size], score[:, size:]
    turned_first, turned_second = turned[:size], turned[size:]
    alone = diagonal == 1
    kept_ref[...] = 0.5 * (first + jnp.where(alone, turned_first, turned_second))
    sent_ref[...] = 0.5 * (second + jnp.where(alone, turned_second, turned_first))


def block_scores(every, dist_table, first_kernel, second_kernel, head, size, table):
    map_bins = every.shape[0]
    channels = dist_table.shape[2]
    tiles = tiles_of(size)
    pair_rows = size + 2 * MARGIN
    vmem = pl.BlockSpec(memory_space=pltpu.VMEM)
    block = jax.ShapeDtypeStruct((size, size), jnp.float32)
    return pl.pallas_call(
        functools.partial(map_kernel, map_bins, size, table),
        out_shape=(block, block),
        in_specs=[vmem] * 5,
        out_specs=(vmem, vmem),
        scratch_shapes=[
            pltpu.VMEM((8 * pair_rows, channels), jnp.float32),
            pltpu.VMEM((8 * tiles, channels), jnp.float32),
            pltpu.VMEM((pair_rows // 2, 16 * (tiles - 2), channels), jnp.bfloat16),
            pltpu.VMEM((pair_rows // 2, 16 * (tiles - 1), channels), jnp.bfloat16),
            pltpu.VMEM((size // 2 + SECOND_SPACING, 16 * (tiles - 2), channels), jnp.bfloat16),
            pltpu.VMEM((12 * channels, 2 * channels), jnp.bfloat16),
            pltpu.VMEM((12 * channels, 2 * channels), jnp.bfloat16),
            pltpu.VMEM((size // 2, 4 * size), jnp.float32),
            pltpu.VMEM((size, 2 * size), jnp.float32),
            pltpu.SemaphoreType.DMA((4,)),
        ],
        compiler_params=pltpu.CompilerParams(vmem_limit_bytes=40 * 1024 * 1024),
    )(
        every,
        dist_table,
        first_kernel.reshape(9 * channels, channels),
        second_kernel.reshape(9 * channels, channels),
        head,
    )


def on_device(
    embedding,
    bases_table,
    edit_pos,
    edit_tok,
    w_row,
    w_col,
    dist_gain,
    first_kernel,
    second_kernel,
    head_weight,
):
    n_rows, n_cols = lax.axis_size("row"), lax.axis_size("col")
    devices = n_rows * n_cols
    map_bins = embedding.shape[0] * devices // POOL
    table, target = plan(n_rows, n_cols)
    size = map_bins // max(n_rows, n_cols)
    copies, dist_table, head = projected(
        embedding, bases_table, edit_pos, edit_tok, w_row, w_col, dist_gain, head_weight, map_bins, devices, size, table
    )
    got = lax.all_to_all(copies, ("row", "col"), 0, 0)
    every = got.reshape(map_bins, got.shape[2])
    kept, sent = block_scores(every, dist_table, first_kernel, second_kernel, head, size, table)
    received = lax.ppermute(sent, ("row", "col"), [(device, target[device]) for device in range(devices)])
    place = lookup(table)[5]
    axis = 1 if n_rows > n_cols else 0
    return jnp.where(
        place == 0,
        jnp.concatenate([kept, received], axis=axis),
        jnp.concatenate([received, kept], axis=axis),
    )


def solution(mesh):
    placed = (P(("row", "col"), None), P(), P("cand"), P("cand"), P(), P(), P(), P(), P(), P())
    return jax.shard_map(
        on_device, mesh=mesh, in_specs=placed, out_specs=P(("cand", "row"), "col"), check_vma=False
    )
```

```python
import functools
import math

import jax
import jax.numpy as jnp
from jax import lax
from jax.experimental import pallas as pl
from jax.experimental.pallas import tpu as pltpu
from jax.sharding import PartitionSpec as P

POOL = 4
FIRST_SPACING = 2
SECOND_SPACING = 4
BASES = 4
MARGIN = FIRST_SPACING + SECOND_SPACING
PAD = 8
GROUP = 8
OUTSIDE = -1e30


def plan(n_rows, n_cols):
    wide = n_rows > n_cols
    blocks = max(n_rows, n_cols)
    assert blocks == 2 * min(n_rows, n_cols)

    def owner(i, j):
        return i * n_cols + j // 2 if wide else (i // 2) * n_cols + j

    held = {}
    for i in range(blocks):
        for j in range(blocks):
            held.setdefault(owner(i, j), []).append((i, j))

    def other(device, block):
        return next(b for b in held[device] if b != block)

    jobs, target = {}, {}

    def assign(device, kept, sent):
        place = held[device].index(kept)
        jobs[device] = (*kept, *sent, int(kept[0] == kept[1]), place)
        target[device] = owner(*sent)

    def walk(device, block):
        while device not in jobs:
            if block[0] == block[1]:
                return device, block
            sent = (block[1], block[0])
            assign(device, block, sent)
            device = owner(*sent)
            block = other(device, sent)
        return None, None

    for d in range(blocks):
        start = owner(d, d)
        if start not in jobs:
            end, last = walk(start, other(start, (d, d)))
            assign(end, last, (d, d))
    for device in sorted(held):
        if device not in jobs:
            walk(device, held[device][0])
    return [jobs[device] for device in sorted(jobs)], target


def tiles_of(size):
    return (size + 2 * PAD) // 4


def relu(x):
    return jnp.maximum(x, 0.0)


def lookup(table):
    n_cols = lax.axis_size("col")
    here = lax.axis_index("row") * n_cols + lax.axis_index("col")
    found = []
    for values in zip(*table):
        value = jnp.int32(values[0])
        for device in range(1, len(values)):
            value = jnp.where(here == device, jnp.int32(values[device]), value)
        found.append(value)
    return found


def project_kernel(
    map_bins, size, table, embedding_hbm, bases_hbm, pos_hbm, tok_hbm, w_row_hbm, w_col_hbm, gain_hbm, head_hbm,
    copies_ref, dist_ref, head_ref,
    embedding_ref, bases_ref, pos_ref, tok_ref, w_row_ref, w_col_ref, gain_ref, weight_ref, arrived,
):
    moves = [
        pltpu.make_async_copy(source, target, arrived.at[n])
        for n, (source, target) in enumerate(
            (
                (embedding_hbm, embedding_ref),
                (w_row_hbm, w_row_ref),
                (w_col_hbm, w_col_ref),
                (pos_hbm, pos_ref),
                (tok_hbm, tok_ref),
                (bases_hbm, bases_ref),
                (gain_hbm, gain_ref),
                (head_hbm, weight_ref),
            )
        )
    ]
    for move in moves:
        move.start()
    got_embedding, got_w_row, got_w_col, *small = moves
    shard_bins = embedding_ref.shape[0]
    copies, pooled_bins, _ = copies_ref.shape
    channels = gain_ref.shape[1]
    edits = pos_ref.shape[1]
    row_a, col_a, row_b, col_b, _, _ = lookup(table)
    phases, count, _ = dist_ref.shape
    at = lax.broadcasted_iota(jnp.int32, (count, channels), 0)
    lane = at & 7
    start = jnp.where((lane & 2) == 0, (col_a - row_a) * size, (col_b - row_b) * size)
    start = start + 4 * (at >> 3) + 2 * (lane >> 2) + (lane & 1) - 2 - 4 * ((size + 2 * MARGIN) // 4 - 1)
    feature = [
        jnp.log1p(jnp.abs(start - phase).astype(jnp.float32)) * (1.0 / math.log(map_bins))
        for phase in range(phases)
    ]
    first_bin = (lax.axis_index("row") * lax.axis_size("col") + lax.axis_index("col")) * shard_bins
    bins = first_bin + lax.broadcasted_iota(jnp.int32, (pooled_bins, edits), 0) * POOL
    back = lax.broadcasted_iota(jnp.int32, (pooled_bins, shard_bins), 1) - POOL * (
        lax.broadcasted_iota(jnp.int32, (pooled_bins, shard_bins), 0)
    )
    take = ((back >= 0) & (back < POOL)).astype(jnp.float32).astype(jnp.bfloat16)
    for move in small:
        move.wait()
    for phase in range(phases):
        dist_ref[phase] = gain_ref[...] * feature[phase]
    weight = jnp.concatenate([weight_ref[...].astype(jnp.float32)] * 2, axis=1)
    line = lax.broadcasted_iota(jnp.int32, head_ref.shape, 0)
    half = lax.broadcasted_iota(jnp.int32, head_ref.shape, 1) >= channels
    head_ref[...] = jnp.where(line == half.astype(jnp.int32), weight, 0.0).astype(jnp.bfloat16)
    ahead = pos_ref[...] - bins
    in_bin = ((ahead >= 0) & (ahead < POOL)).astype(jnp.float32)
    edited = None
    for base in range(BASES):
        is_base = (tok_ref[...] == base).astype(jnp.float32)
        count = jnp.sum(in_bin * is_base, axis=1, keepdims=True)
        term = count * bases_ref[base : base + 1].astype(jnp.float32)
        edited = term if edited is None else edited + term
    got_embedding.wait()
    summed = edited + jnp.dot(take, embedding_ref[...], preferred_element_type=jnp.float32)
    pooled = (summed * (1.0 / POOL)).astype(jnp.bfloat16)
    sides = []
    for move, ref in ((got_w_row, w_row_ref), (got_w_col, w_col_ref)):
        move.wait()
        sides.append(jnp.dot(pooled, ref[...], preferred_element_type=jnp.float32).astype(jnp.bfloat16))
    both = jnp.concatenate(sides, axis=1)
    for k in range(copies):
        copies_ref[k] = both


def projected(embedding, bases_table, edit_pos, edit_tok, w_row, w_col, dist_gain, head_weight, map_bins, copies, size, table):
    vmem = pl.BlockSpec(memory_space=pltpu.VMEM)
    operands = (
        embedding,
        bases_table,
        edit_pos[None],
        edit_tok[None],
        w_row,
        w_col,
        dist_gain[None],
        head_weight[None],
    )
    channels = w_row.shape[1]
    return pl.pallas_call(
        functools.partial(project_kernel, map_bins, size, table),
        out_shape=(
            jax.ShapeDtypeStruct((copies, embedding.shape[0] // POOL, 2 * channels), jnp.bfloat16),
            jax.ShapeDtypeStruct((4, 8 * (tiles_of(size) + (size + 2 * MARGIN) // 4 - 1), channels), jnp.float32),
            jax.ShapeDtypeStruct((16, 2 * channels), jnp.bfloat16),
        ),
        in_specs=[pl.BlockSpec(memory_space=pltpu.HBM)] * 8,
        out_specs=(vmem, vmem, vmem),
        scratch_shapes=[pltpu.VMEM(x.shape, x.dtype) for x in operands] + [pltpu.SemaphoreType.DMA((8,))],
        compiler_params=pltpu.CompilerParams(vmem_limit_bytes=16 * 1024 * 1024),
    )(*(pltpu.with_memory_space_constraint(x, pltpu.HBM) for x in operands))


def map_kernel(
    map_bins, size, table, proj_ref, dist_ref, first_ref, second_ref, head_ref,
    kept_ref, sent_ref, row_ref, col_ref, own_ref, moved_ref, hidden_ref, pairs_one_ref, pairs_two_ref,
    mixed_ref, score_ref,
):
    channels = head_ref.shape[1] // 2
    tiles = tiles_of(size)
    wide = 16 * (tiles - 2)
    breadth = 4 * size
    pair_rows = size + 2 * MARGIN
    couples = pair_rows // 2
    hidden_couples = size // 2 + SECOND_SPACING
    depth = 3 * channels
    row_a, col_a, row_b, col_b, diagonal, _ = lookup(table)
    rows, cols = (row_a * size, row_b * size), (col_a * size, col_b * size)
    for ref, given in ((pairs_one_ref, first_ref), (pairs_two_ref, second_ref)):
        ref[3 * depth :, :channels] = jnp.zeros((depth, channels), jnp.bfloat16)
        ref[:depth, channels:] = jnp.zeros((depth, channels), jnp.bfloat16)
        ref[: 3 * depth, :channels] = given[...]
        ref[depth:, channels:] = given[...]

    def of_block(lane, values):
        return jnp.where((lane & 2) == 0, values[0], values[1])

    def spread(ref, part, offset, along):
        count = ref.shape[0]
        at = lax.broadcasted_iota(jnp.int32, (count, map_bins), 0)
        lane = at & 7
        bins = along(at >> 3, lane) + of_block(lane, offset)
        hot = (bins == lax.broadcasted_iota(jnp.int32, (count, map_bins), 1)).astype(jnp.float32)
        found = jnp.dot(
            hot.astype(jnp.bfloat16),
            proj_ref[:, part * channels : (part + 1) * channels],
            preferred_element_type=jnp.float32,
        )
        bins = bins[:, :channels]
        ref[...] = jnp.where((bins >= 0) & (bins < map_bins), found, OUTSIDE)

    spread(col_ref, 1, cols, lambda tile, lane: 4 * tile + 2 * (lane >> 2) + (lane & 1) - PAD)
    spread(row_ref, 0, rows, lambda row, lane: row - MARGIN)
    lane = lax.broadcasted_iota(jnp.int32, (16, channels), 0) & 7
    last_start = map_bins - size
    left = of_block(lane, [jnp.where(col > 0, 1.0, 0.0) for col in cols])
    right = of_block(lane, [jnp.where(col < last_start, 1.0, 0.0) for col in cols])
    above = of_block(lane, [jnp.where(row > 0, 1.0, 0.0) for row in rows])
    below = of_block(lane, [jnp.where(row < last_start, 1.0, 0.0) for row in rows])

    def couple(two):
        parts = [x.reshape(-1, 1, 8, channels) for x in two]
        return jnp.concatenate(parts, axis=1).reshape(-1, channels).astype(jnp.bfloat16)

    def build(c):
        values, ahead = [], []
        for p in (2 * c, 2 * c + 1):
            at = 8 * (pair_rows // 4 - 1 - p // 4)
            apart = dist_ref[p % 4, at : at + 8 * tiles]
            line = jnp.concatenate([row_ref[8 * p : 8 * p + 8]] * tiles, axis=0)
            value = relu(col_ref[...] + apart + line)
            values.append(value[8 : 8 * (tiles - 1)])
            ahead.append(pltpu.roll(value, 8 * tiles - 4, 0)[: 8 * (tiles - 1)])
        own_ref[c] = couple(values)
        moved_ref[c] = couple(ahead)

    def paired(taps, bases, step, weight):
        lhs = [
            jnp.concatenate([tap for k in range(4) for tap in taps(base + k * step)], axis=1) for base in bases
        ]
        out = jnp.dot(jnp.concatenate(lhs, axis=0), weight[...], preferred_element_type=jnp.float32)
        tall = out.shape[0] // len(bases)
        return [
            [out[n * tall : (n + 1) * tall, half * channels : (half + 1) * channels] for half in range(2)]
            for n in range(len(bases))
        ]

    def first_taps(c):
        return moved_ref[c, :wide], own_ref[c], moved_ref[c, 16 : wide + 16]

    def second_taps(c):
        return tuple(hidden_ref[c, 16 * b : 16 * b + breadth] for b in range(3))

    def keep_hidden(bases, out):
        for n, base in enumerate(bases):
            for half in range(2):
                c = base + half
                value = own_ref[c + 1].astype(jnp.float32) + relu(out[n][half])
                for edge, flags in ((c < 2, above), (c >= hidden_couples - 2, below)):
                    if edge:
                        value = value * jnp.concatenate([flags] * (tiles - 2), axis=0)
                value = jnp.concatenate(
                    [value[:16] * left, value[16 : wide - 16], value[wide - 16 :] * right], axis=0
                )
                hidden_ref[c] = value.astype(jnp.bfloat16)

    def keep_score(bases, out):
        last = []
        for n, base in enumerate(bases):
            halves = []
            for half in range(2):
                own = hidden_ref[base + 2 * half + 2, 16 : 16 + breadth].astype(jnp.float32)
                halves.append((own + relu(out[n][half])).astype(jnp.bfloat16))
            last.append(jnp.concatenate(halves, axis=1))
        got = lax.dot_general(
            head_ref[...],
            jnp.concatenate(last, axis=0),
            (((1,), (1,)), ((), ())),
            preferred_element_type=jnp.float32,
        )
        lines = [got[half : half + 1, n * breadth : (n + 1) * breadth] for half in range(2) for n in range(2)]
        mixed_ref[bases[0] : bases[0] + 4] = jnp.concatenate(lines, axis=0)

    first_groups, second_groups = hidden_couples // 4, size // 8
    for c in range(8):
        build(c)
    for s in range(first_groups + 1):
        one = two = None
        first_bases, second_bases = (4 * s, 4 * s + 2), (4 * (s - 2), 4 * (s - 2) + 1)
        if s < first_groups:
            one = paired(first_taps, first_bases, 1, pairs_one_ref)
        for c in range(4 * (s + 2), min(4 * (s + 3), couples)):
            build(c)
        if 0 <= s - 2 < second_groups:
            two = paired(second_taps, second_bases, 2, pairs_two_ref)
        if one is not None:
            keep_hidden(first_bases, one)
        if two is not None:
            keep_score(second_bases, two)
    source = lax.broadcasted_iota(jnp.int32, (breadth, breadth), 0)
    place = ((source >> 3) & 1) * (2 * size) + ((source >> 1) & 1) * size
    place = place + 4 * (source >> 4) + 2 * ((source >> 2) & 1) + (source & 1)
    order = (place == lax.broadcasted_iota(jnp.int32, (breadth, breadth), 1)).astype(jnp.float32)
    order = order.astype(jnp.bfloat16)
    rest, ordered = mixed_ref[...], None
    for _ in range(3):
        piece = rest.astype(jnp.bfloat16)
        rest = rest - piece.astype(jnp.float32)
        moved = jnp.dot(piece, order, preferred_element_type=jnp.float32)
        ordered = moved if ordered is None else ordered + moved
    for row in range(2):
        score_ref[pl.ds(row, size // 2, 2)] = ordered[:, row * 2 * size : (row + 1) * 2 * size]
    score = score_ref[...]
    turned = score.T
    first, second = score[:, :size], score[:, size:]
    turned_first, turned_second = turned[:size], turned[size:]
    alone = diagonal == 1
    kept_ref[...] = 0.5 * (first + jnp.where(alone, turned_first, turned_second))
    sent_ref[...] = 0.5 * (second + jnp.where(alone, turned_second, turned_first))


def block_scores(every, dist_table, first_kernel, second_kernel, head, size, table):
    map_bins = every.shape[0]
    channels = dist_table.shape[2]
    tiles = tiles_of(size)
    pair_rows = size + 2 * MARGIN
    vmem = pl.BlockSpec(memory_space=pltpu.VMEM)
    block = jax.ShapeDtypeStruct((size, size), jnp.float32)
    return pl.pallas_call(
        functools.partial(map_kernel, map_bins, size, table),
        out_shape=(block, block),
        in_specs=[vmem] * 5,
        out_specs=(vmem, vmem),
        scratch_shapes=[
            pltpu.VMEM((8 * pair_rows, channels), jnp.float32),
            pltpu.VMEM((8 * tiles, channels), jnp.float32),
            pltpu.VMEM((pair_rows // 2, 16 * (tiles - 2), channels), jnp.bfloat16),
            pltpu.VMEM((pair_rows // 2, 16 * (tiles - 1), channels), jnp.bfloat16),
            pltpu.VMEM((size // 2 + SECOND_SPACING, 16 * (tiles - 2), channels), jnp.bfloat16),
            pltpu.VMEM((12 * channels, 2 * channels), jnp.bfloat16),
            pltpu.VMEM((12 * channels, 2 * channels), jnp.bfloat16),
            pltpu.VMEM((size // 2, 4 * size), jnp.float32),
            pltpu.VMEM((size, 2 * size), jnp.float32),
        ],
        compiler_params=pltpu.CompilerParams(vmem_limit_bytes=40 * 1024 * 1024),
    )(
        every,
        dist_table,
        first_kernel.reshape(9 * channels, channels),
        second_kernel.reshape(9 * channels, channels),
        head,
    )


def on_device(
    embedding,
    bases_table,
    edit_pos,
    edit_tok,
    w_row,
    w_col,
    dist_gain,
    first_kernel,
    second_kernel,
    head_weight,
):
    n_rows, n_cols = lax.axis_size("row"), lax.axis_size("col")
    devices = n_rows * n_cols
    map_bins = embedding.shape[0] * devices // POOL
    table, target = plan(n_rows, n_cols)
    size = map_bins // max(n_rows, n_cols)
    copies, dist_table, head = projected(
        embedding, bases_table, edit_pos, edit_tok, w_row, w_col, dist_gain, head_weight, map_bins, devices, size, table
    )
    got = lax.all_to_all(copies, ("row", "col"), 0, 0)
    every = got.reshape(map_bins, got.shape[2])
    kept, sent = block_scores(every, dist_table, first_kernel, second_kernel, head, size, table)
    received = lax.ppermute(sent, ("row", "col"), [(device, target[device]) for device in range(devices)])
    place = lookup(table)[5]
    axis = 1 if n_rows > n_cols else 0
    return jnp.where(
        place == 0,
        jnp.concatenate([kept, received], axis=axis),
        jnp.concatenate([received, kept], axis=axis),
    )


def solution(mesh):
    placed = (P(("row", "col"), None), P(), P("cand"), P("cand"), P(), P(), P(), P(), P(), P())
    return jax.shard_map(
        on_device, mesh=mesh, in_specs=placed, out_specs=P(("cand", "row"), "col"), check_vma=False
    )
```

```python
import functools
import math

import jax
import jax.numpy as jnp
from jax import lax
from jax.experimental import pallas as pl
from jax.experimental.pallas import tpu as pltpu
from jax.sharding import PartitionSpec as P

POOL = 4
FIRST_SPACING = 2
SECOND_SPACING = 4
BASES = 4
MARGIN = FIRST_SPACING + SECOND_SPACING
PAD = 8
GROUP = 8
OUTSIDE = -1e30


def plan(n_rows, n_cols):
    wide = n_rows > n_cols
    blocks = max(n_rows, n_cols)
    assert blocks == 2 * min(n_rows, n_cols)

    def owner(i, j):
        return i * n_cols + j // 2 if wide else (i // 2) * n_cols + j

    held = {}
    for i in range(blocks):
        for j in range(blocks):
            held.setdefault(owner(i, j), []).append((i, j))

    def other(device, block):
        return next(b for b in held[device] if b != block)

    jobs, target = {}, {}

    def assign(device, kept, sent):
        place = held[device].index(kept)
        jobs[device] = (*kept, *sent, int(kept[0] == kept[1]), place)
        target[device] = owner(*sent)

    def walk(device, block):
        while device not in jobs:
            if block[0] == block[1]:
                return device, block
            sent = (block[1], block[0])
            assign(device, block, sent)
            device = owner(*sent)
            block = other(device, sent)
        return None, None

    for d in range(blocks):
        start = owner(d, d)
        if start not in jobs:
            end, last = walk(start, other(start, (d, d)))
            assign(end, last, (d, d))
    for device in sorted(held):
        if device not in jobs:
            walk(device, held[device][0])
    return [jobs[device] for device in sorted(jobs)], target


def tiles_of(size):
    return (size + 2 * PAD) // 4


def relu(x):
    return jnp.maximum(x, 0.0)


def lookup(table):
    n_cols = lax.axis_size("col")
    here = lax.axis_index("row") * n_cols + lax.axis_index("col")
    found = []
    for values in zip(*table):
        value = jnp.int32(values[0])
        for device in range(1, len(values)):
            value = jnp.where(here == device, jnp.int32(values[device]), value)
        found.append(value)
    return found


def project_kernel(
    map_bins, size, table, embedding_hbm, bases_hbm, pos_hbm, tok_hbm, w_row_hbm, w_col_hbm, gain_hbm, head_hbm,
    copies_ref, dist_ref, head_ref,
    embedding_ref, bases_ref, pos_ref, tok_ref, w_row_ref, w_col_ref, gain_ref, weight_ref, arrived,
):
    moves = [
        pltpu.make_async_copy(source, target, arrived.at[n])
        for n, (source, target) in enumerate(
            (
                (embedding_hbm, embedding_ref),
                (w_row_hbm, w_row_ref),
                (w_col_hbm, w_col_ref),
                (pos_hbm, pos_ref),
                (tok_hbm, tok_ref),
                (bases_hbm, bases_ref),
                (gain_hbm, gain_ref),
                (head_hbm, weight_ref),
            )
        )
    ]
    for move in moves:
        move.start()
    got_embedding, got_w_row, got_w_col, *small = moves
    shard_bins = embedding_ref.shape[0]
    copies, pooled_bins, _ = copies_ref.shape
    channels = gain_ref.shape[1]
    edits = pos_ref.shape[1]
    row_a, col_a, row_b, col_b, _, _ = lookup(table)
    phases, count, _ = dist_ref.shape
    at = lax.broadcasted_iota(jnp.int32, (count, channels), 0)
    lane = at & 7
    start = jnp.where((lane & 2) == 0, (col_a - row_a) * size, (col_b - row_b) * size)
    start = start + 4 * (at >> 3) + 2 * (lane >> 2) + (lane & 1) - 2 - 4 * ((size + 2 * MARGIN) // 4 - 1)
    feature = [
        jnp.log1p(jnp.abs(start - phase).astype(jnp.float32)) * (1.0 / math.log(map_bins))
        for phase in range(phases)
    ]
    first_bin = (lax.axis_index("row") * lax.axis_size("col") + lax.axis_index("col")) * shard_bins
    bins = first_bin + lax.broadcasted_iota(jnp.int32, (pooled_bins, edits), 0) * POOL
    back = lax.broadcasted_iota(jnp.int32, (pooled_bins, shard_bins), 1) - POOL * (
        lax.broadcasted_iota(jnp.int32, (pooled_bins, shard_bins), 0)
    )
    take = ((back >= 0) & (back < POOL)).astype(jnp.float32).astype(jnp.bfloat16)
    for move in small:
        move.wait()
    for phase in range(phases):
        dist_ref[phase] = gain_ref[...] * feature[phase]
    weight = jnp.concatenate([weight_ref[...].astype(jnp.float32)] * 2, axis=1)
    line = lax.broadcasted_iota(jnp.int32, head_ref.shape, 0)
    half = lax.broadcasted_iota(jnp.int32, head_ref.shape, 1) >= channels
    head_ref[...] = jnp.where(line == half.astype(jnp.int32), weight, 0.0).astype(jnp.bfloat16)
    ahead = pos_ref[...] - bins
    in_bin = ((ahead >= 0) & (ahead < POOL)).astype(jnp.float32)
    edited = None
    for base in range(BASES):
        is_base = (tok_ref[...] == base).astype(jnp.float32)
        count = jnp.sum(in_bin * is_base, axis=1, keepdims=True)
        term = count * bases_ref[base : base + 1].astype(jnp.float32)
        edited = term if edited is None else edited + term
    got_embedding.wait()
    summed = edited + jnp.dot(take, embedding_ref[...], preferred_element_type=jnp.float32)
    pooled = (summed * (1.0 / POOL)).astype(jnp.bfloat16)
    sides = []
    for move, ref in ((got_w_row, w_row_ref), (got_w_col, w_col_ref)):
        move.wait()
        sides.append(jnp.dot(pooled, ref[...], preferred_element_type=jnp.float32).astype(jnp.bfloat16))
    both = jnp.concatenate(sides, axis=1)
    for k in range(copies):
        copies_ref[k] = both


def projected(embedding, bases_table, edit_pos, edit_tok, w_row, w_col, dist_gain, head_weight, map_bins, copies, size, table):
    vmem = pl.BlockSpec(memory_space=pltpu.VMEM)
    operands = (
        embedding,
        bases_table,
        edit_pos[None],
        edit_tok[None],
        w_row,
        w_col,
        dist_gain[None],
        head_weight[None],
    )
    channels = w_row.shape[1]
    return pl.pallas_call(
        functools.partial(project_kernel, map_bins, size, table),
        out_shape=(
            jax.ShapeDtypeStruct((copies, embedding.shape[0] // POOL, 2 * channels), jnp.bfloat16),
            jax.ShapeDtypeStruct((4, 8 * (tiles_of(size) + (size + 2 * MARGIN) // 4 - 1), channels), jnp.float32),
            jax.ShapeDtypeStruct((16, 2 * channels), jnp.bfloat16),
        ),
        in_specs=[pl.BlockSpec(memory_space=pltpu.HBM)] * 8,
        out_specs=(vmem, vmem, vmem),
        scratch_shapes=[pltpu.VMEM(x.shape, x.dtype) for x in operands] + [pltpu.SemaphoreType.DMA((8,))],
        compiler_params=pltpu.CompilerParams(vmem_limit_bytes=16 * 1024 * 1024),
    )(*(pltpu.with_memory_space_constraint(x, pltpu.HBM) for x in operands))


def map_kernel(
    map_bins, size, table, proj_ref, dist_ref, first_ref, second_ref, head_ref,
    kept_ref, sent_ref, row_ref, col_ref, own_ref, moved_ref, hidden_ref, pairs_one_ref, pairs_two_ref,
    mixed_ref, score_ref,
):
    channels = head_ref.shape[1] // 2
    tiles = tiles_of(size)
    wide = 16 * (tiles - 2)
    breadth = 4 * size
    pair_rows = size + 2 * MARGIN
    couples = pair_rows // 2
    hidden_couples = size // 2 + SECOND_SPACING
    depth = 3 * channels
    row_a, col_a, row_b, col_b, diagonal, _ = lookup(table)
    rows, cols = (row_a * size, row_b * size), (col_a * size, col_b * size)
    for ref, given in ((pairs_one_ref, first_ref), (pairs_two_ref, second_ref)):
        ref[3 * depth :, :channels] = jnp.zeros((depth, channels), jnp.bfloat16)
        ref[:depth, channels:] = jnp.zeros((depth, channels), jnp.bfloat16)
        ref[: 3 * depth, :channels] = given[...]
        ref[depth:, channels:] = given[...]

    def of_block(lane, values):
        return jnp.where((lane & 2) == 0, values[0], values[1])

    def spread(ref, part, offset, along):
        count = ref.shape[0]
        at = lax.broadcasted_iota(jnp.int32, (count, map_bins), 0)
        lane = at & 7
        bins = along(at >> 3, lane) + of_block(lane, offset)
        hot = (bins == lax.broadcasted_iota(jnp.int32, (count, map_bins), 1)).astype(jnp.float32)
        found = jnp.dot(
            hot.astype(jnp.bfloat16),
            proj_ref[:, part * channels : (part + 1) * channels],
            preferred_element_type=jnp.float32,
        )
        bins = bins[:, :channels]
        ref[...] = jnp.where((bins >= 0) & (bins < map_bins), found, OUTSIDE)

    spread(col_ref, 1, cols, lambda tile, lane: 4 * tile + 2 * (lane >> 2) + (lane & 1) - PAD)
    spread(row_ref, 0, rows, lambda row, lane: row - MARGIN)
    lane = lax.broadcasted_iota(jnp.int32, (16, channels), 0) & 7
    last_start = map_bins - size
    left = of_block(lane, [jnp.where(col > 0, 1.0, 0.0) for col in cols])
    right = of_block(lane, [jnp.where(col < last_start, 1.0, 0.0) for col in cols])
    above = of_block(lane, [jnp.where(row > 0, 1.0, 0.0) for row in rows])
    below = of_block(lane, [jnp.where(row < last_start, 1.0, 0.0) for row in rows])

    def couple(two):
        parts = [x.reshape(-1, 1, 8, channels) for x in two]
        return jnp.concatenate(parts, axis=1).reshape(-1, channels).astype(jnp.bfloat16)

    def build(c):
        values, ahead = [], []
        for p in (2 * c, 2 * c + 1):
            at = 8 * (pair_rows // 4 - 1 - p // 4)
            apart = dist_ref[p % 4, at : at + 8 * tiles]
            line = jnp.concatenate([row_ref[8 * p : 8 * p + 8]] * tiles, axis=0)
            value = relu(col_ref[...] + apart + line)
            values.append(value[8 : 8 * (tiles - 1)])
            ahead.append(pltpu.roll(value, 8 * tiles - 4, 0)[: 8 * (tiles - 1)])
        own_ref[c] = couple(values)
        moved_ref[c] = couple(ahead)

    def paired(taps, bases, step, weight):
        lhs = [
            jnp.concatenate([tap for k in range(4) for tap in taps(base + k * step)], axis=1) for base in bases
        ]
        lhs = lhs[0] if len(lhs) == 1 else jnp.concatenate(lhs, axis=0)
        out = jnp.dot(lhs, weight[...], preferred_element_type=jnp.float32)
        tall = out.shape[0] // len(bases)
        return [
            [out[n * tall : (n + 1) * tall, half * channels : (half + 1) * channels] for half in range(2)]
            for n in range(len(bases))
        ]

    def first_taps(c):
        return moved_ref[c, :wide], own_ref[c], moved_ref[c, 16 : wide + 16]

    def second_taps(c):
        return tuple(hidden_ref[c, 16 * b : 16 * b + breadth] for b in range(3))

    def keep_hidden(bases, out):
        for n, base in enumerate(bases):
            for half in range(2):
                c = base + half
                value = own_ref[c + 1].astype(jnp.float32) + relu(out[n][half])
                for edge, flags in ((c < 2, above), (c >= hidden_couples - 2, below)):
                    if edge:
                        value = value * jnp.concatenate([flags] * (tiles - 2), axis=0)
                value = jnp.concatenate(
                    [value[:16] * left, value[16 : wide - 16], value[wide - 16 :] * right], axis=0
                )
                hidden_ref[c] = value.astype(jnp.bfloat16)

    def keep_score(bases, out):
        last = []
        for n, base in enumerate(bases):
            halves = []
            for half in range(2):
                own = hidden_ref[base + 2 * half + 2, 16 : 16 + breadth].astype(jnp.float32)
                halves.append((own + relu(out[n][half])).astype(jnp.bfloat16))
            last.append(jnp.concatenate(halves, axis=1))
        got = lax.dot_general(
            head_ref[...],
            jnp.concatenate(last, axis=0),
            (((1,), (1,)), ((), ())),
            preferred_element_type=jnp.float32,
        )
        lines = [got[half : half + 1, n * breadth : (n + 1) * breadth] for half in range(2) for n in range(2)]
        mixed_ref[bases[0] : bases[0] + 4] = jnp.concatenate(lines, axis=0)

    first_groups, second_groups = hidden_couples // 4, size // 8
    for c in range(8):
        build(c)
    for s in range(first_groups + 1):
        later = list(range(4 * (s + 2), min(4 * (s + 3), couples)))
        seconds = []
        for part in range(2):
            one = None
            first_base, second_base = 4 * s + 2 * part, 4 * (s - 2) + part
            if s < first_groups:
                one = paired(first_taps, (first_base,), 1, pairs_one_ref)
            for c in later[2 * part : 2 * part + 2]:
                build(c)
            if 0 <= s - 2 < second_groups:
                seconds += paired(second_taps, (second_base,), 2, pairs_two_ref)
            if one is not None:
                keep_hidden((first_base,), one)
        if seconds:
            keep_score((4 * (s - 2), 4 * (s - 2) + 1), seconds)
    source = lax.broadcasted_iota(jnp.int32, (breadth, breadth), 0)
    place = ((source >> 3) & 1) * (2 * size) + ((source >> 1) & 1) * size
    place = place + 4 * (source >> 4) + 2 * ((source >> 2) & 1) + (source & 1)
    order = (place == lax.broadcasted_iota(jnp.int32, (breadth, breadth), 1)).astype(jnp.float32)
    order = order.astype(jnp.bfloat16)
    rest, ordered = mixed_ref[...], None
    for _ in range(3):
        piece = rest.astype(jnp.bfloat16)
        rest = rest - piece.astype(jnp.float32)
        moved = jnp.dot(piece, order, preferred_element_type=jnp.float32)
        ordered = moved if ordered is None else ordered + moved
    for row in range(2):
        score_ref[pl.ds(row, size // 2, 2)] = ordered[:, row * 2 * size : (row + 1) * 2 * size]
    score = score_ref[...]
    turned = score.T
    first, second = score[:, :size], score[:, size:]
    turned_first, turned_second = turned[:size], turned[size:]
    alone = diagonal == 1
    kept_ref[...] = 0.5 * (first + jnp.where(alone, turned_first, turned_second))
    sent_ref[...] = 0.5 * (second + jnp.where(alone, turned_second, turned_first))


def block_scores(every, dist_table, first_kernel, second_kernel, head, size, table):
    map_bins = every.shape[0]
    channels = dist_table.shape[2]
    tiles = tiles_of(size)
    pair_rows = size + 2 * MARGIN
    vmem = pl.BlockSpec(memory_space=pltpu.VMEM)
    block = jax.ShapeDtypeStruct((size, size), jnp.float32)
    return pl.pallas_call(
        functools.partial(map_kernel, map_bins, size, table),
        out_shape=(block, block),
        in_specs=[vmem] * 5,
        out_specs=(vmem, vmem),
        scratch_shapes=[
            pltpu.VMEM((8 * pair_rows, channels), jnp.float32),
            pltpu.VMEM((8 * tiles, channels), jnp.float32),
            pltpu.VMEM((pair_rows // 2, 16 * (tiles - 2), channels), jnp.bfloat16),
            pltpu.VMEM((pair_rows // 2, 16 * (tiles - 1), channels), jnp.bfloat16),
            pltpu.VMEM((size // 2 + SECOND_SPACING, 16 * (tiles - 2), channels), jnp.bfloat16),
            pltpu.VMEM((12 * channels, 2 * channels), jnp.bfloat16),
            pltpu.VMEM((12 * channels, 2 * channels), jnp.bfloat16),
            pltpu.VMEM((size // 2, 4 * size), jnp.float32),
            pltpu.VMEM((size, 2 * size), jnp.float32),
        ],
        compiler_params=pltpu.CompilerParams(vmem_limit_bytes=40 * 1024 * 1024),
    )(
        every,
        dist_table,
        first_kernel.reshape(9 * channels, channels),
        second_kernel.reshape(9 * channels, channels),
        head,
    )


def on_device(
    embedding,
    bases_table,
    edit_pos,
    edit_tok,
    w_row,
    w_col,
    dist_gain,
    first_kernel,
    second_kernel,
    head_weight,
):
    n_rows, n_cols = lax.axis_size("row"), lax.axis_size("col")
    devices = n_rows * n_cols
    map_bins = embedding.shape[0] * devices // POOL
    table, target = plan(n_rows, n_cols)
    size = map_bins // max(n_rows, n_cols)
    copies, dist_table, head = projected(
        embedding, bases_table, edit_pos, edit_tok, w_row, w_col, dist_gain, head_weight, map_bins, devices, size, table
    )
    got = lax.all_to_all(copies, ("row", "col"), 0, 0)
    every = got.reshape(map_bins, got.shape[2])
    kept, sent = block_scores(every, dist_table, first_kernel, second_kernel, head, size, table)
    received = lax.ppermute(sent, ("row", "col"), [(device, target[device]) for device in range(devices)])
    place = lookup(table)[5]
    axis = 1 if n_rows > n_cols else 0
    return jnp.where(
        place == 0,
        jnp.concatenate([kept, received], axis=axis),
        jnp.concatenate([received, kept], axis=axis),
    )


def solution(mesh):
    placed = (P(("row", "col"), None), P(), P("cand"), P("cand"), P(), P(), P(), P(), P(), P())
    return jax.shard_map(
        on_device, mesh=mesh, in_specs=placed, out_specs=P(("cand", "row"), "col"), check_vma=False
    )
```

```python
import functools
import math

import jax
import jax.numpy as jnp
from jax import lax
from jax.experimental import pallas as pl
from jax.experimental.pallas import tpu as pltpu
from jax.sharding import PartitionSpec as P

POOL = 4
FIRST_SPACING = 2
SECOND_SPACING = 4
BASES = 4
MARGIN = FIRST_SPACING + SECOND_SPACING
PAD = 8
GROUP = 8
OUTSIDE = -1e30


def plan(n_rows, n_cols):
    wide = n_rows > n_cols
    blocks = max(n_rows, n_cols)
    assert blocks == 2 * min(n_rows, n_cols)

    def owner(i, j):
        return i * n_cols + j // 2 if wide else (i // 2) * n_cols + j

    held = {}
    for i in range(blocks):
        for j in range(blocks):
            held.setdefault(owner(i, j), []).append((i, j))

    def other(device, block):
        return next(b for b in held[device] if b != block)

    jobs, target = {}, {}

    def assign(device, kept, sent):
        place = held[device].index(kept)
        jobs[device] = (*kept, *sent, int(kept[0] == kept[1]), place)
        target[device] = owner(*sent)

    def walk(device, block):
        while device not in jobs:
            if block[0] == block[1]:
                return device, block
            sent = (block[1], block[0])
            assign(device, block, sent)
            device = owner(*sent)
            block = other(device, sent)
        return None, None

    for d in range(blocks):
        start = owner(d, d)
        if start not in jobs:
            end, last = walk(start, other(start, (d, d)))
            assign(end, last, (d, d))
    for device in sorted(held):
        if device not in jobs:
            walk(device, held[device][0])
    return [jobs[device] for device in sorted(jobs)], target


def tiles_of(size):
    return (size + 2 * PAD) // 4


def relu(x):
    return jnp.maximum(x, 0.0)


def lookup(table):
    n_cols = lax.axis_size("col")
    here = lax.axis_index("row") * n_cols + lax.axis_index("col")
    found = []
    for values in zip(*table):
        value = jnp.int32(values[0])
        for device in range(1, len(values)):
            value = jnp.where(here == device, jnp.int32(values[device]), value)
        found.append(value)
    return found


def project_kernel(
    map_bins, size, table, embedding_hbm, bases_hbm, pos_hbm, tok_hbm, w_row_hbm, w_col_hbm, gain_hbm, head_hbm,
    copies_ref, dist_ref, head_ref,
    embedding_ref, bases_ref, pos_ref, tok_ref, w_row_ref, w_col_ref, gain_ref, weight_ref, arrived,
):
    moves = [
        pltpu.make_async_copy(source, target, arrived.at[n])
        for n, (source, target) in enumerate(
            (
                (embedding_hbm, embedding_ref),
                (w_row_hbm, w_row_ref),
                (w_col_hbm, w_col_ref),
                (pos_hbm, pos_ref),
                (tok_hbm, tok_ref),
                (bases_hbm, bases_ref),
                (gain_hbm, gain_ref),
                (head_hbm, weight_ref),
            )
        )
    ]
    for move in moves:
        move.start()
    got_embedding, got_w_row, got_w_col, *small = moves
    shard_bins = embedding_ref.shape[0]
    copies, pooled_bins, _ = copies_ref.shape
    channels = gain_ref.shape[1]
    edits = pos_ref.shape[1]
    row_a, col_a, row_b, col_b, _, _ = lookup(table)
    phases, count, _ = dist_ref.shape
    at = lax.broadcasted_iota(jnp.int32, (count, channels), 0)
    lane = at & 7
    start = jnp.where((lane & 2) == 0, (col_a - row_a) * size, (col_b - row_b) * size)
    start = start + 4 * (at >> 3) + 2 * (lane >> 2) + (lane & 1) - 2 - 4 * ((size + 2 * MARGIN) // 4 - 1)
    feature = [
        jnp.log1p(jnp.abs(start - phase).astype(jnp.float32)) * (1.0 / math.log(map_bins))
        for phase in range(phases)
    ]
    first_bin = (lax.axis_index("row") * lax.axis_size("col") + lax.axis_index("col")) * shard_bins
    bins = first_bin + lax.broadcasted_iota(jnp.int32, (pooled_bins, edits), 0) * POOL
    back = lax.broadcasted_iota(jnp.int32, (pooled_bins, shard_bins), 1) - POOL * (
        lax.broadcasted_iota(jnp.int32, (pooled_bins, shard_bins), 0)
    )
    take = ((back >= 0) & (back < POOL)).astype(jnp.float32).astype(jnp.bfloat16)
    for move in small:
        move.wait()
    for phase in range(phases):
        dist_ref[phase] = gain_ref[...] * feature[phase]
    weight = jnp.concatenate([weight_ref[...].astype(jnp.float32)] * 2, axis=1)
    line = lax.broadcasted_iota(jnp.int32, head_ref.shape, 0)
    half = lax.broadcasted_iota(jnp.int32, head_ref.shape, 1) >= channels
    head_ref[...] = jnp.where(line == half.astype(jnp.int32), weight, 0.0).astype(jnp.bfloat16)
    ahead = pos_ref[...] - bins
    in_bin = ((ahead >= 0) & (ahead < POOL)).astype(jnp.float32)
    edited = None
    for base in range(BASES):
        is_base = (tok_ref[...] == base).astype(jnp.float32)
        count = jnp.sum(in_bin * is_base, axis=1, keepdims=True)
        term = count * bases_ref[base : base + 1].astype(jnp.float32)
        edited = term if edited is None else edited + term
    got_embedding.wait()
    summed = edited + jnp.dot(take, embedding_ref[...], preferred_element_type=jnp.float32)
    pooled = (summed * (1.0 / POOL)).astype(jnp.bfloat16)
    sides = []
    for move, ref in ((got_w_row, w_row_ref), (got_w_col, w_col_ref)):
        move.wait()
        sides.append(jnp.dot(pooled, ref[...], preferred_element_type=jnp.float32).astype(jnp.bfloat16))
    both = jnp.concatenate(sides, axis=1)
    for k in range(copies):
        copies_ref[k] = both


def projected(embedding, bases_table, edit_pos, edit_tok, w_row, w_col, dist_gain, head_weight, map_bins, copies, size, table):
    vmem = pl.BlockSpec(memory_space=pltpu.VMEM)
    operands = (
        embedding,
        bases_table,
        edit_pos[None],
        edit_tok[None],
        w_row,
        w_col,
        dist_gain[None],
        head_weight[None],
    )
    channels = w_row.shape[1]
    return pl.pallas_call(
        functools.partial(project_kernel, map_bins, size, table),
        out_shape=(
            jax.ShapeDtypeStruct((copies, embedding.shape[0] // POOL, 2 * channels), jnp.bfloat16),
            jax.ShapeDtypeStruct((4, 8 * (tiles_of(size) + (size + 2 * MARGIN) // 4 - 1), channels), jnp.float32),
            jax.ShapeDtypeStruct((16, 2 * channels), jnp.bfloat16),
        ),
        in_specs=[pl.BlockSpec(memory_space=pltpu.HBM)] * 8,
        out_specs=(vmem, vmem, vmem),
        scratch_shapes=[pltpu.VMEM(x.shape, x.dtype) for x in operands] + [pltpu.SemaphoreType.DMA((8,))],
        compiler_params=pltpu.CompilerParams(vmem_limit_bytes=16 * 1024 * 1024),
    )(*(pltpu.with_memory_space_constraint(x, pltpu.HBM) for x in operands))


def map_kernel(
    map_bins, size, table, proj_ref, dist_ref, first_ref, second_ref, head_ref,
    kept_ref, sent_ref, row_ref, col_ref, own_ref, moved_ref, hidden_ref, pairs_one_ref, pairs_two_ref,
    mixed_ref, score_ref,
):
    channels = head_ref.shape[1] // 2
    tiles = tiles_of(size)
    wide = 16 * (tiles - 2)
    breadth = 4 * size
    pair_rows = size + 2 * MARGIN
    couples = pair_rows // 2
    hidden_couples = size // 2 + SECOND_SPACING
    depth = 3 * channels
    row_a, col_a, row_b, col_b, diagonal, _ = lookup(table)
    rows, cols = (row_a * size, row_b * size), (col_a * size, col_b * size)
    def place_weights(ref, given):
        ref[3 * depth :, :channels] = jnp.zeros((depth, channels), jnp.bfloat16)
        ref[:depth, channels:] = jnp.zeros((depth, channels), jnp.bfloat16)
        ref[: 3 * depth, :channels] = given[...]
        ref[depth:, channels:] = given[...]

    place_weights(pairs_one_ref, first_ref)

    def of_block(lane, values):
        return jnp.where((lane & 2) == 0, values[0], values[1])

    def spread(ref, part, offset, along):
        count = ref.shape[0]
        at = lax.broadcasted_iota(jnp.int32, (count, map_bins), 0)
        lane = at & 7
        bins = along(at >> 3, lane) + of_block(lane, offset)
        hot = (bins == lax.broadcasted_iota(jnp.int32, (count, map_bins), 1)).astype(jnp.float32)
        found = jnp.dot(
            hot.astype(jnp.bfloat16),
            proj_ref[:, part * channels : (part + 1) * channels],
            preferred_element_type=jnp.float32,
        )
        bins = bins[:, :channels]
        ref[...] = jnp.where((bins >= 0) & (bins < map_bins), found, OUTSIDE)

    spread(col_ref, 1, cols, lambda tile, lane: 4 * tile + 2 * (lane >> 2) + (lane & 1) - PAD)
    spread(row_ref, 0, rows, lambda row, lane: row - MARGIN)
    lane = lax.broadcasted_iota(jnp.int32, (16, channels), 0) & 7
    last_start = map_bins - size
    left = of_block(lane, [jnp.where(col > 0, 1.0, 0.0) for col in cols])
    right = of_block(lane, [jnp.where(col < last_start, 1.0, 0.0) for col in cols])
    above = of_block(lane, [jnp.where(row > 0, 1.0, 0.0) for row in rows])
    below = of_block(lane, [jnp.where(row < last_start, 1.0, 0.0) for row in rows])

    def couple(two):
        parts = [x.reshape(-1, 1, 8, channels) for x in two]
        return jnp.concatenate(parts, axis=1).reshape(-1, channels).astype(jnp.bfloat16)

    def build(c):
        values, ahead = [], []
        for p in (2 * c, 2 * c + 1):
            at = 8 * (pair_rows // 4 - 1 - p // 4)
            apart = dist_ref[p % 4, at : at + 8 * tiles]
            line = jnp.concatenate([row_ref[8 * p : 8 * p + 8]] * tiles, axis=0)
            value = relu(col_ref[...] + apart + line)
            values.append(value[8 : 8 * (tiles - 1)])
            ahead.append(pltpu.roll(value, 8 * tiles - 4, 0)[: 8 * (tiles - 1)])
        own_ref[c] = couple(values)
        moved_ref[c] = couple(ahead)

    def paired(taps, bases, step, weight):
        lhs = [
            jnp.concatenate([tap for k in range(4) for tap in taps(base + k * step)], axis=1) for base in bases
        ]
        lhs = lhs[0] if len(lhs) == 1 else jnp.concatenate(lhs, axis=0)
        out = jnp.dot(lhs, weight[...], preferred_element_type=jnp.float32)
        tall = out.shape[0] // len(bases)
        return [
            [out[n * tall : (n + 1) * tall, half * channels : (half + 1) * channels] for half in range(2)]
            for n in range(len(bases))
        ]

    def first_taps(c):
        return moved_ref[c, :wide], own_ref[c], moved_ref[c, 16 : wide + 16]

    def second_taps(c):
        return tuple(hidden_ref[c, 16 * b : 16 * b + breadth] for b in range(3))

    def keep_hidden(bases, out):
        for n, base in enumerate(bases):
            for half in range(2):
                c = base + half
                value = own_ref[c + 1].astype(jnp.float32) + relu(out[n][half])
                for edge, flags in ((c < 2, above), (c >= hidden_couples - 2, below)):
                    if edge:
                        value = value * jnp.concatenate([flags] * (tiles - 2), axis=0)
                value = jnp.concatenate(
                    [value[:16] * left, value[16 : wide - 16], value[wide - 16 :] * right], axis=0
                )
                hidden_ref[c] = value.astype(jnp.bfloat16)

    def keep_score(base, out):
        halves = []
        for half in range(2):
            own = hidden_ref[base + 2 * half + 2, 16 : 16 + breadth].astype(jnp.float32)
            halves.append((own + relu(out[half])).astype(jnp.bfloat16))
        got = lax.dot_general(
            head_ref[...],
            jnp.concatenate(halves, axis=1),
            (((1,), (1,)), ((), ())),
            preferred_element_type=jnp.float32,
        )
        for half in range(2):
            mixed_ref[base + 2 * half : base + 2 * half + 1] = got[half : half + 1]

    first_groups, second_groups = hidden_couples // 4, size // 8
    for c in range(6):
        build(c)
    waiting = None
    for s in range(first_groups + 1):
        for part in range(2):
            one = two = None
            first_base, second_base = 4 * s + 2 * part, 4 * (s - 2) + part
            if s < first_groups:
                one = paired(first_taps, (first_base,), 1, pairs_one_ref)
            if first_base == 0:
                place_weights(pairs_two_ref, second_ref)
            if waiting is not None:
                keep_score(*waiting)
                waiting = None
            for c in range(first_base + 6, min(first_base + 8, couples)):
                build(c)
            if 0 <= s - 2 < second_groups:
                two = paired(second_taps, (second_base,), 2, pairs_two_ref)
            if one is not None:
                keep_hidden((first_base,), one)
            if two is not None:
                waiting = second_base, two[0]
    keep_score(*waiting)
    source = lax.broadcasted_iota(jnp.int32, (breadth, breadth), 0)
    place = ((source >> 3) & 1) * (2 * size) + ((source >> 1) & 1) * size
    place = place + 4 * (source >> 4) + 2 * ((source >> 2) & 1) + (source & 1)
    order = (place == lax.broadcasted_iota(jnp.int32, (breadth, breadth), 1)).astype(jnp.float32)
    order = order.astype(jnp.bfloat16)
    rest, ordered = mixed_ref[...], None
    for _ in range(3):
        piece = rest.astype(jnp.bfloat16)
        rest = rest - piece.astype(jnp.float32)
        moved = jnp.dot(piece, order, preferred_element_type=jnp.float32)
        ordered = moved if ordered is None else ordered + moved
    for row in range(2):
        score_ref[pl.ds(row, size // 2, 2)] = ordered[:, row * 2 * size : (row + 1) * 2 * size]
    score = score_ref[...]
    turned = score.T
    first, second = score[:, :size], score[:, size:]
    turned_first, turned_second = turned[:size], turned[size:]
    alone = diagonal == 1
    kept_ref[...] = 0.5 * (first + jnp.where(alone, turned_first, turned_second))
    sent_ref[...] = 0.5 * (second + jnp.where(alone, turned_second, turned_first))


def block_scores(every, dist_table, first_kernel, second_kernel, head, size, table):
    map_bins = every.shape[0]
    channels = dist_table.shape[2]
    tiles = tiles_of(size)
    pair_rows = size + 2 * MARGIN
    vmem = pl.BlockSpec(memory_space=pltpu.VMEM)
    block = jax.ShapeDtypeStruct((size, size), jnp.float32)
    return pl.pallas_call(
        functools.partial(map_kernel, map_bins, size, table),
        out_shape=(block, block),
        in_specs=[vmem] * 5,
        out_specs=(vmem, vmem),
        scratch_shapes=[
            pltpu.VMEM((8 * pair_rows, channels), jnp.float32),
            pltpu.VMEM((8 * tiles, channels), jnp.float32),
            pltpu.VMEM((pair_rows // 2, 16 * (tiles - 2), channels), jnp.bfloat16),
            pltpu.VMEM((pair_rows // 2, 16 * (tiles - 1), channels), jnp.bfloat16),
            pltpu.VMEM((size // 2 + SECOND_SPACING, 16 * (tiles - 2), channels), jnp.bfloat16),
            pltpu.VMEM((12 * channels, 2 * channels), jnp.bfloat16),
            pltpu.VMEM((12 * channels, 2 * channels), jnp.bfloat16),
            pltpu.VMEM((size // 2, 4 * size), jnp.float32),
            pltpu.VMEM((size, 2 * size), jnp.float32),
        ],
        compiler_params=pltpu.CompilerParams(vmem_limit_bytes=40 * 1024 * 1024),
    )(
        every,
        dist_table,
        first_kernel.reshape(9 * channels, channels),
        second_kernel.reshape(9 * channels, channels),
        head,
    )


def on_device(
    embedding,
    bases_table,
    edit_pos,
    edit_tok,
    w_row,
    w_col,
    dist_gain,
    first_kernel,
    second_kernel,
    head_weight,
):
    n_rows, n_cols = lax.axis_size("row"), lax.axis_size("col")
    devices = n_rows * n_cols
    map_bins = embedding.shape[0] * devices // POOL
    table, target = plan(n_rows, n_cols)
    size = map_bins // max(n_rows, n_cols)
    copies, dist_table, head = projected(
        embedding, bases_table, edit_pos, edit_tok, w_row, w_col, dist_gain, head_weight, map_bins, devices, size, table
    )
    got = lax.all_to_all(copies, ("row", "col"), 0, 0)
    every = got.reshape(map_bins, got.shape[2])
    kept, sent = block_scores(every, dist_table, first_kernel, second_kernel, head, size, table)
    received = lax.ppermute(sent, ("row", "col"), [(device, target[device]) for device in range(devices)])
    place = lookup(table)[5]
    axis = 1 if n_rows > n_cols else 0
    return jnp.where(
        place == 0,
        jnp.concatenate([kept, received], axis=axis),
        jnp.concatenate([received, kept], axis=axis),
    )


def solution(mesh):
    placed = (P(("row", "col"), None), P(), P("cand"), P("cand"), P(), P(), P(), P(), P(), P())
    return jax.shard_map(
        on_device, mesh=mesh, in_specs=placed, out_specs=P(("cand", "row"), "col"), check_vma=False
    )
```

```python
import functools
import math

import jax
import jax.numpy as jnp
from jax import lax
from jax.experimental import pallas as pl
from jax.experimental.pallas import tpu as pltpu
from jax.sharding import PartitionSpec as P

POOL = 4
FIRST_SPACING = 2
SECOND_SPACING = 4
BASES = 4
MARGIN = FIRST_SPACING + SECOND_SPACING
PAD = 8
GROUP = 8
OUTSIDE = -1e30


def plan(n_rows, n_cols):
    wide = n_rows > n_cols
    blocks = max(n_rows, n_cols)
    assert blocks == 2 * min(n_rows, n_cols)

    def owner(i, j):
        return i * n_cols + j // 2 if wide else (i // 2) * n_cols + j

    held = {}
    for i in range(blocks):
        for j in range(blocks):
            held.setdefault(owner(i, j), []).append((i, j))

    def other(device, block):
        return next(b for b in held[device] if b != block)

    jobs, target = {}, {}

    def assign(device, kept, sent):
        place = held[device].index(kept)
        jobs[device] = (*kept, *sent, int(kept[0] == kept[1]), place)
        target[device] = owner(*sent)

    def walk(device, block):
        while device not in jobs:
            if block[0] == block[1]:
                return device, block
            sent = (block[1], block[0])
            assign(device, block, sent)
            device = owner(*sent)
            block = other(device, sent)
        return None, None

    for d in range(blocks):
        start = owner(d, d)
        if start not in jobs:
            end, last = walk(start, other(start, (d, d)))
            assign(end, last, (d, d))
    for device in sorted(held):
        if device not in jobs:
            walk(device, held[device][0])
    return [jobs[device] for device in sorted(jobs)], target


def tiles_of(size):
    return (size + 2 * PAD) // 4


def relu(x):
    return jnp.maximum(x, 0.0)


def lookup(table):
    n_cols = lax.axis_size("col")
    here = lax.axis_index("row") * n_cols + lax.axis_index("col")
    found = []
    for values in zip(*table):
        value = jnp.int32(values[0])
        for device in range(1, len(values)):
            value = jnp.where(here == device, jnp.int32(values[device]), value)
        found.append(value)
    return found


def project_kernel(
    map_bins, size, table, embedding_hbm, bases_hbm, pos_hbm, tok_hbm, w_row_hbm, w_col_hbm, gain_hbm, head_hbm,
    copies_ref, dist_ref, head_ref,
    embedding_ref, bases_ref, pos_ref, tok_ref, w_row_ref, w_col_ref, gain_ref, weight_ref, arrived,
):
    moves = [
        pltpu.make_async_copy(source, target, arrived.at[n])
        for n, (source, target) in enumerate(
            (
                (embedding_hbm, embedding_ref),
                (w_row_hbm, w_row_ref),
                (w_col_hbm, w_col_ref),
                (pos_hbm, pos_ref),
                (tok_hbm, tok_ref),
                (bases_hbm, bases_ref),
                (gain_hbm, gain_ref),
                (head_hbm, weight_ref),
            )
        )
    ]
    for move in moves:
        move.start()
    got_embedding, got_w_row, got_w_col, *small = moves
    shard_bins = embedding_ref.shape[0]
    copies, pooled_bins, _ = copies_ref.shape
    channels = gain_ref.shape[1]
    edits = pos_ref.shape[1]
    row_a, col_a, row_b, col_b, _, _ = lookup(table)
    phases, count, _ = dist_ref.shape
    at = lax.broadcasted_iota(jnp.int32, (count, channels), 0)
    lane = at & 7
    start = jnp.where((lane & 2) == 0, (col_a - row_a) * size, (col_b - row_b) * size)
    start = start + 4 * (at >> 3) + 2 * (lane >> 2) + (lane & 1) - 2 - 4 * ((size + 2 * MARGIN) // 4 - 1)
    feature = [
        jnp.log1p(jnp.abs(start - phase).astype(jnp.float32)) * (1.0 / math.log(map_bins))
        for phase in range(phases)
    ]
    first_bin = (lax.axis_index("row") * lax.axis_size("col") + lax.axis_index("col")) * shard_bins
    bins = first_bin + lax.broadcasted_iota(jnp.int32, (pooled_bins, edits), 0) * POOL
    back = lax.broadcasted_iota(jnp.int32, (pooled_bins, shard_bins), 1) - POOL * (
        lax.broadcasted_iota(jnp.int32, (pooled_bins, shard_bins), 0)
    )
    take = ((back >= 0) & (back < POOL)).astype(jnp.float32).astype(jnp.bfloat16)
    for move in small:
        move.wait()
    for phase in range(phases):
        dist_ref[phase] = gain_ref[...] * feature[phase]
    weight = jnp.concatenate([weight_ref[...].astype(jnp.float32)] * 2, axis=1)
    line = lax.broadcasted_iota(jnp.int32, head_ref.shape, 0)
    half = lax.broadcasted_iota(jnp.int32, head_ref.shape, 1) >= channels
    head_ref[...] = jnp.where(line == half.astype(jnp.int32), weight, 0.0).astype(jnp.bfloat16)
    ahead = pos_ref[...] - bins
    in_bin = ((ahead >= 0) & (ahead < POOL)).astype(jnp.float32)
    edited = None
    for base in range(BASES):
        is_base = (tok_ref[...] == base).astype(jnp.float32)
        count = jnp.sum(in_bin * is_base, axis=1, keepdims=True)
        term = count * bases_ref[base : base + 1].astype(jnp.float32)
        edited = term if edited is None else edited + term
    got_embedding.wait()
    summed = edited + jnp.dot(take, embedding_ref[...], preferred_element_type=jnp.float32)
    pooled = (summed * (1.0 / POOL)).astype(jnp.bfloat16)
    sides = []
    for move, ref in ((got_w_row, w_row_ref), (got_w_col, w_col_ref)):
        move.wait()
        sides.append(jnp.dot(pooled, ref[...], preferred_element_type=jnp.float32).astype(jnp.bfloat16))
    both = jnp.concatenate(sides, axis=1)
    for k in range(copies):
        copies_ref[k] = both


def projected(embedding, bases_table, edit_pos, edit_tok, w_row, w_col, dist_gain, head_weight, map_bins, copies, size, table):
    vmem = pl.BlockSpec(memory_space=pltpu.VMEM)
    operands = (
        embedding,
        bases_table,
        edit_pos[None],
        edit_tok[None],
        w_row,
        w_col,
        dist_gain[None],
        head_weight[None],
    )
    channels = w_row.shape[1]
    return pl.pallas_call(
        functools.partial(project_kernel, map_bins, size, table),
        out_shape=(
            jax.ShapeDtypeStruct((copies, embedding.shape[0] // POOL, 2 * channels), jnp.bfloat16),
            jax.ShapeDtypeStruct((4, 8 * (tiles_of(size) + (size + 2 * MARGIN) // 4 - 1), channels), jnp.float32),
            jax.ShapeDtypeStruct((16, 2 * channels), jnp.bfloat16),
        ),
        in_specs=[pl.BlockSpec(memory_space=pltpu.HBM)] * 8,
        out_specs=(vmem, vmem, vmem),
        scratch_shapes=[pltpu.VMEM(x.shape, x.dtype) for x in operands] + [pltpu.SemaphoreType.DMA((8,))],
        compiler_params=pltpu.CompilerParams(vmem_limit_bytes=16 * 1024 * 1024),
    )(*(pltpu.with_memory_space_constraint(x, pltpu.HBM) for x in operands))


def map_kernel(
    map_bins, size, table, proj_ref, dist_ref, first_ref, second_ref, head_ref,
    kept_ref, sent_ref, row_ref, col_ref, own_ref, moved_ref, hidden_ref, pairs_one_ref, pairs_two_ref,
    last_ref, mixed_ref, score_ref,
):
    channels = head_ref.shape[1] // 2
    tiles = tiles_of(size)
    wide = 16 * (tiles - 2)
    breadth = 4 * size
    pair_rows = size + 2 * MARGIN
    couples = pair_rows // 2
    hidden_couples = size // 2 + SECOND_SPACING
    depth = 3 * channels
    row_a, col_a, row_b, col_b, diagonal, _ = lookup(table)
    rows, cols = (row_a * size, row_b * size), (col_a * size, col_b * size)
    for ref, given in ((pairs_one_ref, first_ref), (pairs_two_ref, second_ref)):
        ref[3 * depth :, :channels] = jnp.zeros((depth, channels), jnp.bfloat16)
        ref[:depth, channels:] = jnp.zeros((depth, channels), jnp.bfloat16)
        ref[: 3 * depth, :channels] = given[...]
        ref[depth:, channels:] = given[...]

    def of_block(lane, values):
        return jnp.where((lane & 2) == 0, values[0], values[1])

    def spread(ref, part, offset, along):
        count = ref.shape[0]
        at = lax.broadcasted_iota(jnp.int32, (count, map_bins), 0)
        lane = at & 7
        bins = along(at >> 3, lane) + of_block(lane, offset)
        hot = (bins == lax.broadcasted_iota(jnp.int32, (count, map_bins), 1)).astype(jnp.float32)
        found = jnp.dot(
            hot.astype(jnp.bfloat16),
            proj_ref[:, part * channels : (part + 1) * channels],
            preferred_element_type=jnp.float32,
        )
        bins = bins[:, :channels]
        ref[...] = jnp.where((bins >= 0) & (bins < map_bins), found, OUTSIDE)

    spread(col_ref, 1, cols, lambda tile, lane: 4 * tile + 2 * (lane >> 2) + (lane & 1) - PAD)
    spread(row_ref, 0, rows, lambda row, lane: row - MARGIN)
    lane = lax.broadcasted_iota(jnp.int32, (16, channels), 0) & 7
    last_start = map_bins - size
    left = of_block(lane, [jnp.where(col > 0, 1.0, 0.0) for col in cols])
    right = of_block(lane, [jnp.where(col < last_start, 1.0, 0.0) for col in cols])
    above = of_block(lane, [jnp.where(row > 0, 1.0, 0.0) for row in rows])
    below = of_block(lane, [jnp.where(row < last_start, 1.0, 0.0) for row in rows])

    def couple(two):
        parts = [x.reshape(-1, 1, 8, channels) for x in two]
        return jnp.concatenate(parts, axis=1).reshape(-1, channels).astype(jnp.bfloat16)

    def build(c):
        values, ahead = [], []
        for p in (2 * c, 2 * c + 1):
            at = 8 * (pair_rows // 4 - 1 - p // 4)
            apart = dist_ref[p % 4, at : at + 8 * tiles]
            line = jnp.concatenate([row_ref[8 * p : 8 * p + 8]] * tiles, axis=0)
            value = relu(col_ref[...] + apart + line)
            values.append(value[8 : 8 * (tiles - 1)])
            ahead.append(pltpu.roll(value, 8 * tiles - 4, 0)[: 8 * (tiles - 1)])
        own_ref[c] = couple(values)
        moved_ref[c] = couple(ahead)

    def paired(taps, bases, step, weight):
        lhs = [
            jnp.concatenate([tap for k in range(4) for tap in taps(base + k * step)], axis=1) for base in bases
        ]
        lhs = lhs[0] if len(lhs) == 1 else jnp.concatenate(lhs, axis=0)
        out = jnp.dot(lhs, weight[...], preferred_element_type=jnp.float32)
        tall = out.shape[0] // len(bases)
        return [
            [out[n * tall : (n + 1) * tall, half * channels : (half + 1) * channels] for half in range(2)]
            for n in range(len(bases))
        ]

    def first_taps(c):
        return moved_ref[c, :wide], own_ref[c], moved_ref[c, 16 : wide + 16]

    def second_taps(c):
        return tuple(hidden_ref[c, 16 * b : 16 * b + breadth] for b in range(3))

    def keep_hidden(bases, out):
        for n, base in enumerate(bases):
            for half in range(2):
                c = base + half
                value = own_ref[c + 1].astype(jnp.float32) + relu(out[n][half])
                for edge, flags in ((c < 2, above), (c >= hidden_couples - 2, below)):
                    if edge:
                        value = value * jnp.concatenate([flags] * (tiles - 2), axis=0)
                value = jnp.concatenate(
                    [value[:16] * left, value[16 : wide - 16], value[wide - 16 :] * right], axis=0
                )
                hidden_ref[c] = value.astype(jnp.bfloat16)

    def keep_last(base, out):
        for half in range(2):
            own = hidden_ref[base + 2 * half + 2, 16 : 16 + breadth].astype(jnp.float32)
            last_ref[base // 4 * 2 + base % 4, :, half * channels : (half + 1) * channels] = (
                own + relu(out[half])
            ).astype(jnp.bfloat16)

    def keep_scores(start, count):
        got = lax.dot_general(
            head_ref[...],
            last_ref[start : start + count].reshape(count * breadth, 2 * channels),
            (((1,), (1,)), ((), ())),
            preferred_element_type=jnp.float32,
        )
        lines = [
            got[half : half + 1, n * breadth : (n + 1) * breadth]
            for pair in range(0, count, 2)
            for half in range(2)
            for n in (pair, pair + 1)
        ]
        mixed_ref[2 * start : 2 * (start + count)] = jnp.concatenate(lines, axis=0)

    first_groups, second_groups = hidden_couples // 4, size // 8
    for c in range(8):
        build(c)
    for s in range(first_groups + 1):
        later = list(range(4 * (s + 2), min(4 * (s + 3), couples)))
        for part in range(2):
            one = seconds = None
            first_base, second_base = 4 * s + 2 * part, 4 * (s - 2) + part
            if s < first_groups:
                one = paired(first_taps, (first_base,), 1, pairs_one_ref)
            for c in later[2 * part : 2 * part + 2]:
                build(c)
            if 0 <= s - 2 < second_groups:
                seconds = paired(second_taps, (second_base,), 2, pairs_two_ref)
            if one is not None:
                keep_hidden((first_base,), one)
            if seconds:
                keep_last(second_base, seconds[0])
    for start in range(0, size // 4, 4):
        keep_scores(start, 4)
    source = lax.broadcasted_iota(jnp.int32, (breadth, breadth), 0)
    place = ((source >> 3) & 1) * (2 * size) + ((source >> 1) & 1) * size
    place = place + 4 * (source >> 4) + 2 * ((source >> 2) & 1) + (source & 1)
    order = (place == lax.broadcasted_iota(jnp.int32, (breadth, breadth), 1)).astype(jnp.float32)
    order = order.astype(jnp.bfloat16)
    rest, ordered = mixed_ref[...], None
    for _ in range(3):
        piece = rest.astype(jnp.bfloat16)
        rest = rest - piece.astype(jnp.float32)
        moved = jnp.dot(piece, order, preferred_element_type=jnp.float32)
        ordered = moved if ordered is None else ordered + moved
    for row in range(2):
        score_ref[pl.ds(row, size // 2, 2)] = ordered[:, row * 2 * size : (row + 1) * 2 * size]
    score = score_ref[...]
    turned = score.T
    first, second = score[:, :size], score[:, size:]
    turned_first, turned_second = turned[:size], turned[size:]
    alone = diagonal == 1
    kept_ref[...] = 0.5 * (first + jnp.where(alone, turned_first, turned_second))
    sent_ref[...] = 0.5 * (second + jnp.where(alone, turned_second, turned_first))


def block_scores(every, dist_table, first_kernel, second_kernel, head, size, table):
    map_bins = every.shape[0]
    channels = dist_table.shape[2]
    tiles = tiles_of(size)
    pair_rows = size + 2 * MARGIN
    vmem = pl.BlockSpec(memory_space=pltpu.VMEM)
    block = jax.ShapeDtypeStruct((size, size), jnp.float32)
    return pl.pallas_call(
        functools.partial(map_kernel, map_bins, size, table),
        out_shape=(block, block),
        in_specs=[vmem] * 5,
        out_specs=(vmem, vmem),
        scratch_shapes=[
            pltpu.VMEM((8 * pair_rows, channels), jnp.float32),
            pltpu.VMEM((8 * tiles, channels), jnp.float32),
            pltpu.VMEM((pair_rows // 2, 16 * (tiles - 2), channels), jnp.bfloat16),
            pltpu.VMEM((pair_rows // 2, 16 * (tiles - 1), channels), jnp.bfloat16),
            pltpu.VMEM((size // 2 + SECOND_SPACING, 16 * (tiles - 2), channels), jnp.bfloat16),
            pltpu.VMEM((12 * channels, 2 * channels), jnp.bfloat16),
            pltpu.VMEM((12 * channels, 2 * channels), jnp.bfloat16),
            pltpu.VMEM((size // 4, 4 * size, 2 * channels), jnp.bfloat16),
            pltpu.VMEM((size // 2, 4 * size), jnp.float32),
            pltpu.VMEM((size, 2 * size), jnp.float32),
        ],
        compiler_params=pltpu.CompilerParams(vmem_limit_bytes=40 * 1024 * 1024),
    )(
        every,
        dist_table,
        first_kernel.reshape(9 * channels, channels),
        second_kernel.reshape(9 * channels, channels),
        head,
    )


def on_device(
    embedding,
    bases_table,
    edit_pos,
    edit_tok,
    w_row,
    w_col,
    dist_gain,
    first_kernel,
    second_kernel,
    head_weight,
):
    n_rows, n_cols = lax.axis_size("row"), lax.axis_size("col")
    devices = n_rows * n_cols
    map_bins = embedding.shape[0] * devices // POOL
    table, target = plan(n_rows, n_cols)
    size = map_bins // max(n_rows, n_cols)
    copies, dist_table, head = projected(
        embedding, bases_table, edit_pos, edit_tok, w_row, w_col, dist_gain, head_weight, map_bins, devices, size, table
    )
    got = lax.all_to_all(copies, ("row", "col"), 0, 0)
    every = got.reshape(map_bins, got.shape[2])
    kept, sent = block_scores(every, dist_table, first_kernel, second_kernel, head, size, table)
    received = lax.ppermute(sent, ("row", "col"), [(device, target[device]) for device in range(devices)])
    place = lookup(table)[5]
    axis = 1 if n_rows > n_cols else 0
    return jnp.where(
        place == 0,
        jnp.concatenate([kept, received], axis=axis),
        jnp.concatenate([received, kept], axis=axis),
    )


def solution(mesh):
    placed = (P(("row", "col"), None), P(), P("cand"), P("cand"), P(), P(), P(), P(), P(), P())
    return jax.shard_map(
        on_device, mesh=mesh, in_specs=placed, out_specs=P(("cand", "row"), "col"), check_vma=False
    )
```

```python
import functools
import math

import jax
import jax.numpy as jnp
from jax import lax
from jax.experimental import pallas as pl
from jax.experimental.pallas import tpu as pltpu
from jax.sharding import PartitionSpec as P

POOL = 4
FIRST_SPACING = 2
SECOND_SPACING = 4
BASES = 4
MARGIN = FIRST_SPACING + SECOND_SPACING
PAD = 8
GROUP = 8
OUTSIDE = -1e30


def plan(n_rows, n_cols):
    wide = n_rows > n_cols
    blocks = max(n_rows, n_cols)
    assert blocks == 2 * min(n_rows, n_cols)

    def owner(i, j):
        return i * n_cols + j // 2 if wide else (i // 2) * n_cols + j

    held = {}
    for i in range(blocks):
        for j in range(blocks):
            held.setdefault(owner(i, j), []).append((i, j))

    def other(device, block):
        return next(b for b in held[device] if b != block)

    jobs, target = {}, {}

    def assign(device, kept, sent):
        place = held[device].index(kept)
        jobs[device] = (*kept, *sent, int(kept[0] == kept[1]), place)
        target[device] = owner(*sent)

    def walk(device, block):
        while device not in jobs:
            if block[0] == block[1]:
                return device, block
            sent = (block[1], block[0])
            assign(device, block, sent)
            device = owner(*sent)
            block = other(device, sent)
        return None, None

    for d in range(blocks):
        start = owner(d, d)
        if start not in jobs:
            end, last = walk(start, other(start, (d, d)))
            assign(end, last, (d, d))
    for device in sorted(held):
        if device not in jobs:
            walk(device, held[device][0])
    return [jobs[device] for device in sorted(jobs)], target


def tiles_of(size):
    return (size + 2 * PAD) // 4


def relu(x):
    return jnp.maximum(x, 0.0)


def lookup(table):
    n_cols = lax.axis_size("col")
    here = lax.axis_index("row") * n_cols + lax.axis_index("col")
    found = []
    for values in zip(*table):
        value = jnp.int32(values[0])
        for device in range(1, len(values)):
            value = jnp.where(here == device, jnp.int32(values[device]), value)
        found.append(value)
    return found


def project_kernel(
    map_bins, size, table, embedding_hbm, bases_hbm, pos_hbm, tok_hbm, w_row_hbm, w_col_hbm, gain_hbm, head_hbm,
    copies_ref, dist_ref, head_ref,
    embedding_ref, bases_ref, pos_ref, tok_ref, w_row_ref, w_col_ref, gain_ref, weight_ref, arrived,
):
    moves = [
        pltpu.make_async_copy(source, target, arrived.at[n])
        for n, (source, target) in enumerate(
            (
                (embedding_hbm, embedding_ref),
                (w_row_hbm, w_row_ref),
                (w_col_hbm, w_col_ref),
                (pos_hbm, pos_ref),
                (tok_hbm, tok_ref),
                (bases_hbm, bases_ref),
                (gain_hbm, gain_ref),
                (head_hbm, weight_ref),
            )
        )
    ]
    for move in moves:
        move.start()
    got_embedding, got_w_row, got_w_col, *small = moves
    shard_bins = embedding_ref.shape[0]
    copies, pooled_bins, _ = copies_ref.shape
    channels = gain_ref.shape[1]
    edits = pos_ref.shape[1]
    row_a, col_a, row_b, col_b, _, _ = lookup(table)
    phases, count, _ = dist_ref.shape
    at = lax.broadcasted_iota(jnp.int32, (count, channels), 0)
    lane = at & 7
    start = jnp.where((lane & 2) == 0, (col_a - row_a) * size, (col_b - row_b) * size)
    start = start + 4 * (at >> 3) + 2 * (lane >> 2) + (lane & 1) - 2 - 4 * ((size + 2 * MARGIN) // 4 - 1)
    feature = [
        jnp.log1p(jnp.abs(start - phase).astype(jnp.float32)) * (1.0 / math.log(map_bins))
        for phase in range(phases)
    ]
    first_bin = (lax.axis_index("row") * lax.axis_size("col") + lax.axis_index("col")) * shard_bins
    bins = first_bin + lax.broadcasted_iota(jnp.int32, (pooled_bins, edits), 0) * POOL
    back = lax.broadcasted_iota(jnp.int32, (pooled_bins, shard_bins), 1) - POOL * (
        lax.broadcasted_iota(jnp.int32, (pooled_bins, shard_bins), 0)
    )
    take = ((back >= 0) & (back < POOL)).astype(jnp.float32).astype(jnp.bfloat16)
    for move in small:
        move.wait()
    for phase in range(phases):
        dist_ref[phase] = gain_ref[...] * feature[phase]
    weight = jnp.broadcast_to(weight_ref[...].astype(jnp.float32), (channels, channels)).T
    column = lax.broadcasted_iota(jnp.int32, (channels, channels), 1)
    for n in range(head_ref.shape[0] // (2 * channels)):
        for half in range(2):
            at = (2 * n + half) * channels
            of_couple = 4 * (n // 2) + n % 2 + 2 * half
            head_ref[at : at + channels] = jnp.where(column == of_couple, weight, 0.0).astype(jnp.bfloat16)
    ahead = pos_ref[...] - bins
    in_bin = ((ahead >= 0) & (ahead < POOL)).astype(jnp.float32)
    edited = None
    for base in range(BASES):
        is_base = (tok_ref[...] == base).astype(jnp.float32)
        count = jnp.sum(in_bin * is_base, axis=1, keepdims=True)
        term = count * bases_ref[base : base + 1].astype(jnp.float32)
        edited = term if edited is None else edited + term
    got_embedding.wait()
    summed = edited + jnp.dot(take, embedding_ref[...], preferred_element_type=jnp.float32)
    pooled = (summed * (1.0 / POOL)).astype(jnp.bfloat16)
    sides = []
    for move, ref in ((got_w_row, w_row_ref), (got_w_col, w_col_ref)):
        move.wait()
        sides.append(jnp.dot(pooled, ref[...], preferred_element_type=jnp.float32).astype(jnp.bfloat16))
    both = jnp.concatenate(sides, axis=1)
    for k in range(copies):
        copies_ref[k] = both


def projected(embedding, bases_table, edit_pos, edit_tok, w_row, w_col, dist_gain, head_weight, map_bins, copies, size, table):
    vmem = pl.BlockSpec(memory_space=pltpu.VMEM)
    operands = (
        embedding,
        bases_table,
        edit_pos[None],
        edit_tok[None],
        w_row,
        w_col,
        dist_gain[None],
        head_weight[None],
    )
    channels = w_row.shape[1]
    return pl.pallas_call(
        functools.partial(project_kernel, map_bins, size, table),
        out_shape=(
            jax.ShapeDtypeStruct((copies, embedding.shape[0] // POOL, 2 * channels), jnp.bfloat16),
            jax.ShapeDtypeStruct((4, 8 * (tiles_of(size) + (size + 2 * MARGIN) // 4 - 1), channels), jnp.float32),
            jax.ShapeDtypeStruct((size // 2 * channels, channels), jnp.bfloat16),
        ),
        in_specs=[pl.BlockSpec(memory_space=pltpu.HBM)] * 8,
        out_specs=(vmem, vmem, vmem),
        scratch_shapes=[pltpu.VMEM(x.shape, x.dtype) for x in operands] + [pltpu.SemaphoreType.DMA((8,))],
        compiler_params=pltpu.CompilerParams(vmem_limit_bytes=16 * 1024 * 1024),
    )(*(pltpu.with_memory_space_constraint(x, pltpu.HBM) for x in operands))


def map_kernel(
    map_bins, size, table, proj_ref, dist_ref, first_ref, second_ref, head_ref,
    kept_ref, sent_ref, row_ref, col_ref, own_ref, moved_ref, hidden_ref, pairs_one_ref, pairs_two_ref,
    last_ref, score_ref,
):
    channels = head_ref.shape[1]
    tiles = tiles_of(size)
    wide = 16 * (tiles - 2)
    breadth = 4 * size
    pair_rows = size + 2 * MARGIN
    couples = pair_rows // 2
    hidden_couples = size // 2 + SECOND_SPACING
    depth = 3 * channels
    row_a, col_a, row_b, col_b, diagonal, _ = lookup(table)
    rows, cols = (row_a * size, row_b * size), (col_a * size, col_b * size)
    for ref, given in ((pairs_one_ref, first_ref), (pairs_two_ref, second_ref)):
        ref[3 * depth :, :channels] = jnp.zeros((depth, channels), jnp.bfloat16)
        ref[:depth, channels:] = jnp.zeros((depth, channels), jnp.bfloat16)
        ref[: 3 * depth, :channels] = given[...]
        ref[depth:, channels:] = given[...]

    def of_block(lane, values):
        return jnp.where((lane & 2) == 0, values[0], values[1])

    def spread(ref, part, offset, along):
        count = ref.shape[0]
        at = lax.broadcasted_iota(jnp.int32, (count, map_bins), 0)
        lane = at & 7
        bins = along(at >> 3, lane) + of_block(lane, offset)
        hot = (bins == lax.broadcasted_iota(jnp.int32, (count, map_bins), 1)).astype(jnp.float32)
        found = jnp.dot(
            hot.astype(jnp.bfloat16),
            proj_ref[:, part * channels : (part + 1) * channels],
            preferred_element_type=jnp.float32,
        )
        bins = bins[:, :channels]
        ref[...] = jnp.where((bins >= 0) & (bins < map_bins), found, OUTSIDE)

    spread(col_ref, 1, cols, lambda tile, lane: 4 * tile + 2 * (lane >> 2) + (lane & 1) - PAD)
    spread(row_ref, 0, rows, lambda row, lane: row - MARGIN)
    lane = lax.broadcasted_iota(jnp.int32, (16, channels), 0) & 7
    last_start = map_bins - size
    left = of_block(lane, [jnp.where(col > 0, 1.0, 0.0) for col in cols])
    right = of_block(lane, [jnp.where(col < last_start, 1.0, 0.0) for col in cols])
    above = of_block(lane, [jnp.where(row > 0, 1.0, 0.0) for row in rows])
    below = of_block(lane, [jnp.where(row < last_start, 1.0, 0.0) for row in rows])

    def couple(two):
        parts = [x.reshape(-1, 1, 8, channels) for x in two]
        return jnp.concatenate(parts, axis=1).reshape(-1, channels).astype(jnp.bfloat16)

    def build(c):
        values, ahead = [], []
        for p in (2 * c, 2 * c + 1):
            at = 8 * (pair_rows // 4 - 1 - p // 4)
            apart = dist_ref[p % 4, at : at + 8 * tiles]
            line = jnp.concatenate([row_ref[8 * p : 8 * p + 8]] * tiles, axis=0)
            value = relu(col_ref[...] + apart + line)
            values.append(value[8 : 8 * (tiles - 1)])
            ahead.append(pltpu.roll(value, 8 * tiles - 4, 0)[: 8 * (tiles - 1)])
        own_ref[c] = couple(values)
        moved_ref[c] = couple(ahead)

    def paired(taps, bases, step, weight):
        lhs = [
            jnp.concatenate([tap for k in range(4) for tap in taps(base + k * step)], axis=1) for base in bases
        ]
        lhs = lhs[0] if len(lhs) == 1 else jnp.concatenate(lhs, axis=0)
        out = jnp.dot(lhs, weight[...], preferred_element_type=jnp.float32)
        tall = out.shape[0] // len(bases)
        return [
            [out[n * tall : (n + 1) * tall, half * channels : (half + 1) * channels] for half in range(2)]
            for n in range(len(bases))
        ]

    def first_taps(c):
        return moved_ref[c, :wide], own_ref[c], moved_ref[c, 16 : wide + 16]

    def second_taps(c):
        return tuple(hidden_ref[c, 16 * b : 16 * b + breadth] for b in range(3))

    def keep_hidden(bases, out):
        for n, base in enumerate(bases):
            for half in range(2):
                c = base + half
                value = own_ref[c + 1].astype(jnp.float32) + relu(out[n][half])
                for edge, flags in ((c < 2, above), (c >= hidden_couples - 2, below)):
                    if edge:
                        value = value * jnp.concatenate([flags] * (tiles - 2), axis=0)
                value = jnp.concatenate(
                    [value[:16] * left, value[16 : wide - 16], value[wide - 16 :] * right], axis=0
                )
                hidden_ref[c] = value.astype(jnp.bfloat16)

    def keep_last(base, out):
        for half in range(2):
            own = hidden_ref[base + 2 * half + 2, 16 : 16 + breadth].astype(jnp.float32)
            last_ref[base // 4 * 2 + base % 4, :, half * channels : (half + 1) * channels] = (
                own + relu(out[half])
            ).astype(jnp.bfloat16)

    first_groups, second_groups = hidden_couples // 4, size // 8
    for c in range(8):
        build(c)
    for s in range(first_groups + 1):
        later = list(range(4 * (s + 2), min(4 * (s + 3), couples)))
        for part in range(2):
            one = seconds = None
            first_base, second_base = 4 * s + 2 * part, 4 * (s - 2) + part
            if s < first_groups:
                one = paired(first_taps, (first_base,), 1, pairs_one_ref)
            for c in later[2 * part : 2 * part + 2]:
                build(c)
            if 0 <= s - 2 < second_groups:
                seconds = paired(second_taps, (second_base,), 2, pairs_two_ref)
            if one is not None:
                keep_hidden((first_base,), one)
            if seconds:
                keep_last(second_base, seconds[0])
    every_last = jnp.concatenate([last_ref[n] for n in range(size // 4)], axis=1)
    by_couple = jnp.dot(every_last, head_ref[...], preferred_element_type=jnp.float32)
    mixed = by_couple.T[: size // 2]
    source = lax.broadcasted_iota(jnp.int32, (breadth, breadth), 0)
    place = ((source >> 3) & 1) * (2 * size) + ((source >> 1) & 1) * size
    place = place + 4 * (source >> 4) + 2 * ((source >> 2) & 1) + (source & 1)
    order = (place == lax.broadcasted_iota(jnp.int32, (breadth, breadth), 1)).astype(jnp.float32)
    order = order.astype(jnp.bfloat16)
    rest, ordered = mixed, None
    for _ in range(3):
        piece = rest.astype(jnp.bfloat16)
        rest = rest - piece.astype(jnp.float32)
        moved = jnp.dot(piece, order, preferred_element_type=jnp.float32)
        ordered = moved if ordered is None else ordered + moved
    for row in range(2):
        score_ref[pl.ds(row, size // 2, 2)] = ordered[:, row * 2 * size : (row + 1) * 2 * size]
    score = score_ref[...]
    turned = score.T
    first, second = score[:, :size], score[:, size:]
    turned_first, turned_second = turned[:size], turned[size:]
    alone = diagonal == 1
    kept_ref[...] = 0.5 * (first + jnp.where(alone, turned_first, turned_second))
    sent_ref[...] = 0.5 * (second + jnp.where(alone, turned_second, turned_first))


def block_scores(every, dist_table, first_kernel, second_kernel, head, size, table):
    map_bins = every.shape[0]
    channels = dist_table.shape[2]
    tiles = tiles_of(size)
    pair_rows = size + 2 * MARGIN
    vmem = pl.BlockSpec(memory_space=pltpu.VMEM)
    block = jax.ShapeDtypeStruct((size, size), jnp.float32)
    return pl.pallas_call(
        functools.partial(map_kernel, map_bins, size, table),
        out_shape=(block, block),
        in_specs=[vmem] * 5,
        out_specs=(vmem, vmem),
        scratch_shapes=[
            pltpu.VMEM((8 * pair_rows, channels), jnp.float32),
            pltpu.VMEM((8 * tiles, channels), jnp.float32),
            pltpu.VMEM((pair_rows // 2, 16 * (tiles - 2), channels), jnp.bfloat16),
            pltpu.VMEM((pair_rows // 2, 16 * (tiles - 1), channels), jnp.bfloat16),
            pltpu.VMEM((size // 2 + SECOND_SPACING, 16 * (tiles - 2), channels), jnp.bfloat16),
            pltpu.VMEM((12 * channels, 2 * channels), jnp.bfloat16),
            pltpu.VMEM((12 * channels, 2 * channels), jnp.bfloat16),
            pltpu.VMEM((size // 4, 4 * size, 2 * channels), jnp.bfloat16),
            pltpu.VMEM((size, 2 * size), jnp.float32),
        ],
        compiler_params=pltpu.CompilerParams(vmem_limit_bytes=40 * 1024 * 1024),
    )(
        every,
        dist_table,
        first_kernel.reshape(9 * channels, channels),
        second_kernel.reshape(9 * channels, channels),
        head,
    )


def on_device(
    embedding,
    bases_table,
    edit_pos,
    edit_tok,
    w_row,
    w_col,
    dist_gain,
    first_kernel,
    second_kernel,
    head_weight,
):
    n_rows, n_cols = lax.axis_size("row"), lax.axis_size("col")
    devices = n_rows * n_cols
    map_bins = embedding.shape[0] * devices // POOL
    table, target = plan(n_rows, n_cols)
    size = map_bins // max(n_rows, n_cols)
    copies, dist_table, head = projected(
        embedding, bases_table, edit_pos, edit_tok, w_row, w_col, dist_gain, head_weight, map_bins, devices, size, table
    )
    got = lax.all_to_all(copies, ("row", "col"), 0, 0)
    every = got.reshape(map_bins, got.shape[2])
    kept, sent = block_scores(every, dist_table, first_kernel, second_kernel, head, size, table)
    received = lax.ppermute(sent, ("row", "col"), [(device, target[device]) for device in range(devices)])
    place = lookup(table)[5]
    axis = 1 if n_rows > n_cols else 0
    return jnp.where(
        place == 0,
        jnp.concatenate([kept, received], axis=axis),
        jnp.concatenate([received, kept], axis=axis),
    )


def solution(mesh):
    placed = (P(("row", "col"), None), P(), P("cand"), P("cand"), P(), P(), P(), P(), P(), P())
    return jax.shard_map(
        on_device, mesh=mesh, in_specs=placed, out_specs=P(("cand", "row"), "col"), check_vma=False
    )
```

```python
import functools
import math

import jax
import jax.numpy as jnp
from jax import lax
from jax.experimental import pallas as pl
from jax.experimental.pallas import tpu as pltpu
from jax.sharding import PartitionSpec as P

POOL = 4
FIRST_SPACING = 2
SECOND_SPACING = 4
BASES = 4
MARGIN = FIRST_SPACING + SECOND_SPACING
PAD = 8
GROUP = 8
OUTSIDE = -1e30


def plan(n_rows, n_cols):
    wide = n_rows > n_cols
    blocks = max(n_rows, n_cols)
    assert blocks == 2 * min(n_rows, n_cols)

    def owner(i, j):
        return i * n_cols + j // 2 if wide else (i // 2) * n_cols + j

    held = {}
    for i in range(blocks):
        for j in range(blocks):
            held.setdefault(owner(i, j), []).append((i, j))

    def other(device, block):
        return next(b for b in held[device] if b != block)

    jobs, target = {}, {}

    def assign(device, kept, sent):
        place = held[device].index(kept)
        jobs[device] = (*kept, *sent, int(kept[0] == kept[1]), place)
        target[device] = owner(*sent)

    def walk(device, block):
        while device not in jobs:
            if block[0] == block[1]:
                return device, block
            sent = (block[1], block[0])
            assign(device, block, sent)
            device = owner(*sent)
            block = other(device, sent)
        return None, None

    for d in range(blocks):
        start = owner(d, d)
        if start not in jobs:
            end, last = walk(start, other(start, (d, d)))
            assign(end, last, (d, d))
    for device in sorted(held):
        if device not in jobs:
            walk(device, held[device][0])
    return [jobs[device] for device in sorted(jobs)], target


def tiles_of(size):
    return (size + 2 * PAD) // 4


def relu(x):
    return jnp.maximum(x, 0.0)


def lookup(table):
    n_cols = lax.axis_size("col")
    here = lax.axis_index("row") * n_cols + lax.axis_index("col")
    found = []
    for values in zip(*table):
        value = jnp.int32(values[0])
        for device in range(1, len(values)):
            value = jnp.where(here == device, jnp.int32(values[device]), value)
        found.append(value)
    return found


def project_kernel(
    map_bins, size, table, embedding_hbm, bases_hbm, pos_hbm, tok_hbm, w_row_hbm, w_col_hbm, gain_hbm, head_hbm,
    copies_ref, dist_ref, head_ref,
    embedding_ref, bases_ref, pos_ref, tok_ref, w_row_ref, w_col_ref, gain_ref, weight_ref, arrived,
):
    moves = [
        pltpu.make_async_copy(source, target, arrived.at[n])
        for n, (source, target) in enumerate(
            (
                (embedding_hbm, embedding_ref),
                (w_row_hbm, w_row_ref),
                (w_col_hbm, w_col_ref),
                (pos_hbm, pos_ref),
                (tok_hbm, tok_ref),
                (bases_hbm, bases_ref),
                (gain_hbm, gain_ref),
                (head_hbm, weight_ref),
            )
        )
    ]
    for move in moves:
        move.start()
    got_embedding, got_w_row, got_w_col, *small = moves
    shard_bins = embedding_ref.shape[0]
    copies, pooled_bins, _ = copies_ref.shape
    channels = gain_ref.shape[1]
    edits = pos_ref.shape[1]
    row_a, col_a, row_b, col_b, _, _ = lookup(table)
    phases, count, _ = dist_ref.shape
    at = lax.broadcasted_iota(jnp.int32, (count, channels), 0)
    lane = at & 7
    start = jnp.where((lane & 2) == 0, (col_a - row_a) * size, (col_b - row_b) * size)
    start = start + 4 * (at >> 3) + 2 * (lane >> 2) + (lane & 1) - 2 - 4 * ((size + 2 * MARGIN) // 4 - 1)
    feature = [
        jnp.log1p(jnp.abs(start - phase).astype(jnp.float32)) * (1.0 / math.log(map_bins))
        for phase in range(phases)
    ]
    first_bin = (lax.axis_index("row") * lax.axis_size("col") + lax.axis_index("col")) * shard_bins
    bins = first_bin + lax.broadcasted_iota(jnp.int32, (pooled_bins, edits), 0) * POOL
    back = lax.broadcasted_iota(jnp.int32, (pooled_bins, shard_bins), 1) - POOL * (
        lax.broadcasted_iota(jnp.int32, (pooled_bins, shard_bins), 0)
    )
    take = ((back >= 0) & (back < POOL)).astype(jnp.float32).astype(jnp.bfloat16)
    for move in small:
        move.wait()
    for phase in range(phases):
        dist_ref[phase] = gain_ref[...] * feature[phase]
    weight = jnp.concatenate([weight_ref[...].astype(jnp.float32)] * 2, axis=1)
    line = lax.broadcasted_iota(jnp.int32, head_ref.shape, 0)
    half = lax.broadcasted_iota(jnp.int32, head_ref.shape, 1) >= channels
    head_ref[...] = jnp.where(line == half.astype(jnp.int32), weight, 0.0).astype(jnp.bfloat16)
    ahead = pos_ref[...] - bins
    in_bin = ((ahead >= 0) & (ahead < POOL)).astype(jnp.float32)
    edited = None
    for base in range(BASES):
        is_base = (tok_ref[...] == base).astype(jnp.float32)
        count = jnp.sum(in_bin * is_base, axis=1, keepdims=True)
        term = count * bases_ref[base : base + 1].astype(jnp.float32)
        edited = term if edited is None else edited + term
    got_embedding.wait()
    summed = edited + jnp.dot(take, embedding_ref[...], preferred_element_type=jnp.float32)
    pooled = (summed * (1.0 / POOL)).astype(jnp.bfloat16)
    sides = []
    for move, ref in ((got_w_row, w_row_ref), (got_w_col, w_col_ref)):
        move.wait()
        sides.append(jnp.dot(pooled, ref[...], preferred_element_type=jnp.float32).astype(jnp.bfloat16))
    both = jnp.concatenate(sides, axis=1)
    for k in range(copies):
        copies_ref[k] = both


def projected(embedding, bases_table, edit_pos, edit_tok, w_row, w_col, dist_gain, head_weight, map_bins, copies, size, table):
    vmem = pl.BlockSpec(memory_space=pltpu.VMEM)
    operands = (
        embedding,
        bases_table,
        edit_pos[None],
        edit_tok[None],
        w_row,
        w_col,
        dist_gain[None],
        head_weight[None],
    )
    channels = w_row.shape[1]
    return pl.pallas_call(
        functools.partial(project_kernel, map_bins, size, table),
        out_shape=(
            jax.ShapeDtypeStruct((copies, embedding.shape[0] // POOL, 2 * channels), jnp.bfloat16),
            jax.ShapeDtypeStruct((4, 8 * (tiles_of(size) + (size + 2 * MARGIN) // 4 - 1), channels), jnp.float32),
            jax.ShapeDtypeStruct((16, 2 * channels), jnp.bfloat16),
        ),
        in_specs=[pl.BlockSpec(memory_space=pltpu.HBM)] * 8,
        out_specs=(vmem, vmem, vmem),
        scratch_shapes=[pltpu.VMEM(x.shape, x.dtype) for x in operands] + [pltpu.SemaphoreType.DMA((8,))],
        compiler_params=pltpu.CompilerParams(vmem_limit_bytes=16 * 1024 * 1024),
    )(*(pltpu.with_memory_space_constraint(x, pltpu.HBM) for x in operands))


def map_kernel(
    map_bins, size, table, proj_ref, dist_ref, first_ref, second_ref, head_ref,
    kept_ref, sent_ref, row_ref, col_ref, own_ref, moved_ref, hidden_ref, pairs_one_ref, pairs_two_ref,
    last_ref, mixed_ref, score_ref,
):
    channels = head_ref.shape[1] // 2
    tiles = tiles_of(size)
    wide = 16 * (tiles - 2)
    breadth = 4 * size
    pair_rows = size + 2 * MARGIN
    couples = pair_rows // 2
    hidden_couples = size // 2 + SECOND_SPACING
    depth = 3 * channels
    row_a, col_a, row_b, col_b, diagonal, _ = lookup(table)
    rows, cols = (row_a * size, row_b * size), (col_a * size, col_b * size)
    def place_weights(ref, given):
        ref[3 * depth :, :channels] = jnp.zeros((depth, channels), jnp.bfloat16)
        ref[:depth, channels:] = jnp.zeros((depth, channels), jnp.bfloat16)
        ref[: 3 * depth, :channels] = given[...]
        ref[depth:, channels:] = given[...]

    place_weights(pairs_one_ref, first_ref)

    def of_block(lane, values):
        return jnp.where((lane & 2) == 0, values[0], values[1])

    def spread(ref, part, offset, along):
        count = ref.shape[0]
        at = lax.broadcasted_iota(jnp.int32, (count, map_bins), 0)
        lane = at & 7
        bins = along(at >> 3, lane) + of_block(lane, offset)
        hot = (bins == lax.broadcasted_iota(jnp.int32, (count, map_bins), 1)).astype(jnp.float32)
        found = jnp.dot(
            hot.astype(jnp.bfloat16),
            proj_ref[:, part * channels : (part + 1) * channels],
            preferred_element_type=jnp.float32,
        )
        bins = bins[:, :channels]
        ref[...] = jnp.where((bins >= 0) & (bins < map_bins), found, OUTSIDE)

    spread(col_ref, 1, cols, lambda tile, lane: 4 * tile + 2 * (lane >> 2) + (lane & 1) - PAD)
    spread(row_ref, 0, rows, lambda row, lane: row - MARGIN)
    lane = lax.broadcasted_iota(jnp.int32, (16, channels), 0) & 7
    last_start = map_bins - size
    left = of_block(lane, [jnp.where(col > 0, 1.0, 0.0) for col in cols])
    right = of_block(lane, [jnp.where(col < last_start, 1.0, 0.0) for col in cols])
    above = of_block(lane, [jnp.where(row > 0, 1.0, 0.0) for row in rows])
    below = of_block(lane, [jnp.where(row < last_start, 1.0, 0.0) for row in rows])

    def couple(two):
        parts = [x.reshape(-1, 1, 8, channels) for x in two]
        return jnp.concatenate(parts, axis=1).reshape(-1, channels).astype(jnp.bfloat16)

    def build(c):
        values, ahead = [], []
        for p in (2 * c, 2 * c + 1):
            at = 8 * (pair_rows // 4 - 1 - p // 4)
            apart = dist_ref[p % 4, at : at + 8 * tiles]
            line = jnp.concatenate([row_ref[8 * p : 8 * p + 8]] * tiles, axis=0)
            value = relu(col_ref[...] + apart + line)
            values.append(value[8 : 8 * (tiles - 1)])
            ahead.append(pltpu.roll(value, 8 * tiles - 4, 0)[: 8 * (tiles - 1)])
        own_ref[c] = couple(values)
        moved_ref[c] = couple(ahead)

    def paired(taps, bases, step, weight):
        lhs = [
            jnp.concatenate([tap for k in range(4) for tap in taps(base + k * step)], axis=1) for base in bases
        ]
        lhs = lhs[0] if len(lhs) == 1 else jnp.concatenate(lhs, axis=0)
        out = jnp.dot(lhs, weight[...], preferred_element_type=jnp.float32)
        tall = out.shape[0] // len(bases)
        return [
            [out[n * tall : (n + 1) * tall, half * channels : (half + 1) * channels] for half in range(2)]
            for n in range(len(bases))
        ]

    def first_taps(c):
        return moved_ref[c, :wide], own_ref[c], moved_ref[c, 16 : wide + 16]

    def second_taps(c):
        return tuple(hidden_ref[c, 16 * b : 16 * b + breadth] for b in range(3))

    def keep_hidden(bases, out):
        for n, base in enumerate(bases):
            for half in range(2):
                c = base + half
                value = own_ref[c + 1].astype(jnp.float32) + relu(out[n][half])
                for edge, flags in ((c < 2, above), (c >= hidden_couples - 2, below)):
                    if edge:
                        value = value * jnp.concatenate([flags] * (tiles - 2), axis=0)
                value = jnp.concatenate(
                    [value[:16] * left, value[16 : wide - 16], value[wide - 16 :] * right], axis=0
                )
                hidden_ref[c] = value.astype(jnp.bfloat16)

    def keep_last(base, out):
        for half in range(2):
            own = hidden_ref[base + 2 * half + 2, 16 : 16 + breadth].astype(jnp.float32)
            last_ref[base // 4 * 2 + base % 4, :, half * channels : (half + 1) * channels] = (
                own + relu(out[half])
            ).astype(jnp.bfloat16)

    def keep_scores(start, count):
        got = lax.dot_general(
            head_ref[...],
            last_ref[start : start + count].reshape(count * breadth, 2 * channels),
            (((1,), (1,)), ((), ())),
            preferred_element_type=jnp.float32,
        )
        lines = [
            got[half : half + 1, n * breadth : (n + 1) * breadth]
            for pair in range(0, count, 2)
            for half in range(2)
            for n in (pair, pair + 1)
        ]
        mixed_ref[2 * start : 2 * (start + count)] = jnp.concatenate(lines, axis=0)

    first_groups, second_groups = hidden_couples // 4, size // 8
    for c in range(4):
        build(c)
    for s in range(first_groups + 1):
        later = list(range(4 * (s + 2), min(4 * (s + 3), couples)))
        for part in range(2):
            one = seconds = None
            first_base, second_base = 4 * s + 2 * part, 4 * (s - 2) + part
            if s < first_groups:
                one = paired(first_taps, (first_base,), 1, pairs_one_ref)
            if first_base == 0:
                for c in range(4, 8):
                    build(c)
                place_weights(pairs_two_ref, second_ref)
            for c in later[2 * part : 2 * part + 2]:
                build(c)
            if 0 <= s - 2 < second_groups:
                seconds = paired(second_taps, (second_base,), 2, pairs_two_ref)
            if one is not None:
                keep_hidden((first_base,), one)
            if seconds:
                keep_last(second_base, seconds[0])
    for start in range(0, size // 4, 4):
        keep_scores(start, 4)
    source = lax.broadcasted_iota(jnp.int32, (breadth, breadth), 0)
    place = ((source >> 3) & 1) * (2 * size) + ((source >> 1) & 1) * size
    place = place + 4 * (source >> 4) + 2 * ((source >> 2) & 1) + (source & 1)
    order = (place == lax.broadcasted_iota(jnp.int32, (breadth, breadth), 1)).astype(jnp.float32)
    order = order.astype(jnp.bfloat16)
    rest, ordered = mixed_ref[...], None
    for _ in range(3):
        piece = rest.astype(jnp.bfloat16)
        rest = rest - piece.astype(jnp.float32)
        moved = jnp.dot(piece, order, preferred_element_type=jnp.float32)
        ordered = moved if ordered is None else ordered + moved
    for row in range(2):
        score_ref[pl.ds(row, size // 2, 2)] = ordered[:, row * 2 * size : (row + 1) * 2 * size]
    score = score_ref[...]
    turned = score.T
    first, second = score[:, :size], score[:, size:]
    turned_first, turned_second = turned[:size], turned[size:]
    alone = diagonal == 1
    kept_ref[...] = 0.5 * (first + jnp.where(alone, turned_first, turned_second))
    sent_ref[...] = 0.5 * (second + jnp.where(alone, turned_second, turned_first))


def block_scores(every, dist_table, first_kernel, second_kernel, head, size, table):
    map_bins = every.shape[0]
    channels = dist_table.shape[2]
    tiles = tiles_of(size)
    pair_rows = size + 2 * MARGIN
    vmem = pl.BlockSpec(memory_space=pltpu.VMEM)
    block = jax.ShapeDtypeStruct((size, size), jnp.float32)
    return pl.pallas_call(
        functools.partial(map_kernel, map_bins, size, table),
        out_shape=(block, block),
        in_specs=[vmem] * 5,
        out_specs=(vmem, vmem),
        scratch_shapes=[
            pltpu.VMEM((8 * pair_rows, channels), jnp.float32),
            pltpu.VMEM((8 * tiles, channels), jnp.float32),
            pltpu.VMEM((pair_rows // 2, 16 * (tiles - 2), channels), jnp.bfloat16),
            pltpu.VMEM((pair_rows // 2, 16 * (tiles - 1), channels), jnp.bfloat16),
            pltpu.VMEM((size // 2 + SECOND_SPACING, 16 * (tiles - 2), channels), jnp.bfloat16),
            pltpu.VMEM((12 * channels, 2 * channels), jnp.bfloat16),
            pltpu.VMEM((12 * channels, 2 * channels), jnp.bfloat16),
            pltpu.VMEM((size // 4, 4 * size, 2 * channels), jnp.bfloat16),
            pltpu.VMEM((size // 2, 4 * size), jnp.float32),
            pltpu.VMEM((size, 2 * size), jnp.float32),
        ],
        compiler_params=pltpu.CompilerParams(vmem_limit_bytes=40 * 1024 * 1024),
    )(
        every,
        dist_table,
        first_kernel.reshape(9 * channels, channels),
        second_kernel.reshape(9 * channels, channels),
        head,
    )


def on_device(
    embedding,
    bases_table,
    edit_pos,
    edit_tok,
    w_row,
    w_col,
    dist_gain,
    first_kernel,
    second_kernel,
    head_weight,
):
    n_rows, n_cols = lax.axis_size("row"), lax.axis_size("col")
    devices = n_rows * n_cols
    map_bins = embedding.shape[0] * devices // POOL
    table, target = plan(n_rows, n_cols)
    size = map_bins // max(n_rows, n_cols)
    copies, dist_table, head = projected(
        embedding, bases_table, edit_pos, edit_tok, w_row, w_col, dist_gain, head_weight, map_bins, devices, size, table
    )
    got = lax.all_to_all(copies, ("row", "col"), 0, 0)
    every = got.reshape(map_bins, got.shape[2])
    kept, sent = block_scores(every, dist_table, first_kernel, second_kernel, head, size, table)
    received = lax.ppermute(sent, ("row", "col"), [(device, target[device]) for device in range(devices)])
    place = lookup(table)[5]
    axis = 1 if n_rows > n_cols else 0
    return jnp.where(
        place == 0,
        jnp.concatenate([kept, received], axis=axis),
        jnp.concatenate([received, kept], axis=axis),
    )


def solution(mesh):
    placed = (P(("row", "col"), None), P(), P("cand"), P("cand"), P(), P(), P(), P(), P(), P())
    return jax.shard_map(
        on_device, mesh=mesh, in_specs=placed, out_specs=P(("cand", "row"), "col"), check_vma=False
    )
```

```python
import functools
import math

import jax
import jax.numpy as jnp
from jax import lax
from jax.experimental import pallas as pl
from jax.experimental.pallas import tpu as pltpu
from jax.sharding import PartitionSpec as P

POOL = 4
FIRST_SPACING = 2
SECOND_SPACING = 4
BASES = 4
MARGIN = FIRST_SPACING + SECOND_SPACING
PAD = 8
GROUP = 8
OUTSIDE = -1e30


def plan(n_rows, n_cols):
    wide = n_rows > n_cols
    blocks = max(n_rows, n_cols)
    assert blocks == 2 * min(n_rows, n_cols)

    def owner(i, j):
        return i * n_cols + j // 2 if wide else (i // 2) * n_cols + j

    held = {}
    for i in range(blocks):
        for j in range(blocks):
            held.setdefault(owner(i, j), []).append((i, j))

    def other(device, block):
        return next(b for b in held[device] if b != block)

    jobs, target = {}, {}

    def assign(device, kept, sent):
        place = held[device].index(kept)
        jobs[device] = (*kept, *sent, int(kept[0] == kept[1]), place)
        target[device] = owner(*sent)

    def walk(device, block):
        while device not in jobs:
            if block[0] == block[1]:
                return device, block
            sent = (block[1], block[0])
            assign(device, block, sent)
            device = owner(*sent)
            block = other(device, sent)
        return None, None

    for d in range(blocks):
        start = owner(d, d)
        if start not in jobs:
            end, last = walk(start, other(start, (d, d)))
            assign(end, last, (d, d))
    for device in sorted(held):
        if device not in jobs:
            walk(device, held[device][0])
    return [jobs[device] for device in sorted(jobs)], target


def relu(x):
    return jnp.maximum(x, 0.0)


def lookup(table):
    n_cols = lax.axis_size("col")
    here = lax.axis_index("row") * n_cols + lax.axis_index("col")
    found = []
    for values in zip(*table):
        value = jnp.int32(values[0])
        for device in range(1, len(values)):
            value = jnp.where(here == device, jnp.int32(values[device]), value)
        found.append(value)
    return found


def project_kernel(
    map_bins, embedding_hbm, bases_hbm, pos_hbm, tok_hbm, w_row_hbm, w_col_hbm, gain_hbm, head_hbm,
    copies_ref, dist_ref, head_ref,
    embedding_ref, bases_ref, pos_ref, tok_ref, w_row_ref, w_col_ref, gain_ref, weight_ref, arrived,
):
    moves = [
        pltpu.make_async_copy(source, target, arrived.at[n])
        for n, (source, target) in enumerate(
            (
                (embedding_hbm, embedding_ref),
                (w_row_hbm, w_row_ref),
                (w_col_hbm, w_col_ref),
                (pos_hbm, pos_ref),
                (tok_hbm, tok_ref),
                (bases_hbm, bases_ref),
                (gain_hbm, gain_ref),
                (head_hbm, weight_ref),
            )
        )
    ]
    for move in moves:
        move.start()
    got_embedding, got_w_row, got_w_col, *small = moves
    shard_bins = embedding_ref.shape[0]
    copies, pooled_bins, _ = copies_ref.shape
    channels = gain_ref.shape[1]
    edits = pos_ref.shape[1]
    span = dist_ref.shape[0]
    apart = jnp.abs(lax.broadcasted_iota(jnp.int32, (span, channels), 0) - span // 2)
    feature = jnp.log1p(apart.astype(jnp.float32)) * (1.0 / math.log(map_bins))
    first_bin = (lax.axis_index("row") * lax.axis_size("col") + lax.axis_index("col")) * shard_bins
    bins = first_bin + lax.broadcasted_iota(jnp.int32, (pooled_bins, edits), 0) * POOL
    back = lax.broadcasted_iota(jnp.int32, (pooled_bins, shard_bins), 1) - POOL * (
        lax.broadcasted_iota(jnp.int32, (pooled_bins, shard_bins), 0)
    )
    take = ((back >= 0) & (back < POOL)).astype(jnp.float32).astype(jnp.bfloat16)
    for move in small:
        move.wait()
    dist_ref[...] = gain_ref[...] * feature
    weight = jnp.concatenate([weight_ref[...].astype(jnp.float32)] * 2, axis=1)
    line = lax.broadcasted_iota(jnp.int32, head_ref.shape, 0)
    half = lax.broadcasted_iota(jnp.int32, head_ref.shape, 1) >= channels
    head_ref[...] = jnp.where(line == half.astype(jnp.int32), weight, 0.0).astype(jnp.bfloat16)
    ahead = pos_ref[...] - bins
    in_bin = ((ahead >= 0) & (ahead < POOL)).astype(jnp.float32)
    edited = None
    for base in range(BASES):
        is_base = (tok_ref[...] == base).astype(jnp.float32)
        count = jnp.sum(in_bin * is_base, axis=1, keepdims=True)
        term = count * bases_ref[base : base + 1].astype(jnp.float32)
        edited = term if edited is None else edited + term
    got_embedding.wait()
    summed = edited + jnp.dot(take, embedding_ref[...], preferred_element_type=jnp.float32)
    pooled = (summed * (1.0 / POOL)).astype(jnp.bfloat16)
    sides = []
    for move, ref in ((got_w_row, w_row_ref), (got_w_col, w_col_ref)):
        move.wait()
        sides.append(jnp.dot(pooled, ref[...], preferred_element_type=jnp.float32).astype(jnp.bfloat16))
    both = jnp.concatenate(sides, axis=1)
    for k in range(copies):
        copies_ref[k] = both


def projected(embedding, bases_table, edit_pos, edit_tok, w_row, w_col, dist_gain, head_weight, map_bins, copies):
    vmem = pl.BlockSpec(memory_space=pltpu.VMEM)
    operands = (
        embedding,
        bases_table,
        edit_pos[None],
        edit_tok[None],
        w_row,
        w_col,
        dist_gain[None],
        head_weight[None],
    )
    channels = w_row.shape[1]
    return pl.pallas_call(
        functools.partial(project_kernel, map_bins),
        out_shape=(
            jax.ShapeDtypeStruct((copies, embedding.shape[0] // POOL, 2 * channels), jnp.bfloat16),
            jax.ShapeDtypeStruct((2 * map_bins + 4 * PAD, channels), jnp.float32),
            jax.ShapeDtypeStruct((16, 2 * channels), jnp.bfloat16),
        ),
        in_specs=[pl.BlockSpec(memory_space=pltpu.HBM)] * 8,
        out_specs=(vmem, vmem, vmem),
        scratch_shapes=[pltpu.VMEM(x.shape, x.dtype) for x in operands] + [pltpu.SemaphoreType.DMA((8,))],
        compiler_params=pltpu.CompilerParams(vmem_limit_bytes=16 * 1024 * 1024),
    )(*(pltpu.with_memory_space_constraint(x, pltpu.HBM) for x in operands))


def map_kernel(
    map_bins, size, table, proj_ref, dist_table_ref, first_ref, second_ref, head_ref,
    kept_ref, sent_ref, row_ref, col_ref, pair_ref, hidden_ref, pairs_one_ref, pairs_two_ref, score_ref,
):
    channels = dist_table_ref.shape[1]
    block_wide = size + 2 * SECOND_SPACING
    wide = 2 * block_wide
    spread = block_wide + PAD
    breadth = 2 * size
    pair_rows = size + 2 * MARGIN
    hidden_rows = size + 2 * SECOND_SPACING
    depth = 3 * channels
    edge = SECOND_SPACING
    row_a, col_a, row_b, col_b, diagonal, _ = lookup(table)
    blocks = [
        (pl.multiple_of(row_a * size, size), pl.multiple_of(col_a * size, size)),
        (pl.multiple_of(row_b * size, size), pl.multiple_of(col_b * size, size)),
    ]
    outside = jnp.full((2 * PAD, channels), OUTSIDE, jnp.float32)
    for part, ref in enumerate((row_ref, col_ref)):
        ref[:PAD] = outside[:PAD]
        ref[PAD + map_bins :] = outside
        ref[PAD : PAD + map_bins] = proj_ref[:, part * channels : (part + 1) * channels].astype(
            jnp.float32
        )
    for ref, given in ((pairs_one_ref, first_ref), (pairs_two_ref, second_ref)):
        ref[: 3 * depth, :channels] = given[...]
        ref[3 * depth :, :channels] = jnp.zeros((depth, channels), jnp.bfloat16)
        ref[:depth, channels:] = jnp.zeros((depth, channels), jnp.bfloat16)
        ref[depth:, channels:] = given[...]
    zero_apart = dist_table_ref.shape[0] // 2
    at_edge = lax.broadcasted_iota(jnp.int32, (PAD, channels), 0)
    last_start = map_bins - size
    left = [jnp.where((at_edge >= edge) | (col > 0), 1.0, 0.0) for _, col in blocks]
    right = [jnp.where((at_edge < PAD - edge) | (col < last_start), 1.0, 0.0) for _, col in blocks]
    above = [jnp.where(row > 0, 1.0, 0.0) for row, _ in blocks]
    below = [jnp.where(row < last_start, 1.0, 0.0) for row, _ in blocks]

    def build(p):
        values = []
        for row, col in blocks:
            row_part = row_ref[pl.ds(row + (PAD - MARGIN + p), 1)]
            apart = dist_table_ref[pl.ds(col - row + (zero_apart - p), spread)]
            values.append(relu(col_ref[pl.ds(col + (PAD - MARGIN), spread)] + apart + row_part))
        taps = []
        for b in range(3):
            moved = [
                (pltpu.roll(x, spread - b * FIRST_SPACING, 0) if b else x)[:block_wide] for x in values
            ]
            taps.append(jnp.concatenate(moved, axis=0).astype(jnp.bfloat16))
        pair_ref[p] = jnp.concatenate(taps, axis=1)

    def paired(ref, start, offsets, spacing, weight):
        lhs = jnp.concatenate(
            [
                jnp.concatenate([ref[start + base + k * spacing] for k in range(4)], axis=1)
                for base in offsets
            ],
            axis=0,
        )
        return jnp.dot(lhs, weight[...], preferred_element_type=jnp.float32)

    def keep_hidden(start, offsets, out):
        for n, base in enumerate(offsets):
            for half in range(2):
                a = start + base + half * FIRST_SPACING
                conv = out[n * wide : (n + 1) * wide, half * channels : (half + 1) * channels]
                own = pair_ref[a + FIRST_SPACING, :, channels : 2 * channels].astype(jnp.float32)
                value = own + relu(conv)
                for rows, flags in ((a < edge, above), (a >= hidden_rows - edge, below)):
                    if rows:
                        value = jnp.concatenate(
                            [value[:block_wide] * flags[0], value[block_wide:] * flags[1]], axis=0
                        )
                ahead = pltpu.roll(value, wide - edge, 0)
                before, middle, after = [], [], []
                for b in range(2):
                    at = b * block_wide
                    before += [value[at : at + PAD] * left[b], value[at + PAD : at + size]]
                    middle += [ahead[at : at + size]]
                    after += [value[at + PAD : at + size], value[at + size : at + size + PAD] * right[b]]
                hidden_ref[a] = jnp.concatenate(
                    [jnp.concatenate(x, axis=0).astype(jnp.bfloat16) for x in (before, middle, after)], axis=1
                )

    def keep_score(start, offsets, out):
        last = []
        for n, base in enumerate(offsets):
            halves = []
            for half in range(2):
                o = start + base + half * edge
                conv = out[n // 2][n % 2 * breadth : (n % 2 + 1) * breadth, half * channels : (half + 1) * channels]
                own = hidden_ref[o + edge, :, channels : 2 * channels].astype(jnp.float32)
                halves.append((own + relu(conv)).astype(jnp.bfloat16))
            last.append(jnp.concatenate(halves, axis=1))
        got = lax.dot_general(
            head_ref[...],
            jnp.concatenate(last, axis=0),
            (((1,), (1,)), ((), ())),
            preferred_element_type=jnp.float32,
        )
        count = len(offsets)
        lines = [got[half : half + 1, n * breadth : (n + 1) * breadth] for half in range(2) for n in range(count)]
        score_ref[start : start + 8] = jnp.concatenate(lines, axis=0)

    first_offsets, second_offsets = (0, 1, 4, 5), (0, 1, 2, 3)
    first_groups, second_groups = hidden_rows // GROUP, size // GROUP
    for p in range(2 * GROUP):
        build(p)
    for s in range(first_groups + 1):
        later = list(range((s + 2) * GROUP, min((s + 3) * GROUP, pair_rows)))
        two = []
        for part in range(2):
            one = None
            some = first_offsets[2 * part : 2 * part + 2]
            if s < first_groups:
                one = paired(pair_ref, s * GROUP, some, FIRST_SPACING, pairs_one_ref)
            for p in later[4 * part : 4 * part + 4]:
                build(p)
            if 0 <= s - 2 < second_groups:
                start, offsets = (s - 2) * GROUP, second_offsets[2 * part : 2 * part + 2]
                two.append(paired(hidden_ref, start, offsets, SECOND_SPACING, pairs_two_ref))
            if one is not None:
                keep_hidden(s * GROUP, some, one)
        if two:
            keep_score((s - 2) * GROUP, second_offsets, two)
    score = score_ref[...]
    turned = score.T
    first, second = score[:, :size], score[:, size:]
    turned_first, turned_second = turned[:size], turned[size:]
    alone = diagonal == 1
    kept_ref[...] = 0.5 * (first + jnp.where(alone, turned_first, turned_second))
    sent_ref[...] = 0.5 * (second + jnp.where(alone, turned_second, turned_first))


def block_scores(every, dist_table, first_kernel, second_kernel, head, size, table):
    map_bins = every.shape[0]
    channels = dist_table.shape[1]
    wide = 2 * (size + 2 * SECOND_SPACING)
    vmem = pl.BlockSpec(memory_space=pltpu.VMEM)
    block = jax.ShapeDtypeStruct((size, size), jnp.float32)
    return pl.pallas_call(
        functools.partial(map_kernel, map_bins, size, table),
        out_shape=(block, block),
        in_specs=[vmem] * 5,
        out_specs=(vmem, vmem),
        scratch_shapes=[
            pltpu.VMEM((map_bins + 3 * PAD, channels), jnp.float32),
            pltpu.VMEM((map_bins + 3 * PAD, channels), jnp.float32),
            pltpu.VMEM((size + 2 * MARGIN, wide, 3 * channels), jnp.bfloat16),
            pltpu.VMEM((size + 2 * SECOND_SPACING, 2 * size, 3 * channels), jnp.bfloat16),
            pltpu.VMEM((12 * channels, 2 * channels), jnp.bfloat16),
            pltpu.VMEM((12 * channels, 2 * channels), jnp.bfloat16),
            pltpu.VMEM((size, 2 * size), jnp.float32),
        ],
        compiler_params=pltpu.CompilerParams(vmem_limit_bytes=40 * 1024 * 1024),
    )(
        every,
        dist_table,
        first_kernel.reshape(9 * channels, channels),
        second_kernel.reshape(9 * channels, channels),
        head,
    )


def on_device(
    embedding,
    bases_table,
    edit_pos,
    edit_tok,
    w_row,
    w_col,
    dist_gain,
    first_kernel,
    second_kernel,
    head_weight,
):
    n_rows, n_cols = lax.axis_size("row"), lax.axis_size("col")
    devices = n_rows * n_cols
    map_bins = embedding.shape[0] * devices // POOL
    table, target = plan(n_rows, n_cols)
    size = map_bins // max(n_rows, n_cols)
    copies, dist_table, head = projected(
        embedding, bases_table, edit_pos, edit_tok, w_row, w_col, dist_gain, head_weight, map_bins, devices
    )
    got = lax.all_to_all(copies, ("row", "col"), 0, 0)
    every = got.reshape(map_bins, got.shape[2])
    kept, sent = block_scores(every, dist_table, first_kernel, second_kernel, head, size, table)
    received = lax.ppermute(sent, ("row", "col"), [(device, target[device]) for device in range(devices)])
    place = lookup(table)[5]
    axis = 1 if n_rows > n_cols else 0
    return jnp.where(
        place == 0,
        jnp.concatenate([kept, received], axis=axis),
        jnp.concatenate([received, kept], axis=axis),
    )


def solution(mesh):
    placed = (P(("row", "col"), None), P(), P("cand"), P("cand"), P(), P(), P(), P(), P(), P())
    return jax.shard_map(
        on_device, mesh=mesh, in_specs=placed, out_specs=P(("cand", "row"), "col"), check_vma=False
    )
```

```python
import functools
import math

import jax
import jax.numpy as jnp
from jax import lax
from jax.experimental import pallas as pl
from jax.experimental.pallas import tpu as pltpu
from jax.sharding import PartitionSpec as P

POOL = 4
FIRST_SPACING = 2
SECOND_SPACING = 4
BASES = 4
MARGIN = FIRST_SPACING + SECOND_SPACING
PAD = 8
GROUP = 8
OUTSIDE = -1e30


def plan(n_rows, n_cols):
    wide = n_rows > n_cols
    blocks = max(n_rows, n_cols)
    assert blocks == 2 * min(n_rows, n_cols)

    def owner(i, j):
        return i * n_cols + j // 2 if wide else (i // 2) * n_cols + j

    held = {}
    for i in range(blocks):
        for j in range(blocks):
            held.setdefault(owner(i, j), []).append((i, j))

    def other(device, block):
        return next(b for b in held[device] if b != block)

    jobs, target = {}, {}

    def assign(device, kept, sent):
        place = held[device].index(kept)
        jobs[device] = (*kept, *sent, int(kept[0] == kept[1]), place)
        target[device] = owner(*sent)

    def walk(device, block):
        while device not in jobs:
            if block[0] == block[1]:
                return device, block
            sent = (block[1], block[0])
            assign(device, block, sent)
            device = owner(*sent)
            block = other(device, sent)
        return None, None

    for d in range(blocks):
        start = owner(d, d)
        if start not in jobs:
            end, last = walk(start, other(start, (d, d)))
            assign(end, last, (d, d))
    for device in sorted(held):
        if device not in jobs:
            walk(device, held[device][0])
    return [jobs[device] for device in sorted(jobs)], target


def tiles_of(size):
    return (size + 2 * PAD) // 4


def relu(x):
    return jnp.maximum(x, 0.0)


def lookup(table):
    n_cols = lax.axis_size("col")
    here = lax.axis_index("row") * n_cols + lax.axis_index("col")
    found = []
    for values in zip(*table):
        value = jnp.int32(values[0])
        for device in range(1, len(values)):
            value = jnp.where(here == device, jnp.int32(values[device]), value)
        found.append(value)
    return found


def project_kernel(
    map_bins, size, table, embedding_hbm, bases_hbm, pos_hbm, tok_hbm, w_row_hbm, w_col_hbm, gain_hbm, head_hbm,
    copies_ref, dist_ref, head_ref,
    embedding_ref, bases_ref, pos_ref, tok_ref, w_row_ref, w_col_ref, gain_ref, weight_ref, arrived,
):
    moves = [
        pltpu.make_async_copy(source, target, arrived.at[n])
        for n, (source, target) in enumerate(
            (
                (embedding_hbm, embedding_ref),
                (w_row_hbm, w_row_ref),
                (w_col_hbm, w_col_ref),
                (pos_hbm, pos_ref),
                (tok_hbm, tok_ref),
                (bases_hbm, bases_ref),
                (gain_hbm, gain_ref),
                (head_hbm, weight_ref),
            )
        )
    ]
    for move in moves:
        move.start()
    got_embedding, got_w_row, got_w_col, *small = moves
    shard_bins = embedding_ref.shape[0]
    copies, pooled_bins, _ = copies_ref.shape
    channels = gain_ref.shape[1]
    edits = pos_ref.shape[1]
    row_a, col_a, row_b, col_b, _, _ = lookup(table)
    phases, count, _ = dist_ref.shape
    at = lax.broadcasted_iota(jnp.int32, (count, channels), 0)
    lane = at & 7
    start = jnp.where((lane & 2) == 0, (col_a - row_a) * size, (col_b - row_b) * size)
    start = start + 4 * (at >> 3) + 2 * (lane >> 2) + (lane & 1) - 2 - 4 * ((size + 2 * MARGIN) // 4 - 1)
    feature = [
        jnp.log1p(jnp.abs(start - phase).astype(jnp.float32)) * (1.0 / math.log(map_bins))
        for phase in range(phases)
    ]
    first_bin = (lax.axis_index("row") * lax.axis_size("col") + lax.axis_index("col")) * shard_bins
    bins = first_bin + lax.broadcasted_iota(jnp.int32, (pooled_bins, edits), 0) * POOL
    back = lax.broadcasted_iota(jnp.int32, (pooled_bins, shard_bins), 1) - POOL * (
        lax.broadcasted_iota(jnp.int32, (pooled_bins, shard_bins), 0)
    )
    take = ((back >= 0) & (back < POOL)).astype(jnp.float32).astype(jnp.bfloat16)
    for move in small:
        move.wait()
    for phase in range(phases):
        dist_ref[phase] = gain_ref[...] * feature[phase]
    weight = jnp.concatenate([weight_ref[...].astype(jnp.float32)] * 2, axis=1)
    line = lax.broadcasted_iota(jnp.int32, head_ref.shape, 0)
    half = lax.broadcasted_iota(jnp.int32, head_ref.shape, 1) >= channels
    head_ref[...] = jnp.where(line == half.astype(jnp.int32), weight, 0.0).astype(jnp.bfloat16)
    ahead = pos_ref[...] - bins
    in_bin = ((ahead >= 0) & (ahead < POOL)).astype(jnp.float32)
    edited = None
    for base in range(BASES):
        is_base = (tok_ref[...] == base).astype(jnp.float32)
        count = jnp.sum(in_bin * is_base, axis=1, keepdims=True)
        term = count * bases_ref[base : base + 1].astype(jnp.float32)
        edited = term if edited is None else edited + term
    got_embedding.wait()
    summed = edited + jnp.dot(take, embedding_ref[...], preferred_element_type=jnp.float32)
    pooled = (summed * (1.0 / POOL)).astype(jnp.bfloat16)
    sides = []
    for move, ref in ((got_w_row, w_row_ref), (got_w_col, w_col_ref)):
        move.wait()
        sides.append(jnp.dot(pooled, ref[...], preferred_element_type=jnp.float32).astype(jnp.bfloat16))
    both = jnp.concatenate(sides, axis=1)
    for k in range(copies):
        copies_ref[k] = both


def projected(embedding, bases_table, edit_pos, edit_tok, w_row, w_col, dist_gain, head_weight, map_bins, copies, size, table):
    vmem = pl.BlockSpec(memory_space=pltpu.VMEM)
    operands = (
        embedding,
        bases_table,
        edit_pos[None],
        edit_tok[None],
        w_row,
        w_col,
        dist_gain[None],
        head_weight[None],
    )
    channels = w_row.shape[1]
    return pl.pallas_call(
        functools.partial(project_kernel, map_bins, size, table),
        out_shape=(
            jax.ShapeDtypeStruct((copies, embedding.shape[0] // POOL, 2 * channels), jnp.bfloat16),
            jax.ShapeDtypeStruct((4, 8 * (tiles_of(size) + (size + 2 * MARGIN) // 4 - 1), channels), jnp.float32),
            jax.ShapeDtypeStruct((16, 2 * channels), jnp.bfloat16),
        ),
        in_specs=[pl.BlockSpec(memory_space=pltpu.HBM)] * 8,
        out_specs=(vmem, vmem, vmem),
        scratch_shapes=[pltpu.VMEM(x.shape, x.dtype) for x in operands] + [pltpu.SemaphoreType.DMA((8,))],
        compiler_params=pltpu.CompilerParams(vmem_limit_bytes=16 * 1024 * 1024),
    )(*(pltpu.with_memory_space_constraint(x, pltpu.HBM) for x in operands))


def map_kernel(
    map_bins, size, table, proj_ref, dist_ref, first_ref, second_ref, head_ref,
    kept_ref, sent_ref, row_ref, col_ref, own_ref, moved_ref, hidden_ref, pairs_one_ref, pairs_two_ref,
    last_ref, mixed_ref, score_ref,
):
    channels = head_ref.shape[1] // 2
    tiles = tiles_of(size)
    wide = 16 * (tiles - 2)
    breadth = 4 * size
    pair_rows = size + 2 * MARGIN
    couples = pair_rows // 2
    hidden_couples = size // 2 + SECOND_SPACING
    depth = 3 * channels
    row_a, col_a, row_b, col_b, diagonal, _ = lookup(table)
    rows, cols = (row_a * size, row_b * size), (col_a * size, col_b * size)
    for ref, given in ((pairs_one_ref, first_ref), (pairs_two_ref, second_ref)):
        ref[3 * depth :, :channels] = jnp.zeros((depth, channels), jnp.bfloat16)
        ref[:depth, channels:] = jnp.zeros((depth, channels), jnp.bfloat16)
        ref[: 3 * depth, :channels] = given[...]
        ref[depth:, channels:] = given[...]

    def of_block(lane, values):
        return jnp.where((lane & 2) == 0, values[0], values[1])

    def spread(ref, part, offset, along):
        count = ref.shape[0]
        at = lax.broadcasted_iota(jnp.int32, (count, map_bins), 0)
        lane = at & 7
        bins = along(at >> 3, lane) + of_block(lane, offset)
        hot = (bins == lax.broadcasted_iota(jnp.int32, (count, map_bins), 1)).astype(jnp.float32)
        found = jnp.dot(
            hot.astype(jnp.bfloat16),
            proj_ref[:, part * channels : (part + 1) * channels],
            preferred_element_type=jnp.float32,
        )
        bins = bins[:, :channels]
        ref[...] = jnp.where((bins >= 0) & (bins < map_bins), found, OUTSIDE)

    spread(col_ref, 1, cols, lambda tile, lane: 4 * tile + 2 * (lane >> 2) + (lane & 1) - PAD)
    spread(row_ref, 0, rows, lambda row, lane: row - MARGIN)
    lane = lax.broadcasted_iota(jnp.int32, (16, channels), 0) & 7
    last_start = map_bins - size
    left = of_block(lane, [jnp.where(col > 0, 1.0, 0.0) for col in cols])
    right = of_block(lane, [jnp.where(col < last_start, 1.0, 0.0) for col in cols])
    above = of_block(lane, [jnp.where(row > 0, 1.0, 0.0) for row in rows])
    below = of_block(lane, [jnp.where(row < last_start, 1.0, 0.0) for row in rows])

    def couple(two):
        parts = [x.reshape(-1, 1, 8, channels) for x in two]
        return jnp.concatenate(parts, axis=1).reshape(-1, channels).astype(jnp.bfloat16)

    def build(c):
        values, ahead = [], []
        for p in (2 * c, 2 * c + 1):
            at = 8 * (pair_rows // 4 - 1 - p // 4)
            apart = dist_ref[p % 4, at : at + 8 * tiles]
            line = jnp.concatenate([row_ref[8 * p : 8 * p + 8]] * tiles, axis=0)
            value = relu(col_ref[...] + apart + line)
            values.append(value[8 : 8 * (tiles - 1)])
            ahead.append(pltpu.roll(value, 8 * tiles - 4, 0)[: 8 * (tiles - 1)])
        own_ref[c] = couple(values)
        moved_ref[c] = couple(ahead)

    def paired(taps, bases, step, weight):
        lhs = [
            jnp.concatenate([tap for k in range(4) for tap in taps(base + k * step)], axis=1) for base in bases
        ]
        lhs = lhs[0] if len(lhs) == 1 else jnp.concatenate(lhs, axis=0)
        out = jnp.dot(lhs, weight[...], preferred_element_type=jnp.float32)
        tall = out.shape[0] // len(bases)
        return [
            [out[n * tall : (n + 1) * tall, half * channels : (half + 1) * channels] for half in range(2)]
            for n in range(len(bases))
        ]

    def first_taps(c):
        return moved_ref[c, :wide], own_ref[c], moved_ref[c, 16 : wide + 16]

    def second_taps(c):
        return tuple(hidden_ref[c, 16 * b : 16 * b + breadth] for b in range(3))

    def keep_hidden(bases, out):
        for n, base in enumerate(bases):
            for half in range(2):
                c = base + half
                value = own_ref[c + 1].astype(jnp.float32) + relu(out[n][half])
                for edge, flags in ((c < 2, above), (c >= hidden_couples - 2, below)):
                    if edge:
                        value = value * jnp.concatenate([flags] * (tiles - 2), axis=0)
                value = jnp.concatenate(
                    [value[:16] * left, value[16 : wide - 16], value[wide - 16 :] * right], axis=0
                )
                hidden_ref[c] = value.astype(jnp.bfloat16)

    def keep_last(base, out):
        for half in range(2):
            own = hidden_ref[base + 2 * half + 2, 16 : 16 + breadth].astype(jnp.float32)
            last_ref[base // 4 * 2 + base % 4, :, half * channels : (half + 1) * channels] = (
                own + relu(out[half])
            ).astype(jnp.bfloat16)

    def keep_scores(start, count):
        got = lax.dot_general(
            head_ref[...],
            last_ref[start : start + count].reshape(count * breadth, 2 * channels),
            (((1,), (1,)), ((), ())),
            preferred_element_type=jnp.float32,
        )
        lines = [
            got[half : half + 1, n * breadth : (n + 1) * breadth]
            for pair in range(0, count, 2)
            for half in range(2)
            for n in (pair, pair + 1)
        ]
        mixed_ref[2 * start : 2 * (start + count)] = jnp.concatenate(lines, axis=0)

    first_groups, second_groups = hidden_couples // 4, size // 8
    for c in range(8):
        build(c)
    for s in range(first_groups + 1):
        later = list(range(4 * (s + 2), min(4 * (s + 3), couples)))
        for part in range(2):
            one = seconds = None
            first_base, second_base = 4 * s + 2 * part, 4 * (s - 2) + part
            if s < first_groups:
                one = paired(first_taps, (first_base,), 1, pairs_one_ref)
            for c in later[2 * part : 2 * part + 2]:
                build(c)
            if 0 <= s - 2 < second_groups:
                seconds = paired(second_taps, (second_base,), 2, pairs_two_ref)
            if one is not None:
                keep_hidden((first_base,), one)
            if seconds:
                keep_last(second_base, seconds[0])
            if part == 0 and s >= 4 and s % 2 == 0:
                keep_scores(2 * (s - 4), 4)
    keep_scores(size // 4 - 4, 4)
    source = lax.broadcasted_iota(jnp.int32, (breadth, breadth), 0)
    place = ((source >> 3) & 1) * (2 * size) + ((source >> 1) & 1) * size
    place = place + 4 * (source >> 4) + 2 * ((source >> 2) & 1) + (source & 1)
    order = (place == lax.broadcasted_iota(jnp.int32, (breadth, breadth), 1)).astype(jnp.float32)
    order = order.astype(jnp.bfloat16)
    rest, ordered = mixed_ref[...], None
    for _ in range(3):
        piece = rest.astype(jnp.bfloat16)
        rest = rest - piece.astype(jnp.float32)
        moved = jnp.dot(piece, order, preferred_element_type=jnp.float32)
        ordered = moved if ordered is None else ordered + moved
    for row in range(2):
        score_ref[pl.ds(row, size // 2, 2)] = ordered[:, row * 2 * size : (row + 1) * 2 * size]
    score = score_ref[...]
    turned = score.T
    first, second = score[:, :size], score[:, size:]
    turned_first, turned_second = turned[:size], turned[size:]
    alone = diagonal == 1
    kept_ref[...] = 0.5 * (first + jnp.where(alone, turned_first, turned_second))
    sent_ref[...] = 0.5 * (second + jnp.where(alone, turned_second, turned_first))


def block_scores(every, dist_table, first_kernel, second_kernel, head, size, table):
    map_bins = every.shape[0]
    channels = dist_table.shape[2]
    tiles = tiles_of(size)
    pair_rows = size + 2 * MARGIN
    vmem = pl.BlockSpec(memory_space=pltpu.VMEM)
    block = jax.ShapeDtypeStruct((size, size), jnp.float32)
    return pl.pallas_call(
        functools.partial(map_kernel, map_bins, size, table),
        out_shape=(block, block),
        in_specs=[vmem] * 5,
        out_specs=(vmem, vmem),
        scratch_shapes=[
            pltpu.VMEM((8 * pair_rows, channels), jnp.float32),
            pltpu.VMEM((8 * tiles, channels), jnp.float32),
            pltpu.VMEM((pair_rows // 2, 16 * (tiles - 2), channels), jnp.bfloat16),
            pltpu.VMEM((pair_rows // 2, 16 * (tiles - 1), channels), jnp.bfloat16),
            pltpu.VMEM((size // 2 + SECOND_SPACING, 16 * (tiles - 2), channels), jnp.bfloat16),
            pltpu.VMEM((12 * channels, 2 * channels), jnp.bfloat16),
            pltpu.VMEM((12 * channels, 2 * channels), jnp.bfloat16),
            pltpu.VMEM((size // 4, 4 * size, 2 * channels), jnp.bfloat16),
            pltpu.VMEM((size // 2, 4 * size), jnp.float32),
            pltpu.VMEM((size, 2 * size), jnp.float32),
        ],
        compiler_params=pltpu.CompilerParams(vmem_limit_bytes=40 * 1024 * 1024),
    )(
        every,
        dist_table,
        first_kernel.reshape(9 * channels, channels),
        second_kernel.reshape(9 * channels, channels),
        head,
    )


def on_device(
    embedding,
    bases_table,
    edit_pos,
    edit_tok,
    w_row,
    w_col,
    dist_gain,
    first_kernel,
    second_kernel,
    head_weight,
):
    n_rows, n_cols = lax.axis_size("row"), lax.axis_size("col")
    devices = n_rows * n_cols
    map_bins = embedding.shape[0] * devices // POOL
    table, target = plan(n_rows, n_cols)
    size = map_bins // max(n_rows, n_cols)
    copies, dist_table, head = projected(
        embedding, bases_table, edit_pos, edit_tok, w_row, w_col, dist_gain, head_weight, map_bins, devices, size, table
    )
    got = lax.all_to_all(copies, ("row", "col"), 0, 0)
    every = got.reshape(map_bins, got.shape[2])
    kept, sent = block_scores(every, dist_table, first_kernel, second_kernel, head, size, table)
    received = lax.ppermute(sent, ("row", "col"), [(device, target[device]) for device in range(devices)])
    place = lookup(table)[5]
    axis = 1 if n_rows > n_cols else 0
    return jnp.where(
        place == 0,
        jnp.concatenate([kept, received], axis=axis),
        jnp.concatenate([received, kept], axis=axis),
    )


def solution(mesh):
    placed = (P(("row", "col"), None), P(), P("cand"), P("cand"), P(), P(), P(), P(), P(), P())
    return jax.shard_map(
        on_device, mesh=mesh, in_specs=placed, out_specs=P(("cand", "row"), "col"), check_vma=False
    )
```

```python
import functools
import math

import jax
import jax.numpy as jnp
from jax import lax
from jax.experimental import pallas as pl
from jax.experimental.pallas import tpu as pltpu
from jax.sharding import PartitionSpec as P

POOL = 4
FIRST_SPACING = 2
SECOND_SPACING = 4
BASES = 4
MARGIN = FIRST_SPACING + SECOND_SPACING
PAD = 8
GROUP = 8
OUTSIDE = -1e30


def plan(n_rows, n_cols):
    wide = n_rows > n_cols
    blocks = max(n_rows, n_cols)
    assert blocks == 2 * min(n_rows, n_cols)

    def owner(i, j):
        return i * n_cols + j // 2 if wide else (i // 2) * n_cols + j

    held = {}
    for i in range(blocks):
        for j in range(blocks):
            held.setdefault(owner(i, j), []).append((i, j))

    def other(device, block):
        return next(b for b in held[device] if b != block)

    jobs, target = {}, {}

    def assign(device, kept, sent):
        place = held[device].index(kept)
        jobs[device] = (*kept, *sent, int(kept[0] == kept[1]), place)
        target[device] = owner(*sent)

    def walk(device, block):
        while device not in jobs:
            if block[0] == block[1]:
                return device, block
            sent = (block[1], block[0])
            assign(device, block, sent)
            device = owner(*sent)
            block = other(device, sent)
        return None, None

    for d in range(blocks):
        start = owner(d, d)
        if start not in jobs:
            end, last = walk(start, other(start, (d, d)))
            assign(end, last, (d, d))
    for device in sorted(held):
        if device not in jobs:
            walk(device, held[device][0])
    return [jobs[device] for device in sorted(jobs)], target


def tiles_of(size):
    return (size + 2 * PAD) // 4


def relu(x):
    return jnp.maximum(x, 0.0)


def lookup(table):
    n_cols = lax.axis_size("col")
    here = lax.axis_index("row") * n_cols + lax.axis_index("col")
    found = []
    for values in zip(*table):
        value = jnp.int32(values[0])
        for device in range(1, len(values)):
            value = jnp.where(here == device, jnp.int32(values[device]), value)
        found.append(value)
    return found


def project_kernel(
    map_bins, size, table, embedding_hbm, bases_hbm, pos_hbm, tok_hbm, w_row_hbm, w_col_hbm, gain_hbm, head_hbm,
    copies_ref, dist_ref, head_ref,
    embedding_ref, bases_ref, pos_ref, tok_ref, w_row_ref, w_col_ref, gain_ref, weight_ref, arrived,
):
    moves = [
        pltpu.make_async_copy(source, target, arrived.at[n])
        for n, (source, target) in enumerate(
            (
                (embedding_hbm, embedding_ref),
                (w_row_hbm, w_row_ref),
                (w_col_hbm, w_col_ref),
                (pos_hbm, pos_ref),
                (tok_hbm, tok_ref),
                (bases_hbm, bases_ref),
                (gain_hbm, gain_ref),
                (head_hbm, weight_ref),
            )
        )
    ]
    for move in moves:
        move.start()
    got_embedding, got_w_row, got_w_col, *small = moves
    shard_bins = embedding_ref.shape[0]
    copies, pooled_bins, _ = copies_ref.shape
    channels = gain_ref.shape[1]
    edits = pos_ref.shape[1]
    row_a, col_a, row_b, col_b, _, _ = lookup(table)
    phases, count, _ = dist_ref.shape
    at = lax.broadcasted_iota(jnp.int32, (count, channels), 0)
    lane = at & 7
    start = jnp.where((lane & 2) == 0, (col_a - row_a) * size, (col_b - row_b) * size)
    start = start + 4 * (at >> 3) + 2 * (lane >> 2) + (lane & 1) - 2 - 4 * ((size + 2 * MARGIN) // 4 - 1)
    feature = [
        jnp.log1p(jnp.abs(start - phase).astype(jnp.float32)) * (1.0 / math.log(map_bins))
        for phase in range(phases)
    ]
    first_bin = (lax.axis_index("row") * lax.axis_size("col") + lax.axis_index("col")) * shard_bins
    bins = first_bin + lax.broadcasted_iota(jnp.int32, (pooled_bins, edits), 0) * POOL
    back = lax.broadcasted_iota(jnp.int32, (pooled_bins, shard_bins), 1) - POOL * (
        lax.broadcasted_iota(jnp.int32, (pooled_bins, shard_bins), 0)
    )
    take = ((back >= 0) & (back < POOL)).astype(jnp.float32).astype(jnp.bfloat16)
    for move in small:
        move.wait()
    for phase in range(phases):
        dist_ref[phase] = gain_ref[...] * feature[phase]
    weight = jnp.concatenate([weight_ref[...].astype(jnp.float32)] * 2, axis=1)
    line = lax.broadcasted_iota(jnp.int32, head_ref.shape, 0)
    half = lax.broadcasted_iota(jnp.int32, head_ref.shape, 1) >= channels
    head_ref[...] = jnp.where(line == half.astype(jnp.int32), weight, 0.0).astype(jnp.bfloat16)
    ahead = pos_ref[...] - bins
    in_bin = ((ahead >= 0) & (ahead < POOL)).astype(jnp.float32)
    edited = None
    for base in range(BASES):
        is_base = (tok_ref[...] == base).astype(jnp.float32)
        count = jnp.sum(in_bin * is_base, axis=1, keepdims=True)
        term = count * bases_ref[base : base + 1].astype(jnp.float32)
        edited = term if edited is None else edited + term
    got_embedding.wait()
    summed = edited + jnp.dot(take, embedding_ref[...], preferred_element_type=jnp.float32)
    pooled = (summed * (1.0 / POOL)).astype(jnp.bfloat16)
    sides = []
    for move, ref in ((got_w_row, w_row_ref), (got_w_col, w_col_ref)):
        move.wait()
        sides.append(jnp.dot(pooled, ref[...], preferred_element_type=jnp.float32).astype(jnp.bfloat16))
    both = jnp.concatenate(sides, axis=1)
    for k in range(copies):
        copies_ref[k] = both


def projected(embedding, bases_table, edit_pos, edit_tok, w_row, w_col, dist_gain, head_weight, map_bins, copies, size, table):
    vmem = pl.BlockSpec(memory_space=pltpu.VMEM)
    operands = (
        embedding,
        bases_table,
        edit_pos[None],
        edit_tok[None],
        w_row,
        w_col,
        dist_gain[None],
        head_weight[None],
    )
    channels = w_row.shape[1]
    return pl.pallas_call(
        functools.partial(project_kernel, map_bins, size, table),
        out_shape=(
            jax.ShapeDtypeStruct((copies, embedding.shape[0] // POOL, 2 * channels), jnp.bfloat16),
            jax.ShapeDtypeStruct((4, 8 * (tiles_of(size) + (size + 2 * MARGIN) // 4 - 1), channels), jnp.float32),
            jax.ShapeDtypeStruct((16, 2 * channels), jnp.bfloat16),
        ),
        in_specs=[pl.BlockSpec(memory_space=pltpu.HBM)] * 8,
        out_specs=(vmem, vmem, vmem),
        scratch_shapes=[pltpu.VMEM(x.shape, x.dtype) for x in operands] + [pltpu.SemaphoreType.DMA((8,))],
        compiler_params=pltpu.CompilerParams(vmem_limit_bytes=16 * 1024 * 1024),
    )(*(pltpu.with_memory_space_constraint(x, pltpu.HBM) for x in operands))


def map_kernel(
    map_bins, size, table, proj_ref, dist_ref, first_ref, second_ref, head_ref,
    kept_ref, sent_ref, row_ref, col_ref, own_ref, moved_ref, hidden_ref, pairs_one_ref, pairs_two_ref,
    last_ref, mixed_ref, score_ref,
):
    channels = head_ref.shape[1] // 2
    tiles = tiles_of(size)
    wide = 16 * (tiles - 2)
    breadth = 4 * size
    pair_rows = size + 2 * MARGIN
    couples = pair_rows // 2
    hidden_couples = size // 2 + SECOND_SPACING
    depth = 3 * channels
    row_a, col_a, row_b, col_b, diagonal, _ = lookup(table)
    rows, cols = (row_a * size, row_b * size), (col_a * size, col_b * size)
    def place_weights(ref, given):
        ref[3 * depth :, :channels] = jnp.zeros((depth, channels), jnp.bfloat16)
        ref[:depth, channels:] = jnp.zeros((depth, channels), jnp.bfloat16)
        ref[: 3 * depth, :channels] = given[...]
        ref[depth:, channels:] = given[...]

    place_weights(pairs_one_ref, first_ref)

    def of_block(lane, values):
        return jnp.where((lane & 2) == 0, values[0], values[1])

    def spread(ref, part, offset, along):
        count = ref.shape[0]
        at = lax.broadcasted_iota(jnp.int32, (count, map_bins), 0)
        lane = at & 7
        bins = along(at >> 3, lane) + of_block(lane, offset)
        hot = (bins == lax.broadcasted_iota(jnp.int32, (count, map_bins), 1)).astype(jnp.float32)
        found = jnp.dot(
            hot.astype(jnp.bfloat16),
            proj_ref[:, part * channels : (part + 1) * channels],
            preferred_element_type=jnp.float32,
        )
        bins = bins[:, :channels]
        ref[...] = jnp.where((bins >= 0) & (bins < map_bins), found, OUTSIDE)

    spread(col_ref, 1, cols, lambda tile, lane: 4 * tile + 2 * (lane >> 2) + (lane & 1) - PAD)
    spread(row_ref, 0, rows, lambda row, lane: row - MARGIN)
    lane = lax.broadcasted_iota(jnp.int32, (16, channels), 0) & 7
    last_start = map_bins - size
    left = of_block(lane, [jnp.where(col > 0, 1.0, 0.0) for col in cols])
    right = of_block(lane, [jnp.where(col < last_start, 1.0, 0.0) for col in cols])
    above = of_block(lane, [jnp.where(row > 0, 1.0, 0.0) for row in rows])
    below = of_block(lane, [jnp.where(row < last_start, 1.0, 0.0) for row in rows])

    def couple(two):
        parts = [x.reshape(-1, 1, 8, channels) for x in two]
        return jnp.concatenate(parts, axis=1).reshape(-1, channels).astype(jnp.bfloat16)

    def build(c):
        values, ahead = [], []
        for p in (2 * c, 2 * c + 1):
            at = 8 * (pair_rows // 4 - 1 - p // 4)
            apart = dist_ref[p % 4, at : at + 8 * tiles]
            line = jnp.concatenate([row_ref[8 * p : 8 * p + 8]] * tiles, axis=0)
            value = relu(col_ref[...] + apart + line)
            values.append(value[8 : 8 * (tiles - 1)])
            ahead.append(pltpu.roll(value, 8 * tiles - 4, 0)[: 8 * (tiles - 1)])
        own_ref[c] = couple(values)
        moved_ref[c] = couple(ahead)

    def paired(taps, bases, step, weight):
        lhs = [
            jnp.concatenate([tap for k in range(4) for tap in taps(base + k * step)], axis=1) for base in bases
        ]
        lhs = lhs[0] if len(lhs) == 1 else jnp.concatenate(lhs, axis=0)
        out = jnp.dot(lhs, weight[...], preferred_element_type=jnp.float32)
        tall = out.shape[0] // len(bases)
        return [
            [out[n * tall : (n + 1) * tall, half * channels : (half + 1) * channels] for half in range(2)]
            for n in range(len(bases))
        ]

    def first_taps(c):
        return moved_ref[c, :wide], own_ref[c], moved_ref[c, 16 : wide + 16]

    def second_taps(c):
        return tuple(hidden_ref[c, 16 * b : 16 * b + breadth] for b in range(3))

    def keep_hidden(bases, out):
        for n, base in enumerate(bases):
            for half in range(2):
                c = base + half
                value = own_ref[c + 1].astype(jnp.float32) + relu(out[n][half])
                for edge, flags in ((c < 2, above), (c >= hidden_couples - 2, below)):
                    if edge:
                        value = value * jnp.concatenate([flags] * (tiles - 2), axis=0)
                value = jnp.concatenate(
                    [value[:16] * left, value[16 : wide - 16], value[wide - 16 :] * right], axis=0
                )
                hidden_ref[c] = value.astype(jnp.bfloat16)

    def keep_last(base, out):
        for half in range(2):
            own = hidden_ref[base + 2 * half + 2, 16 : 16 + breadth].astype(jnp.float32)
            last_ref[base // 4 * 2 + base % 4, :, half * channels : (half + 1) * channels] = (
                own + relu(out[half])
            ).astype(jnp.bfloat16)

    def keep_scores(start, count):
        got = lax.dot_general(
            head_ref[...],
            last_ref[start : start + count].reshape(count * breadth, 2 * channels),
            (((1,), (1,)), ((), ())),
            preferred_element_type=jnp.float32,
        )
        lines = [
            got[half : half + 1, n * breadth : (n + 1) * breadth]
            for pair in range(0, count, 2)
            for half in range(2)
            for n in (pair, pair + 1)
        ]
        mixed_ref[2 * start : 2 * (start + count)] = jnp.concatenate(lines, axis=0)

    first_groups, second_groups = hidden_couples // 4, size // 8
    for c in range(4):
        build(c)
    for s in range(first_groups + 1):
        later = list(range(4 * (s + 2), min(4 * (s + 3), couples)))
        for part in range(2):
            one = seconds = None
            first_base, second_base = 4 * s + 2 * part, 4 * (s - 2) + part
            if s < first_groups:
                one = paired(first_taps, (first_base,), 1, pairs_one_ref)
            if first_base == 0:
                for c in range(4, 8):
                    build(c)
                place_weights(pairs_two_ref, second_ref)
            for c in later[2 * part : 2 * part + 2]:
                build(c)
            if 0 <= s - 2 < second_groups:
                seconds = paired(second_taps, (second_base,), 2, pairs_two_ref)
            if one is not None:
                keep_hidden((first_base,), one)
            if seconds:
                keep_last(second_base, seconds[0])
            if part == 0 and s >= 4 and s % 2 == 0:
                keep_scores(2 * (s - 4), 4)
    keep_scores(size // 4 - 4, 4)
    source = lax.broadcasted_iota(jnp.int32, (breadth, breadth), 0)
    place = ((source >> 3) & 1) * (2 * size) + ((source >> 1) & 1) * size
    place = place + 4 * (source >> 4) + 2 * ((source >> 2) & 1) + (source & 1)
    order = (place == lax.broadcasted_iota(jnp.int32, (breadth, breadth), 1)).astype(jnp.float32)
    order = order.astype(jnp.bfloat16)
    rest, ordered = mixed_ref[...], None
    for _ in range(3):
        piece = rest.astype(jnp.bfloat16)
        rest = rest - piece.astype(jnp.float32)
        moved = jnp.dot(piece, order, preferred_element_type=jnp.float32)
        ordered = moved if ordered is None else ordered + moved
    for row in range(2):
        score_ref[pl.ds(row, size // 2, 2)] = ordered[:, row * 2 * size : (row + 1) * 2 * size]
    score = score_ref[...]
    turned = score.T
    first, second = score[:, :size], score[:, size:]
    turned_first, turned_second = turned[:size], turned[size:]
    alone = diagonal == 1
    kept_ref[...] = 0.5 * (first + jnp.where(alone, turned_first, turned_second))
    sent_ref[...] = 0.5 * (second + jnp.where(alone, turned_second, turned_first))


def block_scores(every, dist_table, first_kernel, second_kernel, head, size, table):
    map_bins = every.shape[0]
    channels = dist_table.shape[2]
    tiles = tiles_of(size)
    pair_rows = size + 2 * MARGIN
    vmem = pl.BlockSpec(memory_space=pltpu.VMEM)
    block = jax.ShapeDtypeStruct((size, size), jnp.float32)
    return pl.pallas_call(
        functools.partial(map_kernel, map_bins, size, table),
        out_shape=(block, block),
        in_specs=[vmem] * 5,
        out_specs=(vmem, vmem),
        scratch_shapes=[
            pltpu.VMEM((8 * pair_rows, channels), jnp.float32),
            pltpu.VMEM((8 * tiles, channels), jnp.float32),
            pltpu.VMEM((pair_rows // 2, 16 * (tiles - 2), channels), jnp.bfloat16),
            pltpu.VMEM((pair_rows // 2, 16 * (tiles - 1), channels), jnp.bfloat16),
            pltpu.VMEM((size // 2 + SECOND_SPACING, 16 * (tiles - 2), channels), jnp.bfloat16),
            pltpu.VMEM((12 * channels, 2 * channels), jnp.bfloat16),
            pltpu.VMEM((12 * channels, 2 * channels), jnp.bfloat16),
            pltpu.VMEM((size // 4, 4 * size, 2 * channels), jnp.bfloat16),
            pltpu.VMEM((size // 2, 4 * size), jnp.float32),
            pltpu.VMEM((size, 2 * size), jnp.float32),
        ],
        compiler_params=pltpu.CompilerParams(vmem_limit_bytes=40 * 1024 * 1024),
    )(
        every,
        dist_table,
        first_kernel.reshape(9 * channels, channels),
        second_kernel.reshape(9 * channels, channels),
        head,
    )


def on_device(
    embedding,
    bases_table,
    edit_pos,
    edit_tok,
    w_row,
    w_col,
    dist_gain,
    first_kernel,
    second_kernel,
    head_weight,
):
    n_rows, n_cols = lax.axis_size("row"), lax.axis_size("col")
    devices = n_rows * n_cols
    map_bins = embedding.shape[0] * devices // POOL
    table, target = plan(n_rows, n_cols)
    size = map_bins // max(n_rows, n_cols)
    copies, dist_table, head = projected(
        embedding, bases_table, edit_pos, edit_tok, w_row, w_col, dist_gain, head_weight, map_bins, devices, size, table
    )
    got = lax.all_to_all(copies, ("row", "col"), 0, 0)
    every = got.reshape(map_bins, got.shape[2])
    kept, sent = block_scores(every, dist_table, first_kernel, second_kernel, head, size, table)
    received = lax.ppermute(sent, ("row", "col"), [(device, target[device]) for device in range(devices)])
    place = lookup(table)[5]
    axis = 1 if n_rows > n_cols else 0
    return jnp.where(
        place == 0,
        jnp.concatenate([kept, received], axis=axis),
        jnp.concatenate([received, kept], axis=axis),
    )


def solution(mesh):
    placed = (P(("row", "col"), None), P(), P("cand"), P("cand"), P(), P(), P(), P(), P(), P())
    return jax.shard_map(
        on_device, mesh=mesh, in_specs=placed, out_specs=P(("cand", "row"), "col"), check_vma=False
    )
```

```python
import functools
import math

import jax
import jax.numpy as jnp
from jax import lax
from jax.experimental import pallas as pl
from jax.experimental.pallas import tpu as pltpu
from jax.sharding import PartitionSpec as P

POOL = 4
FIRST_SPACING = 2
SECOND_SPACING = 4
BASES = 4
MARGIN = FIRST_SPACING + SECOND_SPACING
PAD = 8
GROUP = 8
OUTSIDE = -1e30


def plan(n_rows, n_cols):
    wide = n_rows > n_cols
    blocks = max(n_rows, n_cols)
    assert blocks == 2 * min(n_rows, n_cols)

    def owner(i, j):
        return i * n_cols + j // 2 if wide else (i // 2) * n_cols + j

    held = {}
    for i in range(blocks):
        for j in range(blocks):
            held.setdefault(owner(i, j), []).append((i, j))

    def other(device, block):
        return next(b for b in held[device] if b != block)

    jobs, target = {}, {}

    def assign(device, kept, sent):
        place = held[device].index(kept)
        jobs[device] = (*kept, *sent, int(kept[0] == kept[1]), place)
        target[device] = owner(*sent)

    def walk(device, block):
        while device not in jobs:
            if block[0] == block[1]:
                return device, block
            sent = (block[1], block[0])
            assign(device, block, sent)
            device = owner(*sent)
            block = other(device, sent)
        return None, None

    for d in range(blocks):
        start = owner(d, d)
        if start not in jobs:
            end, last = walk(start, other(start, (d, d)))
            assign(end, last, (d, d))
    for device in sorted(held):
        if device not in jobs:
            walk(device, held[device][0])
    return [jobs[device] for device in sorted(jobs)], target


def tiles_of(size):
    return (size + 2 * PAD) // 4


def relu(x):
    return jnp.maximum(x, 0.0)


def lookup(table):
    n_cols = lax.axis_size("col")
    here = lax.axis_index("row") * n_cols + lax.axis_index("col")
    found = []
    for values in zip(*table):
        value = jnp.int32(values[0])
        for device in range(1, len(values)):
            value = jnp.where(here == device, jnp.int32(values[device]), value)
        found.append(value)
    return found


def project_kernel(
    map_bins, size, table, embedding_hbm, bases_hbm, pos_hbm, tok_hbm, w_row_hbm, w_col_hbm, gain_hbm, head_hbm,
    copies_ref, dist_ref, head_ref,
    embedding_ref, bases_ref, pos_ref, tok_ref, w_row_ref, w_col_ref, gain_ref, weight_ref, arrived,
):
    moves = [
        pltpu.make_async_copy(source, target, arrived.at[n])
        for n, (source, target) in enumerate(
            (
                (embedding_hbm, embedding_ref),
                (w_row_hbm, w_row_ref),
                (w_col_hbm, w_col_ref),
                (pos_hbm, pos_ref),
                (tok_hbm, tok_ref),
                (bases_hbm, bases_ref),
                (gain_hbm, gain_ref),
                (head_hbm, weight_ref),
            )
        )
    ]
    for move in moves:
        move.start()
    got_embedding, got_w_row, got_w_col, *small = moves
    shard_bins = embedding_ref.shape[0]
    copies, pooled_bins, _ = copies_ref.shape
    channels = gain_ref.shape[1]
    edits = pos_ref.shape[1]
    row_a, col_a, row_b, col_b, _, _ = lookup(table)
    phases, count, _ = dist_ref.shape
    at = lax.broadcasted_iota(jnp.int32, (count, channels), 0)
    lane = at & 7
    start = jnp.where((lane & 2) == 0, (col_a - row_a) * size, (col_b - row_b) * size)
    start = start + 4 * (at >> 3) + 2 * (lane >> 2) + (lane & 1) - 2 - 4 * ((size + 2 * MARGIN) // 4 - 1)
    feature = [
        jnp.log1p(jnp.abs(start - phase).astype(jnp.float32)) * (1.0 / math.log(map_bins))
        for phase in range(phases)
    ]
    first_bin = (lax.axis_index("row") * lax.axis_size("col") + lax.axis_index("col")) * shard_bins
    bins = first_bin + lax.broadcasted_iota(jnp.int32, (pooled_bins, edits), 0) * POOL
    back = lax.broadcasted_iota(jnp.int32, (pooled_bins, shard_bins), 1) - POOL * (
        lax.broadcasted_iota(jnp.int32, (pooled_bins, shard_bins), 0)
    )
    take = ((back >= 0) & (back < POOL)).astype(jnp.float32).astype(jnp.bfloat16)
    for move in small:
        move.wait()
    for phase in range(phases):
        dist_ref[phase] = gain_ref[...] * feature[phase]
    weight = jnp.concatenate([weight_ref[...].astype(jnp.float32)] * 2, axis=1)
    line = lax.broadcasted_iota(jnp.int32, head_ref.shape, 0)
    half = lax.broadcasted_iota(jnp.int32, head_ref.shape, 1) >= channels
    head_ref[...] = jnp.where(line == half.astype(jnp.int32), weight, 0.0).astype(jnp.bfloat16)
    ahead = pos_ref[...] - bins
    in_bin = ((ahead >= 0) & (ahead < POOL)).astype(jnp.float32)
    edited = None
    for base in range(BASES):
        is_base = (tok_ref[...] == base).astype(jnp.float32)
        count = jnp.sum(in_bin * is_base, axis=1, keepdims=True)
        term = count * bases_ref[base : base + 1].astype(jnp.float32)
        edited = term if edited is None else edited + term
    got_embedding.wait()
    summed = edited + jnp.dot(take, embedding_ref[...], preferred_element_type=jnp.float32)
    pooled = (summed * (1.0 / POOL)).astype(jnp.bfloat16)
    sides = []
    for move, ref in ((got_w_row, w_row_ref), (got_w_col, w_col_ref)):
        move.wait()
        sides.append(jnp.dot(pooled, ref[...], preferred_element_type=jnp.float32).astype(jnp.bfloat16))
    both = jnp.concatenate(sides, axis=1)
    for k in range(copies):
        copies_ref[k] = both


def projected(embedding, bases_table, edit_pos, edit_tok, w_row, w_col, dist_gain, head_weight, map_bins, copies, size, table):
    vmem = pl.BlockSpec(memory_space=pltpu.VMEM)
    operands = (
        embedding,
        bases_table,
        edit_pos[None],
        edit_tok[None],
        w_row,
        w_col,
        dist_gain[None],
        head_weight[None],
    )
    channels = w_row.shape[1]
    return pl.pallas_call(
        functools.partial(project_kernel, map_bins, size, table),
        out_shape=(
            jax.ShapeDtypeStruct((copies, embedding.shape[0] // POOL, 2 * channels), jnp.bfloat16),
            jax.ShapeDtypeStruct((4, 8 * (tiles_of(size) + (size + 2 * MARGIN) // 4 - 1), channels), jnp.float32),
            jax.ShapeDtypeStruct((16, 2 * channels), jnp.bfloat16),
        ),
        in_specs=[pl.BlockSpec(memory_space=pltpu.HBM)] * 8,
        out_specs=(vmem, vmem, vmem),
        scratch_shapes=[pltpu.VMEM(x.shape, x.dtype) for x in operands] + [pltpu.SemaphoreType.DMA((8,))],
        compiler_params=pltpu.CompilerParams(vmem_limit_bytes=16 * 1024 * 1024),
    )(*(pltpu.with_memory_space_constraint(x, pltpu.HBM) for x in operands))


def map_kernel(
    map_bins, size, table, proj_ref, dist_ref, first_ref, second_ref, head_ref,
    kept_ref, sent_ref, row_ref, col_ref, own_ref, moved_ref, hidden_ref, pairs_one_ref, pairs_two_ref,
    last_ref, mixed_ref, score_ref,
):
    channels = head_ref.shape[1] // 2
    tiles = tiles_of(size)
    wide = 16 * (tiles - 2)
    breadth = 4 * size
    pair_rows = size + 2 * MARGIN
    couples = pair_rows // 2
    hidden_couples = size // 2 + SECOND_SPACING
    depth = 3 * channels
    row_a, col_a, row_b, col_b, diagonal, _ = lookup(table)
    rows, cols = (row_a * size, row_b * size), (col_a * size, col_b * size)
    for ref, given in ((pairs_one_ref, first_ref), (pairs_two_ref, second_ref)):
        ref[3 * depth :, :channels] = jnp.zeros((depth, channels), jnp.bfloat16)
        ref[:depth, channels:] = jnp.zeros((depth, channels), jnp.bfloat16)
        ref[: 3 * depth, :channels] = given[...]
        ref[depth:, channels:] = given[...]

    def of_block(lane, values):
        return jnp.where((lane & 2) == 0, values[0], values[1])

    def spread(ref, part, offset, along):
        count = ref.shape[0]
        at = lax.broadcasted_iota(jnp.int32, (count, map_bins), 0)
        lane = at & 7
        bins = along(at >> 3, lane) + of_block(lane, offset)
        hot = (bins == lax.broadcasted_iota(jnp.int32, (count, map_bins), 1)).astype(jnp.float32)
        found = jnp.dot(
            hot.astype(jnp.bfloat16),
            proj_ref[:, part * channels : (part + 1) * channels],
            preferred_element_type=jnp.float32,
        )
        bins = bins[:, :channels]
        ref[...] = jnp.where((bins >= 0) & (bins < map_bins), found, OUTSIDE)

    spread(col_ref, 1, cols, lambda tile, lane: 4 * tile + 2 * (lane >> 2) + (lane & 1) - PAD)
    spread(row_ref, 0, rows, lambda row, lane: row - MARGIN)
    lane = lax.broadcasted_iota(jnp.int32, (16, channels), 0) & 7
    last_start = map_bins - size
    left = of_block(lane, [jnp.where(col > 0, 1.0, 0.0) for col in cols])
    right = of_block(lane, [jnp.where(col < last_start, 1.0, 0.0) for col in cols])
    above = of_block(lane, [jnp.where(row > 0, 1.0, 0.0) for row in rows])
    below = of_block(lane, [jnp.where(row < last_start, 1.0, 0.0) for row in rows])

    def couple(two):
        parts = [x.reshape(-1, 1, 8, channels) for x in two]
        return jnp.concatenate(parts, axis=1).reshape(-1, channels).astype(jnp.bfloat16)

    def build(c):
        values, ahead = [], []
        for p in (2 * c, 2 * c + 1):
            at = 8 * (pair_rows // 4 - 1 - p // 4)
            apart = dist_ref[p % 4, at : at + 8 * tiles]
            line = jnp.concatenate([row_ref[8 * p : 8 * p + 8]] * tiles, axis=0)
            value = relu(col_ref[...] + apart + line)
            values.append(value[8 : 8 * (tiles - 1)])
            ahead.append(pltpu.roll(value, 8 * tiles - 4, 0)[: 8 * (tiles - 1)])
        own_ref[c] = couple(values)
        moved_ref[c] = couple(ahead)

    def paired(taps, bases, step, weight):
        lhs = [
            jnp.concatenate([tap for k in range(4) for tap in taps(base + k * step)], axis=1) for base in bases
        ]
        lhs = lhs[0] if len(lhs) == 1 else jnp.concatenate(lhs, axis=0)
        out = jnp.dot(lhs, weight[...], preferred_element_type=jnp.float32)
        tall = out.shape[0] // len(bases)
        return [
            [out[n * tall : (n + 1) * tall, half * channels : (half + 1) * channels] for half in range(2)]
            for n in range(len(bases))
        ]

    def first_taps(c):
        return moved_ref[c, :wide], own_ref[c], moved_ref[c, 16 : wide + 16]

    def second_taps(c):
        return tuple(hidden_ref[c, 16 * b : 16 * b + breadth] for b in range(3))

    def keep_hidden(bases, out):
        for n, base in enumerate(bases):
            for half in range(2):
                c = base + half
                value = own_ref[c + 1].astype(jnp.float32) + relu(out[n][half])
                for edge, flags in ((c < 2, above), (c >= hidden_couples - 2, below)):
                    if edge:
                        value = value * jnp.concatenate([flags] * (tiles - 2), axis=0)
                value = jnp.concatenate(
                    [value[:16] * left, value[16 : wide - 16], value[wide - 16 :] * right], axis=0
                )
                hidden_ref[c] = value.astype(jnp.bfloat16)

    def keep_last(base, out):
        for half in range(2):
            own = hidden_ref[base + 2 * half + 2, 16 : 16 + breadth].astype(jnp.float32)
            last_ref[base // 4 * 2 + base % 4, :, half * channels : (half + 1) * channels] = (
                own + relu(out[half])
            ).astype(jnp.bfloat16)

    def keep_scores(start, count):
        got = lax.dot_general(
            head_ref[...],
            last_ref[start : start + count].reshape(count * breadth, 2 * channels),
            (((1,), (1,)), ((), ())),
            preferred_element_type=jnp.float32,
        )
        lines = [
            got[half : half + 1, n * breadth : (n + 1) * breadth]
            for pair in range(0, count, 2)
            for half in range(2)
            for n in (pair, pair + 1)
        ]
        mixed_ref[2 * start : 2 * (start + count)] = jnp.concatenate(lines, axis=0)

    first_groups, second_groups = hidden_couples // 4, size // 8
    for c in range(8):
        build(c)
    waiting = None
    for s in range(first_groups + 1):
        later = list(range(4 * (s + 2), min(4 * (s + 3), couples)))
        for part in range(2):
            one = seconds = None
            first_base, second_base = 4 * s + 2 * part, 4 * (s - 2) + part
            if s < first_groups:
                one = paired(first_taps, (first_base,), 1, pairs_one_ref)
            if waiting is not None:
                keep_last(*waiting)
                waiting = None
            for c in later[2 * part : 2 * part + 2]:
                build(c)
            if 0 <= s - 2 < second_groups:
                seconds = paired(second_taps, (second_base,), 2, pairs_two_ref)
            if one is not None:
                keep_hidden((first_base,), one)
            if seconds:
                waiting = second_base, seconds[0]
            if part == 0 and s >= 4 and s % 2 == 0:
                keep_scores(2 * (s - 4), 4)
    keep_last(*waiting)
    keep_scores(size // 4 - 4, 4)
    source = lax.broadcasted_iota(jnp.int32, (breadth, breadth), 0)
    place = ((source >> 3) & 1) * (2 * size) + ((source >> 1) & 1) * size
    place = place + 4 * (source >> 4) + 2 * ((source >> 2) & 1) + (source & 1)
    order = (place == lax.broadcasted_iota(jnp.int32, (breadth, breadth), 1)).astype(jnp.float32)
    order = order.astype(jnp.bfloat16)
    rest, ordered = mixed_ref[...], None
    for _ in range(3):
        piece = rest.astype(jnp.bfloat16)
        rest = rest - piece.astype(jnp.float32)
        moved = jnp.dot(piece, order, preferred_element_type=jnp.float32)
        ordered = moved if ordered is None else ordered + moved
    for row in range(2):
        score_ref[pl.ds(row, size // 2, 2)] = ordered[:, row * 2 * size : (row + 1) * 2 * size]
    score = score_ref[...]
    turned = score.T
    first, second = score[:, :size], score[:, size:]
    turned_first, turned_second = turned[:size], turned[size:]
    alone = diagonal == 1
    kept_ref[...] = 0.5 * (first + jnp.where(alone, turned_first, turned_second))
    sent_ref[...] = 0.5 * (second + jnp.where(alone, turned_second, turned_first))


def block_scores(every, dist_table, first_kernel, second_kernel, head, size, table):
    map_bins = every.shape[0]
    channels = dist_table.shape[2]
    tiles = tiles_of(size)
    pair_rows = size + 2 * MARGIN
    vmem = pl.BlockSpec(memory_space=pltpu.VMEM)
    block = jax.ShapeDtypeStruct((size, size), jnp.float32)
    return pl.pallas_call(
        functools.partial(map_kernel, map_bins, size, table),
        out_shape=(block, block),
        in_specs=[vmem] * 5,
        out_specs=(vmem, vmem),
        scratch_shapes=[
            pltpu.VMEM((8 * pair_rows, channels), jnp.float32),
            pltpu.VMEM((8 * tiles, channels), jnp.float32),
            pltpu.VMEM((pair_rows // 2, 16 * (tiles - 2), channels), jnp.bfloat16),
            pltpu.VMEM((pair_rows // 2, 16 * (tiles - 1), channels), jnp.bfloat16),
            pltpu.VMEM((size // 2 + SECOND_SPACING, 16 * (tiles - 2), channels), jnp.bfloat16),
            pltpu.VMEM((12 * channels, 2 * channels), jnp.bfloat16),
            pltpu.VMEM((12 * channels, 2 * channels), jnp.bfloat16),
            pltpu.VMEM((size // 4, 4 * size, 2 * channels), jnp.bfloat16),
            pltpu.VMEM((size // 2, 4 * size), jnp.float32),
            pltpu.VMEM((size, 2 * size), jnp.float32),
        ],
        compiler_params=pltpu.CompilerParams(vmem_limit_bytes=40 * 1024 * 1024),
    )(
        every,
        dist_table,
        first_kernel.reshape(9 * channels, channels),
        second_kernel.reshape(9 * channels, channels),
        head,
    )


def on_device(
    embedding,
    bases_table,
    edit_pos,
    edit_tok,
    w_row,
    w_col,
    dist_gain,
    first_kernel,
    second_kernel,
    head_weight,
):
    n_rows, n_cols = lax.axis_size("row"), lax.axis_size("col")
    devices = n_rows * n_cols
    map_bins = embedding.shape[0] * devices // POOL
    table, target = plan(n_rows, n_cols)
    size = map_bins // max(n_rows, n_cols)
    copies, dist_table, head = projected(
        embedding, bases_table, edit_pos, edit_tok, w_row, w_col, dist_gain, head_weight, map_bins, devices, size, table
    )
    got = lax.all_to_all(copies, ("row", "col"), 0, 0)
    every = got.reshape(map_bins, got.shape[2])
    kept, sent = block_scores(every, dist_table, first_kernel, second_kernel, head, size, table)
    received = lax.ppermute(sent, ("row", "col"), [(device, target[device]) for device in range(devices)])
    place = lookup(table)[5]
    axis = 1 if n_rows > n_cols else 0
    return jnp.where(
        place == 0,
        jnp.concatenate([kept, received], axis=axis),
        jnp.concatenate([received, kept], axis=axis),
    )


def solution(mesh):
    placed = (P(("row", "col"), None), P(), P("cand"), P("cand"), P(), P(), P(), P(), P(), P())
    return jax.shard_map(
        on_device, mesh=mesh, in_specs=placed, out_specs=P(("cand", "row"), "col"), check_vma=False
    )
```
